128 devices in a mesh: corpus: 8 (over z, core), batch: 16 (over y, x).
Axes of the slice: x: 4, y: 4, z: 4, core: 2. Of those that a mesh axis runs over, the one named last changes fastest.
Arguments:
- tokens: bfloat16 [1024, 128, 1024], P(('corpus', 'batch')), may hold values from -6 to 6
- weight_in: bfloat16 [1024, 2048], replicated, may hold values from -0.1875 to 0.1875
- bias_in: float32 [2048], replicated, may hold values from -3 to 3
- weight_out: bfloat16 [2048, 1024], replicated, may hold values from -0.125 to 0.125
- bias_out: float32 [1024], replicated, may hold values from -3 to 3
- norm_gain: float32 [1024], replicated, may hold values from 0.25 to 1.75
- norm_shift: float32 [1024], replicated, may hold values from -3 to 3
- queries: bfloat16 [1024, 1024], P(('corpus', 'batch')), may hold values from -6 to 6
- corpus_table: bfloat16 [8192, 1024], P('corpus'), may hold values from -0.19921875 to 0.19921875
- neg_owner: int32 [1024, 12, 1], P(('corpus', 'batch')), may hold values from 0 to 7; in each aligned block of 96 rows (0 to 95, 96 to 191, ..., all dimensions but the last counted through in order) at most 24 rows name the same one
- neg_row: int32 [1024, 12], P(('corpus', 'batch')), may hold values from 0 to 1023
- neg_count: int32 [1024], P(('corpus', 'batch')), may hold values from 8 to 12
Outputs:
- grad_weight_in: float32 [1024, 2048], P(('corpus', 'batch'))
- grad_bias_in: float32 [2048], replicated
- grad_weight_out: float32 [2048, 1024], P(('corpus', 'batch'))
- grad_bias_out: float32 [1024], replicated
- grad_gain: float32 [1024], replicated
- grad_shift: float32 [1024], replicated
- grad_table: float32 [8192, 1024], P(('corpus', 'batch'))
The draws below stay inside these ranges and needn't reach their ends.
Inputs may be any that keep to these rules, and one draw needn't show every extreme that they name: `neg_owner`: in the rows of one device no corpus shard is named by more than 24 slots, a bound that some block reaches.
All inputs are finite; a program needn't handle non-finite values.
Results may differ from the reference program's by a relative error of at most 0.003.
Values may be sent and summed in bfloat16 or wider, within the bound.
A program may use at most 128 MiB of HBM per device.

```python
import math
import jax
import jax.numpy as jnp
import numpy as np
from jax import lax

D = 1024
FFH = 2048
SEQ = 128
NEG = 12
Q_DEV = 8
CORPUS_DEV = 1024
OWN_CAP = 24
QUERIES = 1024
CORPUS = 8192
N_CORPUS = 8


def common_direction(key, width):
    picks = jax.random.bernoulli(jax.random.fold_in(key, 101), 0.5, (width,))
    return jnp.where(picks, 1.0, -1.0).astype(jnp.float32)


def draw_tokens(key, part):
    direction = common_direction(key, D)
    key = jax.random.fold_in(key, 3)
    noise_key, sign_key = jax.random.split(key)
    signs = jnp.where(jax.random.bernoulli(sign_key, 0.5, (QUERIES, SEQ, 1)), 1.0, -1.0).astype(jnp.float32)
    noise = jnp.clip(jax.random.normal(noise_key, (QUERIES, SEQ, D), jnp.float32), -4.5, 4.5)
    return (noise + signs * direction).astype(jnp.bfloat16)


def draw_queries(key, part):
    direction = common_direction(key, D)
    key = jax.random.fold_in(key, 7)
    noise = jnp.clip(jax.random.normal(key, (QUERIES, D), jnp.float32), -4.0, 4.0)
    amplitude = 1.5
    return (noise + amplitude * direction).astype(jnp.bfloat16)


def plant(result, key, smallest, high):
    place = [jax.random.randint(jax.random.fold_in(key, axis), (), 0, length) for axis, length in enumerate(result.shape)]
    main_axis = result.shape.index(max(result.shape))
    next_to = place[:main_axis] + [(place[main_axis] + 1) % result.shape[main_axis]] + place[main_axis + 1:]
    return result.at[tuple(place)].set(smallest).at[tuple(next_to)].set(high)


def steps_of(key, extent, pieces, least, largest):
    def one(axis_at, parts):
        draws = jax.random.uniform(jax.random.fold_in(jax.random.fold_in(key, 6), axis_at), (parts,), jnp.float32, least / len(pieces), largest / len(pieces))
        return jnp.repeat(jnp.exp(draws), extent[axis_at] // parts).reshape((-1,) + (1,) * (len(extent) - axis_at - 1))

    level = one(*pieces[0])
    for cut in pieces[1:]:
        level = level * one(*cut)
    return level


def routed_block(rng, own, number, rows, count, top, bound, skew):
    sequence = jax.random.permutation(rng, count)
    crowded, ordinary = load_shares(count, rows * top, bound, skew, True), load_shares(count, rows * top, bound, skew, False)
    places = jnp.arange(count)

    def named(tallies, offset_by):
        used = int((tallies > 0).sum())
        fixed = max(1, used // 4)
        moved = fixed + (places - fixed + offset_by * (used - fixed)) % max(1, count - fixed)
        return jnp.zeros((count,), jnp.int32).at[sequence[jnp.where(places < fixed, places, moved)]].set(jnp.asarray(tallies, jnp.int32))

    tallies = jnp.where(number % 4 == 0, named(crowded, number // 4), named(ordinary, number - number // 4 - 1))
    mixed = jax.random.permutation(jax.random.fold_in(own, 3), count)
    donor, taker = mixed[0:count // 2 * 2:2], mixed[1:count // 2 * 2:2]
    slack = jnp.minimum(tallies[donor] - 1, bound - tallies[taker]) // 2
    slack = jnp.where((donor == sequence[0]) | (taker == sequence[0]) | (tallies[taker] == 0), 0, jnp.maximum(slack, 0))
    moved = jax.random.randint(jax.random.fold_in(own, 4), (count // 2,), 0, 1 << 20) % (slack + 1)
    tallies = tallies.at[donor].add(-moved).at[taker].add(moved)
    items = jnp.searchsorted(jnp.cumsum(tallies), jnp.arange(rows * top), side="right").astype(jnp.int32)
    grid = items.reshape(top, rows).T
    grid = grid[jax.random.permutation(jax.random.fold_in(own, 1), rows)]
    offset_by = jax.random.randint(jax.random.fold_in(own, 2), (rows, 1), 0, top)
    return jnp.take_along_axis(grid, (jnp.arange(top)[None, :] + offset_by) % top, axis=1)


def load_shares(count, total, most, skew, full):
    weights = [(1 << 20) // math.isqrt(rank ** skew) + 1 for rank in range(1, count + 1)]
    largest = most if full else min(most, max(-(-total // count), total * weights[0] // sum(weights)))
    least = 1 if total - largest >= count - 1 else 0
    holding, surplus = [largest] + [least] * (count - 1), total - largest - least * (count - 1)
    while surplus > 0:
        free = [i for i in range(1, count) if holding[i] < largest] or [i for i in range(1, count) if holding[i] < most]
        mass, budget = sum([weights[i] for i in free]), surplus
        for i in free:
            extra = min(most - holding[i], max(1, budget * weights[i] // mass), surplus)
            holding[i] = holding[i] + extra
            surplus = surplus - extra
    return np.array(holding)


def scatter_about(rng, shape, scale, reach, pieces=(), kind=jnp.bfloat16):
    level = steps_of(rng, shape, pieces, -0.22, 0.18) if pieces else 1.0
    entries = jax.random.normal(rng, shape, jnp.float32) * scale * level
    return jnp.minimum(jnp.maximum(entries, -reach), reach).astype(kind)


def setup_inputs(seed: int = 0) -> dict:
    key_of = jax.random.split(jax.random.key(seed), 13)
    tokens = draw_tokens(jax.random.fold_in(key_of[12], 71), 0)
    weight_in = scatter_about(key_of[1], (D, FFH), D ** -0.5, 0.1875)
    bias_in = scatter_about(key_of[2], (FFH,), 0.5, 3.0, (), jnp.float32)
    weight_out = scatter_about(key_of[3], (FFH, D), FFH ** -0.5, 0.125)
    bias_out = scatter_about(key_of[4], (D,), 0.5, 3.0, (), jnp.float32)
    norm_gain = jnp.clip(1.0 + 0.15 * jax.random.normal(key_of[5], (D,), jnp.float32), 0.25, 1.75)
    norm_shift = scatter_about(key_of[6], (D,), 0.5, 3.0, (), jnp.float32)
    queries = draw_queries(jax.random.fold_in(key_of[12], 71), 0)
    corpus_table = scatter_about(key_of[8], (CORPUS, D), 0.03125, 0.19921875, ((0, 8),))
    neg_owner_keys = jax.random.split(jax.random.fold_in(key_of[9], 1), QUERIES * NEG // (Q_DEV * NEG))
    neg_owner_turns = jax.random.permutation(jax.random.fold_in(key_of[9], 3), QUERIES * NEG // (Q_DEV * NEG))
    neg_owner = jax.vmap(lambda own, number: routed_block(jax.random.fold_in(key_of[9], 2), own, number, Q_DEV * NEG, N_CORPUS, 1, OWN_CAP, 2))(neg_owner_keys, neg_owner_turns).reshape((QUERIES, NEG, 1))
    neg_row = plant(jax.random.randint(key_of[10], (QUERIES, NEG), 0, CORPUS_DEV), jax.random.fold_in(key_of[10], 1), 0, CORPUS_DEV - 1).astype(jnp.int32)
    neg_count = plant(jax.random.randint(key_of[11], (QUERIES,), 8, NEG + 1), jax.random.fold_in(key_of[11], 1), 8, NEG).astype(jnp.int32)
    return {"tokens": tokens, "weight_in": weight_in, "bias_in": bias_in, "weight_out": weight_out, "bias_out": bias_out, "norm_gain": norm_gain, "norm_shift": norm_shift, "queries": queries, "corpus_table": corpus_table, "neg_owner": neg_owner, "neg_row": neg_row, "neg_count": neg_count}


logit_divisor = 0.05
norm_eps = 1e-06

def gelu_exact(value):
    return 0.5 * value * (1.0 + lax.erf(value * 0.7071067811865476))

def gelu_slope(value):
    cdf = 0.5 * (1.0 + lax.erf(value * 0.7071067811865476))
    return cdf + value * 0.3989422804014327 * jnp.exp(-0.5 * value * value)

def unit_rows(vectors):
    scale = lax.rsqrt(lax.optimization_barrier(jnp.sum(vectors * vectors, axis=-1, keepdims=True)) + norm_eps)
    return (vectors * scale, scale)

def layer_grads(tokens, weight_in, bias_in, weight_out, bias_out, norm_gain, norm_shift, queries, negatives, counts):
    count_q, seq, width = tokens.shape
    slots = negatives.shape[1]
    flat = tokens.reshape(count_q * seq, width)
    pre = jnp.dot(flat, weight_in, preferred_element_type=jnp.float32) + bias_in
    hidden = gelu_exact(pre).astype(jnp.bfloat16)
    summed = flat.astype(jnp.float32) + jnp.dot(hidden, weight_out, preferred_element_type=jnp.float32) + bias_out
    centred = summed - lax.optimization_barrier(jnp.mean(summed, axis=1, keepdims=True))
    inv_std = lax.rsqrt(lax.optimization_barrier(jnp.mean(centred * centred, axis=1, keepdims=True)) + norm_eps)
    normed = centred * inv_std
    outputs = normed * norm_gain + norm_shift
    pooled = lax.optimization_barrier(jnp.sum(outputs.reshape(count_q, seq, width), axis=1))
    vocabulary_lookup_table, emb_scale = unit_rows(pooled)
    question_normalized_lines, unused = unit_rows(queries.astype(jnp.float32))
    distractor_normalized_lines, neg_scale = unit_rows(negatives.astype(jnp.float32))
    relevant_document = lax.optimization_barrier(jnp.sum(question_normalized_lines * vocabulary_lookup_table, axis=1)) / logit_divisor
    distractor_document = lax.optimization_barrier(jnp.sum(question_normalized_lines[:, None, :] * distractor_normalized_lines, axis=2)) / logit_divisor
    live = (jnp.arange(slots, dtype=jnp.int32)[None, :] < counts[:, None]).astype(jnp.float32)
    weights = jnp.exp(distractor_document) * live
    own = jnp.exp(relevant_document)
    total = own + lax.optimization_barrier(jnp.sum(weights, axis=1))
    relevant_slope = own / total - 1.0
    distractor_slope = weights / total[:, None]
    lookup_table_slope = (relevant_slope / logit_divisor)[:, None] * question_normalized_lines
    normalized_slope = (distractor_slope / logit_divisor)[:, :, None] * question_normalized_lines[:, None, :]
    d_pooled = emb_scale * (lookup_table_slope - vocabulary_lookup_table * lax.optimization_barrier(jnp.sum(vocabulary_lookup_table * lookup_table_slope, axis=1, keepdims=True)))
    d_neg = neg_scale * (normalized_slope - distractor_normalized_lines * lax.optimization_barrier(jnp.sum(distractor_normalized_lines * normalized_slope, axis=2, keepdims=True)))
    grad_shift = lax.optimization_barrier(jnp.sum(d_pooled, axis=0)) * seq
    grad_gain = lax.optimization_barrier(jnp.sum(d_pooled * lax.optimization_barrier(jnp.sum(normed.reshape(count_q, seq, width), axis=1)), axis=0))
    d_normed = jnp.broadcast_to((d_pooled * norm_gain)[:, None, :], (count_q, seq, width)).reshape(count_q * seq, width)
    d_sum = inv_std * (d_normed - lax.optimization_barrier(jnp.mean(d_normed, axis=1, keepdims=True)) - normed * lax.optimization_barrier(jnp.mean(d_normed * normed, axis=1, keepdims=True)))
    grad_bias_out = lax.optimization_barrier(jnp.sum(d_sum, axis=0))
    d_sum_low = d_sum.astype(jnp.bfloat16)
    grad_weight_out = lax.dot_general(hidden, d_sum_low, (((0,), (0,)), ((), ())), preferred_element_type=jnp.float32)
    d_hidden = lax.dot_general(d_sum_low, weight_out, (((1,), (1,)), ((), ())), preferred_element_type=jnp.float32)
    d_pre = d_hidden * gelu_slope(pre)
    grad_bias_in = lax.optimization_barrier(jnp.sum(d_pre, axis=0))
    d_pre_low = d_pre.astype(jnp.bfloat16)
    grad_weight_in = lax.dot_general(flat, d_pre_low, (((0,), (0,)), ((), ())), preferred_element_type=jnp.float32)
    return (grad_weight_in, grad_bias_in, grad_weight_out, grad_bias_out, grad_gain, grad_shift, d_neg)

def reference(tokens, weight_in, bias_in, weight_out, bias_out, norm_gain, norm_shift, queries, corpus_table, neg_owner, neg_row, neg_count):
    blocks = QUERIES // Q_DEV
    global_ids = (neg_owner[:, :, 0] * CORPUS_DEV + neg_row).astype(jnp.int32)

    def step(carry, index):
        start = (index * Q_DEV).astype(jnp.int32)
        block_tokens = lax.dynamic_slice_in_dim(tokens, start, Q_DEV, 0)
        block_queries = lax.dynamic_slice_in_dim(queries, start, Q_DEV, 0)
        block_ids = lax.dynamic_slice_in_dim(global_ids, start, Q_DEV, 0)
        block_counts = lax.dynamic_slice_in_dim(neg_count, start, Q_DEV, 0)
        negatives = jnp.take(corpus_table, block_ids, axis=0)
        grads = layer_grads(block_tokens, weight_in, bias_in, weight_out, bias_out, norm_gain, norm_shift, block_queries, negatives, block_counts)
        table = carry[6].at[block_ids.reshape(-1)].add(grads[6].reshape(-1, D))
        return ((carry[0] + grads[0], carry[1] + grads[1], carry[2] + grads[2], carry[3] + grads[3], carry[4] + grads[4], carry[5] + grads[5], table), None)
    start_carry = (jnp.zeros((D, FFH), jnp.float32), jnp.zeros((FFH,), jnp.float32), jnp.zeros((FFH, D), jnp.float32), jnp.zeros((D,), jnp.float32), jnp.zeros((D,), jnp.float32), jnp.zeros((D,), jnp.float32), jnp.zeros((CORPUS, D), jnp.float32))
    final, unused = lax.scan(step, start_carry, jnp.arange(blocks, dtype=jnp.int32))
    return (final[0], final[1], final[2], final[3], final[4], final[5], final[6])
```

```python
import functools

import jax
import jax.numpy as jnp
from jax import lax
from jax.experimental import pallas as pl
from jax.experimental.pallas import tpu as pltpu
from jax.sharding import PartitionSpec as P

logit_divisor = 0.05
norm_eps = 1e-06
MESH = pl.DeviceIdType.MESH
F32, BF16 = jnp.float32, jnp.bfloat16


def gelu_exact(value):
    return 0.5 * value * (1.0 + lax.erf(value * 0.7071067811865476))


def gelu_slope(value):
    cdf = 0.5 * (1.0 + lax.erf(value * 0.7071067811865476))
    return cdf + value * 0.3989422804014327 * jnp.exp(-0.5 * value * value)


def unit_rows(vectors):
    scale = lax.rsqrt(jnp.sum(vectors * vectors, axis=-1, keepdims=True) + norm_eps)
    return (vectors * scale, scale)


def place():
    c, b = lax.axis_index("corpus"), lax.axis_index("batch")
    return c // 2, c % 2, b // 4, b % 4


def device(z, k, y, x):
    return (z * 2 + k, y * 4 + x)


def moved(here, dim, offset):
    z, k, y, x = here
    at = [z, y, x]
    at[dim] = lax.rem(at[dim] + offset, 4)
    return device(at[0], k, at[1], at[2]), at[dim]


def greet(peers):
    barrier = pltpu.get_barrier_semaphore()
    for peer in peers:
        pl.semaphore_signal(barrier, inc=1, device_id=peer, device_id_type=MESH)
    pl.semaphore_wait(barrier, len(peers))


def push(src, dst, send, recv, peer):
    copy = pltpu.make_async_remote_copy(
        src_ref=src, dst_ref=dst, send_sem=send, recv_sem=recv, device_id=peer, device_id_type=MESH
    )
    copy.start()
    return copy


def lookup_kernel(q_ref, id_ref, tab_ref, qall, idall, cos_ref, qcol, idcol, dots, dall, turned, sems, semr, dsem, dsemr):
    here = place()
    z, k, y, x = here
    c = z * 2 + k
    sibling = device(z, 1 - k, y, x)
    column = []
    for j in range(4):
        for e in range(2):
            if j or e:
                column.append(device(lax.rem(z + j, 4), lax.rem(k + e, 2), y, x))
    greet(column + [moved(here, dim, j)[0] for dim in (1, 2) for j in (1, 2, 3)])
    qall[z, k, y, x] = q_ref[...]
    idall[z, k, y, x] = id_ref[...]
    payload = ((0, qall), (1, idall))

    first = []
    for j in (1, 2, 3):
        peer, _ = moved(here, 0, j)
        for n, buf in payload:
            mine = buf.at[z, k, y, x]
            first.append(push(mine, mine, sems.at[0, n, j - 1], semr.at[0, n, j - 1], peer))
    for copy in first:
        copy.wait_recv()
    second = []
    for n, buf, dst in ((0, qall, qcol), (1, idall, idcol)):
        second.append(push(buf.at[:, k, y, x], dst.at[k], sems.at[1, n, 0], semr.at[1, n, 0], sibling))
    third = []
    for j in (1, 2, 3):
        peer, _ = moved(here, 1, j)
        for n, buf in payload:
            mine = buf.at[:, k, y, x]
            third.append(push(mine, mine, sems.at[2, n, j - 1], semr.at[2, n, j - 1], peer))
    qcol[k] = qall[:, k, y, x]
    idcol[k] = idall[:, k, y, x]
    for copy in second + third:
        copy.wait_recv()
    fourth = []
    for j in (1, 2, 3):
        peer, _ = moved(here, 2, j)
        for n, buf in payload:
            mine = buf.at[:, k, :, x]
            fourth.append(push(mine, mine, sems.at[3, n, j - 1], semr.at[3, n, j - 1], peer))

    queries = qcol[...].astype(F32).reshape(8, 16, 512)
    left = queries[:, :8].reshape(64, 512).astype(BF16)
    right = queries[:, 8:].reshape(64, 512).astype(BF16)
    ids = jnp.concatenate([idcol[...].reshape(64, 128), jnp.zeros((64, 128), F32)], axis=0).T[:16, :64]
    dots[...] = jnp.zeros_like(dots)
    rows = 128

    def part(i, carry):
        start = pl.multiple_of(i * rows, rows)
        block = tab_ref[pl.ds(start, rows), :]
        wide = block.astype(F32)
        scale = lax.rsqrt(jnp.sum(wide * wide, axis=1, keepdims=True) + norm_eps)
        score = lax.dot_general(block[:, :512], left, (((1,), (1,)), ((), ())), preferred_element_type=F32)
        score += lax.dot_general(block[:, 512:], right, (((1,), (1,)), ((), ())), preferred_element_type=F32)
        score *= scale
        names = (lax.broadcasted_iota(jnp.int32, (rows, 64), 0) + (start + c * 1024)).astype(F32)
        found = []
        for slot in range(12):
            hit = jnp.where(names == ids[slot : slot + 1, :], score, 0.0)
            found.append(jnp.sum(hit, axis=0, keepdims=True))
        found.append(jnp.zeros((4, 64), F32))
        dots[:, :64] += jnp.concatenate(found, axis=0)
        return carry

    lax.fori_loop(0, 1024 // rows, part, 0)

    back = [push(dots, dall.at[n], dsem.at[n], dsemr.at[n], peer) for n, peer in enumerate(column)]
    for copy in back:
        copy.wait_recv()
    total = dots[...]
    for n in range(7):
        total += dall[n]
    turned[...] = jnp.concatenate([total, jnp.zeros((112, 128), F32)], axis=0).T
    cos_ref[...] = turned[pl.ds(pl.multiple_of((k * 4 + z) * 8, 8), 8), :]

    for copy in fourth:
        copy.wait_recv()
    fifth = []
    for n, buf in payload:
        mine = buf.at[:, k]
        fifth.append(push(mine, mine, sems.at[4, n, 0], semr.at[4, n, 0], sibling))
    for copy in fifth:
        copy.wait_recv()
    for copy in first + second + third + fourth + back + fifth:
        copy.wait_send()


def lookup(q_half, ids, table):
    vmem = pl.BlockSpec(memory_space=pltpu.VMEM)
    return pl.pallas_call(
        lookup_kernel,
        out_shape=(
            jax.ShapeDtypeStruct((4, 2, 4, 4, 16, 512), BF16),
            jax.ShapeDtypeStruct((4, 2, 4, 4, 8, 128), F32),
            jax.ShapeDtypeStruct((8, 128), F32),
        ),
        in_specs=[vmem] * 3,
        out_specs=(vmem,) * 3,
        scratch_shapes=[
            pltpu.VMEM((2, 4, 16, 512), BF16),
            pltpu.VMEM((2, 4, 8, 128), F32),
            pltpu.VMEM((16, 128), F32),
            pltpu.VMEM((7, 16, 128), F32),
            pltpu.VMEM((128, 128), F32),
            pltpu.SemaphoreType.DMA((5, 2, 3)),
            pltpu.SemaphoreType.DMA((5, 2, 3)),
            pltpu.SemaphoreType.DMA((7,)),
            pltpu.SemaphoreType.DMA((7,)),
        ],
        compiler_params=pltpu.CompilerParams(
            collective_id=0, has_side_effects=True, vmem_limit_bytes=40 * 1024 * 1024
        ),
    )(q_half, ids, table)


PARTS = (((0, 384), (384, 768), (768, 1024)), ((0, 384), (384, 640), (640, 1024)))
ORDER = ((0, 1, 2), (1, 2, 0), (2, 0, 1))


def pick(ref, axis, index, columns=None):
    at = [slice(None)] * (len(ref.shape) - 2)
    at[axis] = index
    return ref.at[tuple(at) + (slice(None), slice(None) if columns is None else pl.ds(columns[0], columns[1] - columns[0]))]


def sum_kernel(
    part, small, coef, qall, idall, tab, out, small_out, gtab,
    r0, r1, s1, r2, s2, r3, sm, cg, names, coefs, sem0, rsem0, sems, semr, qs, qr, cs, cr,
):
    here = place()
    z, k, y, x = here
    coord = (z, y, x)
    sibling = device(z, 1 - k, y, x)
    greet([sibling] + [moved(here, dim, j)[0] for dim in (0, 1, 2) for j in (1, 2, 3)])
    sent = []

    zero = []
    for w in range(2):
        for zz in range(4):
            zero.append(push(part.at[w, zz, 1 - k], r0.at[w, zz], sem0.at[w, zz], rsem0.at[w, zz], sibling))
    sent += zero
    sm[0, k] = small[...]
    tiny = [push(sm.at[0, k], sm.at[0, k], qs.at[0, 0], qr.at[0, 0], sibling)]
    cg[z, k, y, x] = coef[...]
    mine = cg.at[z, k, y, x]
    tiny.append(push(mine, mine, cs.at[0, 0], cr.at[0, 0], sibling))
    for copy in tiny:
        copy.wait_recv()
    sent += tiny

    def stage_small(step):
        dim = step - 1
        got = sm[step - 1, 0] + sm[step - 1, 1]
        if step > 1:
            got = (got + sm[step - 1, 2]) + sm[step - 1, 3]
        sm[step, coord[dim]] = got
        block = cg.at[(z, slice(None), y, x) if dim == 0 else (slice(None), slice(None), y, x) if dim == 1 else (slice(None), slice(None), slice(None), x)]
        copies = []
        for j in (1, 2, 3):
            peer, _ = moved(here, dim, j)
            line = sm.at[step, coord[dim]]
            copies.append(push(line, line, qs.at[step, j - 1], qr.at[step, j - 1], peer))
            copies.append(push(block, block, cs.at[step, j - 1], cr.at[step, j - 1], peer))
        return copies

    tiny = stage_small(1)
    sent += tiny

    def add_core(w, zz):
        def one(i, carry):
            yy, xx = i // 4, lax.rem(i, 4)
            r0[w, zz, yy, xx] = (r0[w, zz, yy, xx].astype(F32) + part[w, zz, k, yy, xx].astype(F32)).astype(BF16)
            return carry
        lax.fori_loop(0, 16, one, 0)

    def stage_one(w, p):
        dim = ORDER[p][0]
        copies = []
        for j in (1, 2, 3):
            peer, to = moved(here, dim, j)
            copies.append(
                push(pick(r0.at[w], dim, to, PARTS[w][p]), r1[w][p].at[j - 1], sems.at[0, w, p, j - 1], semr.at[0, w, p, j - 1], peer)
            )
        return copies

    def add_one(w, p):
        dim = ORDER[p][0]
        own = pick(r0.at[w], dim, coord[dim], PARTS[w][p])
        def one(i, carry):
            e, f = i // 4, lax.rem(i, 4)
            total = own[e, f].astype(F32)
            for j in range(3):
                total += r1[w][p][j, e, f].astype(F32)
            s1[w][p][e, f] = total.astype(BF16)
            return carry
        lax.fori_loop(0, 16, one, 0)

    def stage_two(w, p):
        dim = ORDER[p][1]
        left = [d for d in (0, 1, 2) if d != ORDER[p][0]]
        copies = []
        for j in (1, 2, 3):
            peer, to = moved(here, dim, j)
            copies.append(
                push(pick(s1[w][p], left.index(dim), to), r2[w][p].at[j - 1], sems.at[1, w, p, j - 1], semr.at[1, w, p, j - 1], peer)
            )
        return copies

    def add_two(w, p):
        dim = ORDER[p][1]
        left = [d for d in (0, 1, 2) if d != ORDER[p][0]]
        own = pick(s1[w][p], left.index(dim), coord[dim])
        for e in range(4):
            total = own[e].astype(F32)
            for j in range(3):
                total += r2[w][p][j, e].astype(F32)
            s2[w][p][e] = total

    def stage_three(w, p):
        dim = ORDER[p][2]
        copies = []
        for j in (1, 2, 3):
            peer, to = moved(here, dim, j)
            copies.append(push(s2[w][p].at[to], r3[w][p].at[j - 1], sems.at[2, w, p, j - 1], semr.at[2, w, p, j - 1], peer))
        return copies

    def add_three(w, p):
        lo, hi = PARTS[w][p]
        total = s2[w][p][coord[ORDER[p][2]]]
        for j in range(3):
            total += r3[w][p][j]
        out[w, :, lo:hi] = total

    both = [(w, p) for w in range(2) for p in range(3)]
    ones, twos, threes = {}, {}, {}
    for w in range(2):
        for zz in range(4):
            zero[w * 4 + zz].wait_recv()
            add_core(w, zz)
        for p in range(3):
            ones[w, p] = stage_one(w, p)
            sent += ones[w, p]
    for copy in tiny:
        copy.wait_recv()
    tiny = stage_small(2)
    sent += tiny
    for at in both:
        for copy in ones[at]:
            copy.wait_recv()
        add_one(*at)
        twos[at] = stage_two(*at)
        sent += twos[at]
    for copy in tiny:
        copy.wait_recv()
    tiny = stage_small(3)
    sent += tiny
    for at in both:
        for copy in twos[at]:
            copy.wait_recv()
        add_two(*at)
        threes[at] = stage_three(*at)
        sent += threes[at]
    for copy in tiny:
        copy.wait_recv()
    small_out[...] = ((sm[3, 0] + sm[3, 1]) + sm[3, 2]) + sm[3, 3]

    base = (z * 2 + k) * 1024 + (y * 4 + x) * 64
    row = (lax.broadcasted_iota(jnp.int32, (256, 128), 1) + base).astype(F32)
    names[...] = idall[...].reshape(1024, 128)
    coefs[...] = cg[...].reshape(1024, 128)

    def gather(i, carry):
        start = pl.multiple_of(i * 256, 256)
        name, value = names[pl.ds(start, 256), :], coefs[pl.ds(start, 256), :]
        weight = jnp.zeros((256, 128), F32)
        for slot in range(12):
            weight += jnp.where(name[:, slot : slot + 1] == row, value[:, slot : slot + 1], 0.0)
        high = weight.astype(BF16)
        low = (weight - high.astype(F32)).astype(BF16)
        query = qall[i].astype(F32).reshape(32, 16, 512)
        halves = []
        for h in range(2):
            half = query[:, h * 8 : h * 8 + 8].reshape(256, 512).astype(BF16)
            dims = (((0,), (0,)), ((), ()))
            halves.append(
                lax.dot_general(high, half, dims, preferred_element_type=F32)
                + lax.dot_general(low, half, dims, preferred_element_type=F32)
            )
        return tuple(a + b[:64] for a, b in zip(carry, halves))

    sums = lax.fori_loop(0, 4, gather, (jnp.zeros((64, 512), F32),) * 2)
    slope = jnp.concatenate(sums, axis=1)
    rows = tab[...].astype(F32)
    scale = lax.rsqrt(jnp.sum(rows * rows, axis=1, keepdims=True) + norm_eps)
    unit = rows * scale
    gtab[...] = scale * (slope - unit * jnp.sum(unit * slope, axis=1, keepdims=True))

    for at in both:
        for copy in threes[at]:
            copy.wait_recv()
        add_three(*at)
    for copy in sent:
        copy.wait_send()


def sum_all(part, small, coef, qall, idall, tab):
    vmem = pl.BlockSpec(memory_space=pltpu.VMEM)
    def scratch(shape, kind):
        return tuple(tuple(pltpu.VMEM(shape + (16, hi - lo), kind) for lo, hi in row) for row in PARTS)
    dma = pltpu.SemaphoreType.DMA
    return pl.pallas_call(
        sum_kernel,
        out_shape=(
            jax.ShapeDtypeStruct((2, 16, 1024), F32),
            jax.ShapeDtypeStruct((40, 128), F32),
            jax.ShapeDtypeStruct((64, 1024), F32),
        ),
        in_specs=[vmem] * 6,
        out_specs=(vmem,) * 3,
        scratch_shapes=[
            pltpu.VMEM((2, 4, 4, 4, 16, 1024), BF16),
            scratch((3, 4, 4), BF16),
            scratch((4, 4), BF16),
            scratch((3, 4), BF16),
            scratch((4,), F32),
            scratch((3,), F32),
            pltpu.VMEM((4, 4, 40, 128), F32),
            pltpu.VMEM((4, 2, 4, 4, 8, 128), F32),
            pltpu.VMEM((1024, 128), F32),
            pltpu.VMEM((1024, 128), F32),
            dma((2, 4)),
            dma((2, 4)),
            dma((3, 2, 3, 3)),
            dma((3, 2, 3, 3)),
            dma((4, 3)),
            dma((4, 3)),
            dma((4, 3)),
            dma((4, 3)),
        ],
        compiler_params=pltpu.CompilerParams(
            collective_id=1, has_side_effects=True, vmem_limit_bytes=56 * 1024 * 1024
        ),
    )(part, small, coef, qall, idall, tab)


def body(
    tokens,
    weight_in,
    bias_in,
    weight_out,
    bias_out,
    norm_gain,
    norm_shift,
    queries,
    corpus_table,
    neg_owner,
    neg_row,
    neg_count,
):
    count_q, seq, width = tokens.shape
    slots = neg_row.shape[1]
    ids = (neg_owner.reshape(count_q, slots) * 1024 + neg_row).astype(F32)
    ids = jnp.pad(ids, ((0, 0), (0, 128 - slots)), constant_values=-1.0)
    q_half = jnp.concatenate([queries[:, :512], queries[:, 512:]], axis=0)
    qall, idall, raw = lookup(q_half, ids, corpus_table)

    flat = tokens.reshape(count_q * seq, width)
    pre = jnp.dot(flat, weight_in, preferred_element_type=F32) + bias_in
    hidden = gelu_exact(pre).astype(BF16)
    summed = flat.astype(F32) + jnp.dot(hidden, weight_out, preferred_element_type=F32) + bias_out
    centred = summed - jnp.mean(summed, axis=1, keepdims=True)
    inv_std = lax.rsqrt(jnp.mean(centred * centred, axis=1, keepdims=True) + norm_eps)
    normed = centred * inv_std
    outputs = normed * norm_gain + norm_shift
    pooled = jnp.sum(outputs.reshape(count_q, seq, width), axis=1)
    emb, emb_scale = unit_rows(pooled)
    question, q_scale = unit_rows(queries.astype(F32))
    positive = jnp.sum(question * emb, axis=1) / logit_divisor
    negative = raw[:, :slots] * q_scale / logit_divisor
    live = (jnp.arange(slots, dtype=jnp.int32)[None, :] < neg_count[:, None]).astype(F32)
    weights = jnp.exp(negative) * live
    own = jnp.exp(positive)
    total = own + jnp.sum(weights, axis=1)
    positive_slope = own / total - 1.0
    coef = weights / total[:, None] / logit_divisor * q_scale
    coef = jnp.pad(coef, ((0, 0), (0, 128 - slots)))
    emb_slope = (positive_slope / logit_divisor)[:, None] * question
    d_pooled = emb_scale * (emb_slope - emb * jnp.sum(emb * emb_slope, axis=1, keepdims=True))
    grad_shift = jnp.sum(d_pooled, axis=0) * seq
    grad_gain = jnp.sum(d_pooled * jnp.sum(normed.reshape(count_q, seq, width), axis=1), axis=0)
    d_normed = jnp.broadcast_to((d_pooled * norm_gain)[:, None, :], (count_q, seq, width)).reshape(
        count_q * seq, width
    )
    d_sum = inv_std * (
        d_normed
        - jnp.mean(d_normed, axis=1, keepdims=True)
        - normed * jnp.mean(d_normed * normed, axis=1, keepdims=True)
    )
    grad_bias_out = jnp.sum(d_sum, axis=0)
    d_sum_low = d_sum.astype(BF16)
    d_hidden = lax.dot_general(d_sum_low, weight_out, (((1,), (1,)), ((), ())), preferred_element_type=F32)
    d_pre = d_hidden * gelu_slope(pre)
    grad_bias_in = jnp.sum(d_pre, axis=0)
    d_pre_low = d_pre.astype(BF16)
    dims = (((0,), (0,)), ((), ()))
    part_out = lax.dot_general(hidden, d_sum_low, dims, preferred_element_type=F32).astype(BF16)
    part_in = lax.dot_general(flat, d_pre_low, dims, preferred_element_type=F32)
    part_in = part_in.reshape(128, 8, 2, 1024).transpose(0, 2, 1, 3).astype(BF16)
    part = jnp.stack([part_out.reshape(128, 16, 1024), part_in.reshape(128, 16, 1024)])
    part = part.reshape(2, 4, 2, 4, 4, 16, 1024)
    small = jnp.concatenate([grad_bias_in, grad_bias_out, grad_gain, grad_shift]).reshape(40, 128)
    own_rows = lax.dynamic_slice_in_dim(corpus_table, lax.axis_index("batch") * 64, 64, 0)
    out, small, grad_table = sum_all(
        part, small, coef, qall.reshape(4, 32, 16, 512), idall, own_rows
    )
    small = small.reshape(5120)
    grad_in = out[1].reshape(2, 8, 1024).transpose(1, 0, 2).reshape(8, 2048)
    return (grad_in, small[:2048], out[0], small[2048:3072], small[3072:4096], small[4096:], grad_table)


def solution(mesh):
    return jax.shard_map(
        body,
        mesh=mesh,
        in_specs=(
            P(("corpus", "batch"), None, None),
            P(),
            P(),
            P(),
            P(),
            P(),
            P(),
            P(("corpus", "batch"), None),
            P("corpus", None),
            P(("corpus", "batch"), None, None),
            P(("corpus", "batch"), None),
            P(("corpus", "batch")),
        ),
        out_specs=(
            P(("corpus", "batch"), None),
            P(),
            P(("corpus", "batch"), None),
            P(),
            P(),
            P(),
            P(("corpus", "batch"), None),
        ),
        check_vma=False,
    )
```

```python
import functools

import jax
import jax.numpy as jnp
from jax import lax
from jax.experimental import pallas as pl
from jax.experimental.pallas import tpu as pltpu
from jax.sharding import PartitionSpec as P

logit_divisor = 0.05
norm_eps = 1e-06
MESH = pl.DeviceIdType.MESH
F32, BF16 = jnp.float32, jnp.bfloat16
VMEM_BYTES = 60 * 1024 * 1024


def place():
    c, b = lax.axis_index("corpus"), lax.axis_index("batch")
    return c // 2, c % 2, b // 4, b % 4


def device(z, k, y, x):
    return (z * 2 + k, y * 4 + x)


def moved(here, dim, offset):
    z, k, y, x = here
    at = [z, y, x]
    at[dim] = lax.rem(at[dim] + offset, 4)
    return device(at[0], k, at[1], at[2]), at[dim]


def greet(peers):
    barrier = pltpu.get_barrier_semaphore()
    for peer in peers:
        pl.semaphore_signal(barrier, inc=1, device_id=peer, device_id_type=MESH)
    pl.semaphore_wait(barrier, len(peers))


def push(src, dst, send, recv, peer):
    copy = pltpu.make_async_remote_copy(
        src_ref=src, dst_ref=dst, send_sem=send, recv_sem=recv, device_id=peer, device_id_type=MESH
    )
    copy.start()
    return copy


PARTS = (((0, 384), (384, 768), (768, 1024)), ((0, 384), (384, 640), (640, 1024)))
ORDER = ((0, 1, 2), (1, 2, 0), (2, 0, 1))


def pick(ref, axis, index, columns=None):
    at = [slice(None)] * (len(ref.shape) - 2)
    at[axis] = index
    return ref.at[tuple(at) + (slice(None), slice(None) if columns is None else pl.ds(columns[0], columns[1] - columns[0]))]


def dot(a, b, ca=1, cb=0):
    return lax.dot_general(a, b, (((ca,), (cb,)), ((), ())), preferred_element_type=F32)


def step_kernel(
    tok_hbm, win_hbm, wout_hbm, tab_hbm, bias_in, bias_out, gain, shift, queries, q_half, ids_own, counts,
    g_in, g_bias_in, g_out, g_bias_out, g_gain, g_shift, g_table,
    tok, win, wout, tab, tab_own, tok_t, hidden, slope, normed, inv_std, d_sum, d_pre, bias_acc,
    qall, idall, qcol, idcol, dots, dall, turned,
    part, r0, r1, s1, r2, s2, r3, sm, cg,
    load, sems_q, semr_q, dsem, dsemr, sem0, rsem0, sems, semr, qs, qr, cs, cr,
):
    here = place()
    z, k, y, x = here
    coord = (z, y, x)
    c = z * 2 + k
    sibling = device(z, 1 - k, y, x)
    sent = []

    def local(src, dst, n):
        copy = pltpu.make_async_copy(src, dst, load.at[n])
        copy.start()
        return copy

    tok_in = local(tok_hbm, tok, 0)
    win_in = [local(win_hbm.at[:, pl.ds(512 * n, 512)], win.at[:, pl.ds(512 * n, 512)], 1 + n) for n in range(4)]
    tab_in = local(tab_hbm, tab, 5)
    wout_in = local(wout_hbm, wout, 6)
    own_in = local(tab_hbm.at[pl.ds(pl.multiple_of((y * 4 + x) * 64, 64), 64), :], tab_own, 7)

    column = []
    for j in range(4):
        for e in range(2):
            if j or e:
                column.append(device(lax.rem(z + j, 4), lax.rem(k + e, 2), y, x))
    greet(column + [moved(here, dim, j)[0] for dim in (1, 2) for j in (1, 2, 3)])

    qall[z, k, y, x] = q_half[...]
    idall[z, k, y, x] = ids_own[...]
    payload = ((0, qall), (1, idall))
    first = []
    for j in (1, 2, 3):
        peer, _ = moved(here, 0, j)
        for n, buf in payload:
            mine = buf.at[z, k, y, x]
            first.append(push(mine, mine, sems_q.at[0, n, j - 1], semr_q.at[0, n, j - 1], peer))

    def gather_second():
        for copy in first:
            copy.wait_recv()
        copies = []
        for n, buf, dst in ((0, qall, qcol), (1, idall, idcol)):
            copies.append(push(buf.at[:, k, y, x], dst.at[k], sems_q.at[1, n, 0], semr_q.at[1, n, 0], sibling))
        for j in (1, 2, 3):
            peer, _ = moved(here, 1, j)
            for n, buf in payload:
                mine = buf.at[:, k, y, x]
                copies.append(push(mine, mine, sems_q.at[2, n, j - 1], semr_q.at[2, n, j - 1], peer))
        qcol[k] = qall[:, k, y, x]
        idcol[k] = idall[:, k, y, x]
        return copies

    def gather_third():
        copies = []
        for j in (1, 2, 3):
            peer, _ = moved(here, 2, j)
            for n, buf in payload:
                mine = buf.at[:, k, :, x]
                copies.append(push(mine, mine, sems_q.at[3, n, j - 1], semr_q.at[3, n, j - 1], peer))
        return copies

    def gather_last():
        copies = []
        for n, buf in payload:
            mine = buf.at[:, k]
            copies.append(push(mine, mine, sems_q.at[4, n, 0], semr_q.at[4, n, 0], sibling))
        return copies

    def project(n, carry):
        at = pl.ds(pl.multiple_of(n * 256, 256), 256)
        weight = win[:, at]
        bias = bias_in[:, at]
        for m in range(4):
            rows = slice(m * 256, m * 256 + 256)
            pre = dot(tok[rows, :], weight) + bias
            cdf = 0.5 * (1.0 + lax.erf(pre * 0.7071067811865476))
            hidden[rows, at] = (pre * cdf).astype(BF16)
            slope[rows, at] = cdf + pre * 0.3989422804014327 * jnp.exp(-0.5 * pre * pre)
        turn = pl.ds(pl.multiple_of(n * 128, 128), 128)
        tok_t[turn, :] = tok[:, turn].T
        return carry

    tok_in.wait()
    win_in[0].wait()
    lax.fori_loop(0, 2, project, 0)
    second = gather_second()
    win_in[1].wait()
    lax.fori_loop(2, 4, project, 0)
    for copy in second:
        copy.wait_recv()
    third = gather_third()
    sent += first + second + third

    tab_in.wait()
    own_in.wait()
    wide_q = qcol[...].astype(F32).reshape(8, 16, 512)
    left = wide_q[:, :8].reshape(64, 512).astype(BF16)
    right = wide_q[:, 8:].reshape(64, 512).astype(BF16)
    ids = jnp.concatenate([idcol[...].reshape(64, 128), jnp.zeros((64, 128), F32)], axis=0).T[:16, :64]
    dots[...] = jnp.zeros_like(dots)

    def score_rows(i, carry):
        start = pl.multiple_of(i * 128, 128)
        block = tab[pl.ds(start, 128), :]
        wide = block.astype(F32)
        scale = lax.rsqrt(jnp.sum(wide * wide, axis=1, keepdims=True) + norm_eps)
        score = (dot(block[:, :512], left, 1, 1) + dot(block[:, 512:], right, 1, 1)) * scale
        names = (lax.broadcasted_iota(jnp.int32, (128, 64), 0) + (start + c * 1024)).astype(F32)
        found = []
        for slot in range(12):
            hit = jnp.where(names == ids[slot : slot + 1, :], score, 0.0)
            found.append(jnp.sum(hit, axis=0, keepdims=True))
        found.append(jnp.zeros((4, 64), F32))
        dots[:, :64] += jnp.concatenate(found, axis=0)
        return carry

    lax.fori_loop(0, 8, score_rows, 0)
    back = [push(dots, dall.at[n], dsem.at[n], dsemr.at[n], peer) for n, peer in enumerate(column)]
    sent += back

    win_in[2].wait()
    win_in[3].wait()
    lax.fori_loop(4, 8, project, 0)

    for copy in third:
        copy.wait_recv()
    last = gather_last()
    sent += last

    wout_in.wait()
    which = lax.broadcasted_iota(jnp.int32, (8, 1024), 0)

    def normalise(i, carry):
        rows = pl.ds(pl.multiple_of(i * 256, 256), 256)
        summed = tok[rows, :].astype(F32) + dot(hidden[rows, :], wout[...]) + bias_out[...]
        centred = summed - jnp.mean(summed, axis=1, keepdims=True)
        inv = lax.rsqrt(jnp.mean(centred * centred, axis=1, keepdims=True) + norm_eps)
        value = centred * inv
        normed[rows, :] = value
        inv_std[rows, :] = jnp.broadcast_to(inv, (256, 128))
        for h in range(2):
            line = jnp.sum(value[h * 128 : h * 128 + 128], axis=0, keepdims=True)
            carry = jnp.where(which == 2 * i + h, line, carry)
        return carry

    norm_sum = lax.fori_loop(0, 4, normalise, jnp.zeros((8, 1024), F32))

    for copy in back:
        copy.wait_recv()
    total = dots[...]
    for n in range(7):
        total += dall[n]
    turned[...] = jnp.concatenate([total, jnp.zeros((112, 128), F32)], axis=0).T
    raw = turned[pl.ds(pl.multiple_of((k * 4 + z) * 8, 8), 8), :]
    pooled = norm_sum * gain[...] + 128.0 * shift[...]
    emb_scale = lax.rsqrt(jnp.sum(pooled * pooled, axis=1, keepdims=True) + norm_eps)
    emb = pooled * emb_scale
    query = queries[...].astype(F32)
    q_scale = lax.rsqrt(jnp.sum(query * query, axis=1, keepdims=True) + norm_eps)
    question = query * q_scale
    positive = jnp.sum(question * emb, axis=1, keepdims=True) / logit_divisor
    live = lax.broadcasted_iota(jnp.int32, (8, 128), 1) < counts[...]
    weights = jnp.where(live, jnp.exp(raw * q_scale / logit_divisor), 0.0)
    own = jnp.exp(positive)
    whole = own + jnp.sum(weights, axis=1, keepdims=True)
    cg[z, k, y, x] = weights / whole / logit_divisor * q_scale
    emb_slope = ((own / whole - 1.0) / logit_divisor) * question
    d_pooled = emb_scale * (emb_slope - emb * jnp.sum(emb * emb_slope, axis=1, keepdims=True))
    grad_shift = jnp.sum(d_pooled, axis=0, keepdims=True) * 128.0
    grad_gain = jnp.sum(d_pooled * norm_sum, axis=0, keepdims=True)
    lead = d_pooled * gain[...]

    def slopes(step):
        if step == 0:
            mine = cg.at[z, k, y, x]
            return [push(mine, mine, cs.at[0, 0], cr.at[0, 0], sibling)]
        dim = step - 1
        every = slice(None)
        mine = cg.at[((z, every, y, x), (every, every, y, x), (every, every, every, x))[dim]]
        copies = []
        for j in (1, 2, 3):
            peer, _ = moved(here, dim, j)
            copies.append(push(mine, mine, cs.at[step, j - 1], cr.at[step, j - 1], peer))
        return copies

    def arrived(copies):
        for copy in copies:
            copy.wait_recv()

    slope_step = slopes(0)
    sent += slope_step

    def back_norm(i, carry):
        rows = pl.ds(pl.multiple_of(i * 128, 128), 128)
        g = jnp.sum(jnp.where(which == i, lead, 0.0), axis=0, keepdims=True)
        value = normed[rows, :]
        inv = inv_std[rows, :][:, :1]
        both = jnp.mean(value * g, axis=1, keepdims=True)
        ds = inv * (g - jnp.mean(g, axis=1, keepdims=True) - value * both)
        d_sum[rows, :] = ds.astype(BF16)
        return carry + jnp.sum(ds, axis=0, keepdims=True)

    grad_bias_out = lax.fori_loop(0, 8, back_norm, jnp.zeros((1, 1024), F32))
    arrived(slope_step)
    slope_step = slopes(1)
    sent += slope_step

    def grad_out(zz, core):
        at = pl.ds(pl.multiple_of((zz * 2 + core) * 256, 256), 256)
        value = dot(hidden[:, at], d_sum[...], 0, 0)
        part[0, zz, core] = value.astype(BF16).reshape(4, 4, 16, 1024)

    zero = {}
    for zz in range(4):
        grad_out(zz, 1 - k)
        zero[0, zz] = push(part.at[0, zz, 1 - k], r0.at[0, zz], sem0.at[0, zz], rsem0.at[0, zz], sibling)

    def own_blocks(zz, carry):
        grad_out(zz, k)
        return carry

    lax.fori_loop(0, 4, own_blocks, 0)
    arrived(slope_step)
    slope_step = slopes(2)
    sent += slope_step

    def add_core(w, lo, hi, first, last):
        def one(i, carry):
            a, e, f = i // 16, lax.rem(i // 4, 4), lax.rem(i, 4)
            r0[w, a, e, f, :, lo:hi] = (
                r0[w, a, e, f, :, lo:hi].astype(F32) + part[w, a, k, e, f, :, lo:hi].astype(F32)
            ).astype(BF16)
            return carry
        lax.fori_loop(first, last, one, 0)

    def stage_one(w, p):
        dim = ORDER[p][0]
        copies = []
        for j in (1, 2, 3):
            peer, to = moved(here, dim, j)
            src = pick(r0.at[w], dim, to, PARTS[w][p])
            copies.append(push(src, r1[w][p].at[j - 1], sems.at[0, w, p, j - 1], semr.at[0, w, p, j - 1], peer))
        return copies

    def add_one(w, p):
        dim = ORDER[p][0]
        mine = pick(r0.at[w], dim, coord[dim], PARTS[w][p])

        def one(i, carry):
            e, f = i // 4, lax.rem(i, 4)
            value = mine[e, f].astype(F32)
            for j in range(3):
                value += r1[w][p][j, e, f].astype(F32)
            s1[w][p][e, f] = value.astype(BF16)
            return carry
        lax.fori_loop(0, 16, one, 0)

    def stage_two(w, p):
        dim = ORDER[p][1]
        rest = [d for d in (0, 1, 2) if d != ORDER[p][0]]
        copies = []
        for j in (1, 2, 3):
            peer, to = moved(here, dim, j)
            src = pick(s1[w][p], rest.index(dim), to)
            copies.append(push(src, r2[w][p].at[j - 1], sems.at[1, w, p, j - 1], semr.at[1, w, p, j - 1], peer))
        return copies

    def add_two(w, p):
        dim = ORDER[p][1]
        rest = [d for d in (0, 1, 2) if d != ORDER[p][0]]
        mine = pick(s1[w][p], rest.index(dim), coord[dim])
        for e in range(4):
            value = mine[e].astype(F32)
            for j in range(3):
                value += r2[w][p][j, e].astype(F32)
            s2[w][p][e] = value

    def stage_three(w, p):
        dim = ORDER[p][2]
        copies = []
        for j in (1, 2, 3):
            peer, to = moved(here, dim, j)
            copies.append(push(s2[w][p].at[to], r3[w][p].at[j - 1], sems.at[2, w, p, j - 1], semr.at[2, w, p, j - 1], peer))
        return copies

    def add_three(w, p):
        lo, hi = PARTS[w][p]
        value = s2[w][p][coord[ORDER[p][2]]]
        for j in range(3):
            value += r3[w][p][j]
        if w == 0:
            g_out[:, lo:hi] = value
        else:
            for n in range((hi - lo) // 128):
                tile = value[:, n * 128 : n * 128 + 128]
                g_in[:, 2 * lo + 256 * n : 2 * lo + 256 * n + 128] = tile[:8]
                g_in[:, 2 * lo + 256 * n + 128 : 2 * lo + 256 * n + 256] = tile[8:]

    def back_layer(n, carry):
        at = pl.ds(pl.multiple_of(n * 256, 256), 256)
        weight = wout[at, :]
        line = jnp.zeros((1, 256), F32)
        for m in range(4):
            rows = slice(m * 256, m * 256 + 256)
            value = dot(d_sum[rows, :], weight, 1, 1) * slope[rows, at]
            line += jnp.sum(value, axis=0, keepdims=True)
            d_pre[rows, :] = value.astype(BF16)
        bias_acc[:, at] = line
        to = pl.ds(pl.multiple_of(n * 128, 128), 128)
        for m in range(4):
            value = dot(tok_t[m * 256 : m * 256 + 256, :], d_pre[...])
            value = value.reshape(32, 8, 256)
            value = jnp.concatenate([value[:, :, :128], value[:, :, 128:]], axis=1).astype(BF16)
            part[1, m, :, :, :, :, to] = value.reshape(2, 4, 4, 16, 128)
        return carry

    ones, twos, threes = {}, {}, {}

    def run_part(p):
        lo, hi = PARTS[1][p]
        lax.fori_loop(lo // 128, hi // 128, back_layer, 0)
        cut = pl.ds(lo, hi - lo)
        zero[1, p] = push(
            part.at[1, :, 1 - k, :, :, :, cut], r0.at[1, :, :, :, :, cut], sem0.at[1, p], rsem0.at[1, p], sibling
        )

    run_part(0)
    for zz in range(4):
        zero[0, zz].wait_recv()
        add_core(0, 0, 1024, 16 * zz, 16 * zz + 16)
    for p in range(3):
        ones[0, p] = stage_one(0, p)
    arrived(slope_step)
    slope_step = slopes(3)
    sent += slope_step

    def finish_core(p):
        zero[1, p].wait_recv()
        add_core(1, PARTS[1][p][0], PARTS[1][p][1], 0, 64)
        ones[1, p] = stage_one(1, p)

    run_part(1)
    finish_core(0)
    run_part(2)
    finish_core(1)

    sm[0, k] = jnp.concatenate(
        [bias_acc[:, :1024], bias_acc[:, 1024:], grad_bias_out, grad_gain, grad_shift, jnp.zeros((3, 1024), F32)], axis=0
    )
    small = [push(sm.at[0, k], sm.at[0, k], qs.at[0, 0], qr.at[0, 0], sibling)]
    sent += small

    def stage_small(step):
        dim = step - 1
        got = sm[step - 1, 0] + sm[step - 1, 1]
        if step > 1:
            got = (got + sm[step - 1, 2]) + sm[step - 1, 3]
        sm[step, coord[dim]] = got
        copies = []
        for j in (1, 2, 3):
            peer, _ = moved(here, dim, j)
            mine = sm.at[step, coord[dim]]
            copies.append(push(mine, mine, qs.at[step, j - 1], qr.at[step, j - 1], peer))
        return copies

    def second_stage(w, p):
        arrived(ones[w, p])
        add_one(w, p)
        twos[w, p] = stage_two(w, p)

    def third_stage(w, p):
        arrived(twos[w, p])
        add_two(w, p)
        threes[w, p] = stage_three(w, p)

    def end_stage(w, p):
        arrived(threes[w, p])
        add_three(w, p)

    for p in range(3):
        second_stage(0, p)
    finish_core(2)
    arrived(small)
    small = stage_small(1)
    sent += small
    arrived(slope_step)
    arrived(last)

    base = c * 1024 + (y * 4 + x) * 64
    row = (lax.broadcasted_iota(jnp.int32, (256, 128), 1) + base).astype(F32)

    def collect(i, carry):
        name, value = idall[i].reshape(256, 128), cg[i].reshape(256, 128)
        weight = jnp.zeros((256, 128), F32)
        for slot in range(12):
            weight += jnp.where(name[:, slot : slot + 1] == row, value[:, slot : slot + 1], 0.0)
        high = weight.astype(BF16)
        low = (weight - high.astype(F32)).astype(BF16)
        some = qall[i].astype(F32).reshape(32, 16, 512)
        halves = []
        for h in range(2):
            half = some[:, h * 8 : h * 8 + 8].reshape(256, 512).astype(BF16)
            halves.append(dot(high, half, 0, 0) + dot(low, half, 0, 0))
        return tuple(a + b[:64] for a, b in zip(carry, halves))

    sums = lax.fori_loop(0, 4, collect, (jnp.zeros((64, 512), F32),) * 2)
    table_slope = jnp.concatenate(sums, axis=1)
    rows = tab_own[...].astype(F32)
    scale = lax.rsqrt(jnp.sum(rows * rows, axis=1, keepdims=True) + norm_eps)
    unit = rows * scale
    g_table[...] = scale * (table_slope - unit * jnp.sum(unit * table_slope, axis=1, keepdims=True))

    for p in range(3):
        third_stage(0, p)
    arrived(small)
    small = stage_small(2)
    sent += small
    for p in range(3):
        second_stage(1, p)
    arrived(small)
    small = stage_small(3)
    sent += small
    for p in range(3):
        end_stage(0, p)
    for p in range(3):
        third_stage(1, p)
    arrived(small)
    got = ((sm[3, 0] + sm[3, 1]) + sm[3, 2]) + sm[3, 3]
    g_bias_in[:, :1024] = got[0:1]
    g_bias_in[:, 1024:] = got[1:2]
    g_bias_out[...] = got[2:3]
    g_gain[...] = got[3:4]
    g_shift[...] = got[4:5]
    for p in range(3):
        end_stage(1, p)
    for group in (ones, twos, threes):
        for copies in group.values():
            sent += copies
    for copy in sent + list(zero.values()):
        copy.wait_send()


def step(*operands):
    vmem, hbm = pl.BlockSpec(memory_space=pltpu.VMEM), pl.BlockSpec(memory_space=pl.ANY)

    def scratch(shape, kind):
        return tuple(tuple(pltpu.VMEM(shape + (16, hi - lo), kind) for lo, hi in row) for row in PARTS)

    dma = pltpu.SemaphoreType.DMA
    out = jax.ShapeDtypeStruct
    return pl.pallas_call(
        step_kernel,
        out_shape=(
            out((8, 2048), F32),
            out((1, 2048), F32),
            out((16, 1024), F32),
            out((1, 1024), F32),
            out((1, 1024), F32),
            out((1, 1024), F32),
            out((64, 1024), F32),
        ),
        in_specs=[hbm] * 4 + [vmem] * 8,
        out_specs=(vmem,) * 7,
        scratch_shapes=[
            pltpu.VMEM((1024, 1024), BF16),
            pltpu.VMEM((1024, 2048), BF16),
            pltpu.VMEM((2048, 1024), BF16),
            pltpu.VMEM((1024, 1024), BF16),
            pltpu.VMEM((64, 1024), BF16),
            pltpu.VMEM((1024, 1024), BF16),
            pltpu.VMEM((1024, 2048), BF16),
            pltpu.VMEM((1024, 2048), F32),
            pltpu.VMEM((1024, 1024), F32),
            pltpu.VMEM((1024, 128), F32),
            pltpu.VMEM((1024, 1024), BF16),
            pltpu.VMEM((1024, 256), BF16),
            pltpu.VMEM((1, 2048), F32),
            pltpu.VMEM((4, 2, 4, 4, 16, 512), BF16),
            pltpu.VMEM((4, 2, 4, 4, 8, 128), F32),
            pltpu.VMEM((2, 4, 16, 512), BF16),
            pltpu.VMEM((2, 4, 8, 128), F32),
            pltpu.VMEM((16, 128), F32),
            pltpu.VMEM((7, 16, 128), F32),
            pltpu.VMEM((128, 128), F32),
            pltpu.VMEM((2, 4, 2, 4, 4, 16, 1024), BF16),
            pltpu.VMEM((2, 4, 4, 4, 16, 1024), BF16),
            scratch((3, 4, 4), BF16),
            scratch((4, 4), BF16),
            scratch((3, 4), BF16),
            scratch((4,), F32),
            scratch((3,), F32),
            pltpu.VMEM((4, 4, 8, 1024), F32),
            pltpu.VMEM((4, 2, 4, 4, 8, 128), F32),
            dma((8,)),
            dma((5, 2, 3)),
            dma((5, 2, 3)),
            dma((7,)),
            dma((7,)),
            dma((2, 4)),
            dma((2, 4)),
            dma((3, 2, 3, 3)),
            dma((3, 2, 3, 3)),
            dma((4, 3)),
            dma((4, 3)),
            dma((4, 3)),
            dma((4, 3)),
        ],
        compiler_params=pltpu.CompilerParams(
            collective_id=0, has_side_effects=True, vmem_limit_bytes=VMEM_BYTES
        ),
    )(*operands)


def body(
    tokens,
    weight_in,
    bias_in,
    weight_out,
    bias_out,
    norm_gain,
    norm_shift,
    queries,
    corpus_table,
    neg_owner,
    neg_row,
    neg_count,
):
    count_q, seq, width = tokens.shape
    slots = neg_row.shape[1]
    ids = (neg_owner.reshape(count_q, slots) * 1024 + neg_row).astype(F32)
    ids = jnp.pad(ids, ((0, 0), (0, 128 - slots)), constant_values=-1.0)
    q_half = jnp.concatenate([queries[:, :512], queries[:, 512:]], axis=0)
    counts = jnp.broadcast_to(neg_count[:, None], (count_q, 128))
    grad_in, g_bias_in, grad_out, g_bias_out, g_gain, g_shift, grad_table = step(
        tokens.reshape(count_q * seq, width),
        weight_in,
        weight_out,
        corpus_table,
        bias_in[None],
        bias_out[None],
        norm_gain[None],
        norm_shift[None],
        queries,
        q_half,
        ids,
        counts,
    )
    return (grad_in, g_bias_in[0], grad_out, g_bias_out[0], g_gain[0], g_shift[0], grad_table)


def solution(mesh):
    return jax.shard_map(
        body,
        mesh=mesh,
        in_specs=(
            P(("corpus", "batch"), None, None),
            P(),
            P(),
            P(),
            P(),
            P(),
            P(),
            P(("corpus", "batch"), None),
            P("corpus", None),
            P(("corpus", "batch"), None, None),
            P(("corpus", "batch"), None),
            P(("corpus", "batch")),
        ),
        out_specs=(
            P(("corpus", "batch"), None),
            P(),
            P(("corpus", "batch"), None),
            P(),
            P(),
            P(),
            P(("corpus", "batch"), None),
        ),
        check_vma=False,
    )
```

```python
import functools

import jax
import jax.numpy as jnp
from jax import lax
from jax.experimental import pallas as pl
from jax.experimental.pallas import tpu as pltpu
from jax.sharding import PartitionSpec as P

logit_divisor = 0.05
norm_eps = 1e-06
MESH = pl.DeviceIdType.MESH
F32, BF16 = jnp.float32, jnp.bfloat16
VMEM_BYTES = 60 * 1024 * 1024


def place():
    c, b = lax.axis_index("corpus"), lax.axis_index("batch")
    return c // 2, c % 2, b // 4, b % 4


def device(z, k, y, x):
    return (z * 2 + k, y * 4 + x)


def moved(here, dim, offset):
    z, k, y, x = here
    at = [z, y, x]
    at[dim] = lax.rem(at[dim] + offset, 4)
    return device(at[0], k, at[1], at[2]), at[dim]


def put(here, dim, to):
    z, k, y, x = here
    at = [z, y, x]
    at[dim] = to
    return device(at[0], k, at[1], at[2])


def greet(peers):
    barrier = pltpu.get_barrier_semaphore()
    for peer in peers:
        pl.semaphore_signal(barrier, inc=1, device_id=peer, device_id_type=MESH)
    pl.semaphore_wait(barrier, len(peers))


def push(src, dst, send, recv, peer):
    copy = pltpu.make_async_remote_copy(
        src_ref=src, dst_ref=dst, send_sem=send, recv_sem=recv, device_id=peer, device_id_type=MESH
    )
    copy.start()
    return copy


PARTS = (((0, 384), (384, 768), (768, 1024)), ((0, 384), (384, 640), (640, 1024)))
ORDER = ((0, 1, 2), (1, 2, 0), (2, 0, 1))


def pick(ref, axis, index, columns=None):
    at = [slice(None)] * (len(ref.shape) - 2)
    at[axis] = index
    return ref.at[tuple(at) + (slice(None), slice(None) if columns is None else pl.ds(columns[0], columns[1] - columns[0]))]


def dot(a, b, ca=1, cb=0):
    return lax.dot_general(a, b, (((ca,), (cb,)), ((), ())), preferred_element_type=F32)


def step_kernel(
    tok_hbm, win_hbm, wout_hbm, tab_hbm, bias_in, bias_out, gain, shift, queries, slot,
    g_in, g_bias_in, g_out, g_bias_out, g_gain, g_shift, g_table,
    tok, win, wout, tab, tab_own, tok_t, hidden, slope, normed, inv_std, d_sum, d_pre, bias_acc,
    qall, idall, qcol, idcol, dots, dall, turned,
    part, r0, r1, s1, r2, t2, s2, r3, sm, cg,
    load, sems_q, semr_q, dsem, dsemr, sem0, rsem0, sems, semr, qs, qr, cs, cr,
):
    here = place()
    z, k, y, x = here
    coord = (z, y, x)
    c = z * 2 + k
    sibling = device(z, 1 - k, y, x)
    fst = [(1 - k) * (i + 1 - 2 * lax.rem(i, 2)) + k * (3 - i) for i in coord]
    snd = [k * (i + 1 - 2 * lax.rem(i, 2)) + (1 - k) * (3 - i) for i in coord]
    opp = [lax.rem(i + 2, 4) for i in coord]
    sent = []

    def local(src, dst, n):
        copy = pltpu.make_async_copy(src, dst, load.at[n])
        copy.start()
        return copy

    tok_in = local(tok_hbm, tok, 0)
    win_in = [local(win_hbm.at[:, pl.ds(512 * n, 512)], win.at[:, pl.ds(512 * n, 512)], 1 + n) for n in range(4)]
    tab_in = local(tab_hbm, tab, 5)
    wout_in = local(wout_hbm, wout, 6)
    own_in = local(tab_hbm.at[pl.ds(pl.multiple_of((y * 4 + x) * 64, 64), 64), :], tab_own, 7)

    column = []
    for j in range(4):
        for e in range(2):
            if j or e:
                column.append(device(lax.rem(z + j, 4), lax.rem(k + e, 2), y, x))
    greet(column + [moved(here, dim, j)[0] for dim in (1, 2) for j in (1, 2, 3)])

    query = queries[...].astype(F32)
    qall[z, k, y, x] = jnp.concatenate([query[:, :512], query[:, 512:]], axis=0).astype(BF16)
    lane = lax.broadcasted_iota(jnp.int32, (8, 128), 1)
    idall[z, k, y, x] = jnp.where(lane < 12, slot[...], -1.0)
    payload = ((0, qall), (1, idall))
    first = []
    for j in (1, 2, 3):
        peer, _ = moved(here, 0, j)
        for n, buf in payload:
            mine = buf.at[z, k, y, x]
            first.append(push(mine, mine, sems_q.at[0, n, j - 1], semr_q.at[0, n, j - 1], peer))

    def gather_second():
        for copy in first:
            copy.wait_recv()
        copies = []
        for n, buf, dst in ((0, qall, qcol), (1, idall, idcol)):
            copies.append(push(buf.at[:, k, y, x], dst.at[k], sems_q.at[1, n, 0], semr_q.at[1, n, 0], sibling))
        for j in (1, 2, 3):
            peer, _ = moved(here, 1, j)
            for n, buf in payload:
                mine = buf.at[:, k, y, x]
                copies.append(push(mine, mine, sems_q.at[2, n, j - 1], semr_q.at[2, n, j - 1], peer))
        qcol[k] = qall[:, k, y, x]
        idcol[k] = idall[:, k, y, x]
        return copies

    def gather_third():
        copies = []
        for m, to in enumerate((fst[2], snd[2])):
            for n, buf in payload:
                mine = buf.at[:, k, :, x]
                copies.append(push(mine, mine, sems_q.at[3, n, m], semr_q.at[3, n, m], put(here, 2, to)))
        return copies

    def gather_fourth():
        for copy in third[:2]:
            copy.wait_recv()
        copies = []
        for n, buf in payload:
            near = buf.at[:, k, :, fst[2]]
            copies.append(push(near, near, sems_q.at[3, n, 2], semr_q.at[3, n, 2], put(here, 2, snd[2])))
        return copies

    def gather_last():
        copies = []
        for n, buf in payload:
            mine = buf.at[:, k]
            copies.append(push(mine, mine, sems_q.at[4, n, 0], semr_q.at[4, n, 0], sibling))
        return copies

    def project(n, carry):
        at = pl.ds(pl.multiple_of(n * 256, 256), 256)
        weight = win[:, at]
        bias = bias_in[:, at]
        for m in range(4):
            rows = slice(m * 256, m * 256 + 256)
            pre = dot(tok[rows, :], weight) + bias
            cdf = 0.5 * (1.0 + lax.erf(pre * 0.7071067811865476))
            hidden[rows, at] = (pre * cdf).astype(BF16)
            slope[rows, at] = cdf + pre * 0.3989422804014327 * jnp.exp(-0.5 * pre * pre)
        turn = pl.ds(pl.multiple_of(n * 128, 128), 128)
        tok_t[turn, :] = tok[:, turn].T
        return carry

    tok_in.wait()
    win_in[0].wait()
    lax.fori_loop(0, 2, project, 0)
    second = gather_second()
    win_in[1].wait()
    lax.fori_loop(2, 4, project, 0)
    for copy in second:
        copy.wait_recv()
    third = gather_third()
    sent += first + second + third

    tab_in.wait()
    own_in.wait()
    wide_q = qcol[...].astype(F32).reshape(8, 16, 512)
    left = wide_q[:, :8].reshape(64, 512).astype(BF16)
    right = wide_q[:, 8:].reshape(64, 512).astype(BF16)
    ids = jnp.concatenate([idcol[...].reshape(64, 128), jnp.zeros((64, 128), F32)], axis=0).T[:16, :64]
    dots[...] = jnp.zeros_like(dots)

    def score_rows(i, carry):
        start = pl.multiple_of(i * 128, 128)
        block = tab[pl.ds(start, 128), :]
        wide = block.astype(F32)
        scale = lax.rsqrt(jnp.sum(wide * wide, axis=1, keepdims=True) + norm_eps)
        score = (dot(block[:, :512], left, 1, 1) + dot(block[:, 512:], right, 1, 1)) * scale
        names = (lax.broadcasted_iota(jnp.int32, (128, 64), 0) + (start + c * 1024)).astype(F32)
        found = []
        for slot in range(12):
            hit = jnp.where(names == ids[slot : slot + 1, :], score, 0.0)
            found.append(jnp.sum(hit, axis=0, keepdims=True))
        found.append(jnp.zeros((4, 64), F32))
        dots[:, :64] += jnp.concatenate(found, axis=0)
        return carry

    lax.fori_loop(0, 8, score_rows, 0)
    back = [push(dots, dall.at[n], dsem.at[n], dsemr.at[n], peer) for n, peer in enumerate(column)]
    sent += back

    win_in[2].wait()
    win_in[3].wait()
    lax.fori_loop(4, 8, project, 0)

    fourth = gather_fourth()
    sent += fourth

    wout_in.wait()
    which = lax.broadcasted_iota(jnp.int32, (8, 1024), 0)

    def normalise(i, carry):
        rows = pl.ds(pl.multiple_of(i * 256, 256), 256)
        summed = tok[rows, :].astype(F32) + dot(hidden[rows, :], wout[...]) + bias_out[...]
        centred = summed - jnp.mean(summed, axis=1, keepdims=True)
        inv = lax.rsqrt(jnp.mean(centred * centred, axis=1, keepdims=True) + norm_eps)
        value = centred * inv
        normed[rows, :] = value
        inv_std[rows, :] = jnp.broadcast_to(inv, (256, 128))
        for h in range(2):
            line = jnp.sum(value[h * 128 : h * 128 + 128], axis=0, keepdims=True)
            carry = jnp.where(which == 2 * i + h, line, carry)
        return carry

    norm_sum = lax.fori_loop(0, 4, normalise, jnp.zeros((8, 1024), F32))

    for copy in back:
        copy.wait_recv()
    total = dots[...]
    for n in range(7):
        total += dall[n]
    turned[...] = jnp.concatenate([total, jnp.zeros((112, 128), F32)], axis=0).T
    raw = turned[pl.ds(pl.multiple_of((k * 4 + z) * 8, 8), 8), :]
    pooled = norm_sum * gain[...] + 128.0 * shift[...]
    emb_scale = lax.rsqrt(jnp.sum(pooled * pooled, axis=1, keepdims=True) + norm_eps)
    emb = pooled * emb_scale
    q_scale = lax.rsqrt(jnp.sum(query * query, axis=1, keepdims=True) + norm_eps)
    question = query * q_scale
    positive = jnp.sum(question * emb, axis=1, keepdims=True) / logit_divisor
    live = lane.astype(F32) < slot[:, 12:13]
    weights = jnp.where(live, jnp.exp(raw * q_scale / logit_divisor), 0.0)
    own = jnp.exp(positive)
    whole = own + jnp.sum(weights, axis=1, keepdims=True)
    cg[z, k, y, x] = weights / whole / logit_divisor * q_scale
    emb_slope = ((own / whole - 1.0) / logit_divisor) * question
    d_pooled = emb_scale * (emb_slope - emb * jnp.sum(emb * emb_slope, axis=1, keepdims=True))
    grad_shift = jnp.sum(d_pooled, axis=0, keepdims=True) * 128.0
    grad_gain = jnp.sum(d_pooled * norm_sum, axis=0, keepdims=True)
    lead = d_pooled * gain[...]

    def slopes(step):
        if step == 0:
            mine = cg.at[z, k, y, x]
            return [push(mine, mine, cs.at[0, 0], cr.at[0, 0], sibling)]
        dim = step - 1
        every = slice(None)
        mine = cg.at[((z, every, y, x), (every, every, y, x), (every, every, every, x))[dim]]
        copies = []
        for j in (1, 2, 3):
            peer, _ = moved(here, dim, j)
            copies.append(push(mine, mine, cs.at[step, j - 1], cr.at[step, j - 1], peer))
        return copies

    def arrived(copies):
        for copy in copies:
            copy.wait_recv()

    slope_step = slopes(0)
    sent += slope_step

    def back_norm(i, carry):
        rows = pl.ds(pl.multiple_of(i * 128, 128), 128)
        g = jnp.sum(jnp.where(which == i, lead, 0.0), axis=0, keepdims=True)
        value = normed[rows, :]
        inv = inv_std[rows, :][:, :1]
        both = jnp.mean(value * g, axis=1, keepdims=True)
        ds = inv * (g - jnp.mean(g, axis=1, keepdims=True) - value * both)
        d_sum[rows, :] = ds.astype(BF16)
        return carry + jnp.sum(ds, axis=0, keepdims=True)

    grad_bias_out = lax.fori_loop(0, 8, back_norm, jnp.zeros((1, 1024), F32))
    for copy in third[2:] + fourth:
        copy.wait_recv()
    last = gather_last()
    sent += last
    arrived(slope_step)
    slope_step = slopes(1)
    sent += slope_step

    def grad_out(zz, core):
        at = pl.ds(pl.multiple_of((zz * 2 + core) * 256, 256), 256)
        value = dot(hidden[:, at], d_sum[...], 0, 0)
        part[0, zz, core] = value.astype(BF16).reshape(4, 4, 16, 1024)

    zero = {}
    for zz in range(4):
        grad_out(zz, 1 - k)
        zero[0, zz] = push(part.at[0, zz, 1 - k], r0.at[0, zz], sem0.at[0, zz], rsem0.at[0, zz], sibling)

    def own_blocks(zz, carry):
        grad_out(zz, k)
        return carry

    lax.fori_loop(0, 4, own_blocks, 0)
    arrived(slope_step)
    slope_step = slopes(2)
    sent += slope_step

    def add_core(w, lo, hi, first, last):
        def one(i, carry):
            a, e, f = i // 16, lax.rem(i // 4, 4), lax.rem(i, 4)
            r0[w, a, e, f, :, lo:hi] = (
                r0[w, a, e, f, :, lo:hi].astype(F32) + part[w, a, k, e, f, :, lo:hi].astype(F32)
            ).astype(BF16)
            return carry
        lax.fori_loop(first, last, one, 0)

    def swap(dim, w, p, step, near, far, land):
        peer = put(here, dim, fst[dim])
        return [
            push(far, land[0], sems.at[step, w, p, 0], semr.at[step, w, p, 0], peer),
            push(near, land[1], sems.at[step, w, p, 1], semr.at[step, w, p, 1], peer),
        ]

    def relay(dim, w, p, step, src, land):
        return [push(src, land, sems.at[step, w, p, 2], semr.at[step, w, p, 2], put(here, dim, snd[dim]))]

    def rest(p):
        return [d for d in (0, 1, 2) if d != ORDER[p][0]]

    def stage_one(w, p):
        dim = ORDER[p][0]
        cut = PARTS[w][p]
        near, far = pick(r0.at[w], dim, fst[dim], cut), pick(r0.at[w], dim, opp[dim], cut)
        return swap(dim, w, p, 0, near, far, (r1[w][p].at[0], r1[w][p].at[1]))

    def relay_one(w, p):
        dim = ORDER[p][0]
        mine = pick(r0.at[w], dim, snd[dim], PARTS[w][p])

        def one(i, carry):
            e, f = i // 4, lax.rem(i, 4)
            mine[e, f] = (mine[e, f].astype(F32) + r1[w][p][0, e, f].astype(F32)).astype(BF16)
            return carry
        lax.fori_loop(0, 16, one, 0)
        return relay(dim, w, p, 0, mine, r1[w][p].at[2])

    def add_one(w, p):
        dim = ORDER[p][0]
        mine = pick(r0.at[w], dim, coord[dim], PARTS[w][p])

        def one(i, carry):
            e, f = i // 4, lax.rem(i, 4)
            value = mine[e, f].astype(F32) + r1[w][p][1, e, f].astype(F32) + r1[w][p][2, e, f].astype(F32)
            s1[w][p][e, f] = value.astype(BF16)
            return carry
        lax.fori_loop(0, 16, one, 0)

    def stage_two(w, p):
        dim = ORDER[p][1]
        axis = rest(p).index(dim)
        near, far = pick(s1[w][p], axis, fst[dim]), pick(s1[w][p], axis, opp[dim])
        return swap(dim, w, p, 1, near, far, (r2[w][p].at[0], r2[w][p].at[1]))

    def relay_two(w, p):
        dim = ORDER[p][1]
        mine = pick(s1[w][p], rest(p).index(dim), snd[dim])
        for e in range(4):
            t2[w][p][0, e] = mine[e].astype(F32) + r2[w][p][0, e].astype(F32)
        return relay(dim, w, p, 1, t2[w][p].at[0], t2[w][p].at[1])

    def add_two(w, p):
        dim = ORDER[p][1]
        mine = pick(s1[w][p], rest(p).index(dim), coord[dim])
        for e in range(4):
            s2[w][p][e] = mine[e].astype(F32) + r2[w][p][1, e].astype(F32) + t2[w][p][1, e]

    def stage_three(w, p):
        dim = ORDER[p][2]
        return swap(dim, w, p, 2, s2[w][p].at[fst[dim]], s2[w][p].at[opp[dim]], (r3[w][p].at[0], r3[w][p].at[1]))

    def relay_three(w, p):
        dim = ORDER[p][2]
        s2[w][p][snd[dim]] += r3[w][p][0]
        return relay(dim, w, p, 2, s2[w][p].at[snd[dim]], r3[w][p].at[2])

    def add_three(w, p):
        lo, hi = PARTS[w][p]
        value = s2[w][p][coord[ORDER[p][2]]] + r3[w][p][1] + r3[w][p][2]
        if w == 0:
            g_out[:, lo:hi] = value
        else:
            for n in range((hi - lo) // 128):
                tile = value[:, n * 128 : n * 128 + 128]
                g_in[:, 2 * lo + 256 * n : 2 * lo + 256 * n + 128] = tile[:8]
                g_in[:, 2 * lo + 256 * n + 128 : 2 * lo + 256 * n + 256] = tile[8:]

    def back_layer(n, carry):
        at = pl.ds(pl.multiple_of(n * 256, 256), 256)
        weight = wout[at, :]
        line = jnp.zeros((1, 256), F32)
        for m in range(4):
            rows = slice(m * 256, m * 256 + 256)
            value = dot(d_sum[rows, :], weight, 1, 1) * slope[rows, at]
            line += jnp.sum(value, axis=0, keepdims=True)
            d_pre[rows, :] = value.astype(BF16)
        bias_acc[:, at] = line
        to = pl.ds(pl.multiple_of(n * 128, 128), 128)
        for m in range(4):
            value = dot(tok_t[m * 256 : m * 256 + 256, :], d_pre[...])
            value = value.reshape(32, 8, 256)
            value = jnp.concatenate([value[:, :, :128], value[:, :, 128:]], axis=1).astype(BF16)
            part[1, m, :, :, :, :, to] = value.reshape(2, 4, 4, 16, 128)
        return carry

    ones, twos, threes = {}, {}, {}
    groups = (ones, twos, threes)

    def start(step, w, p):
        groups[step][w, p] = (stage_one, stage_two, stage_three)[step](w, p)

    def pass_on(step, w, p):
        groups[step][w, p][0].wait_recv()
        groups[step][w, p] += (relay_one, relay_two, relay_three)[step](w, p)

    def end(step, w, p):
        for copy in groups[step][w, p][1:]:
            copy.wait_recv()
        (add_one, add_two, add_three)[step](w, p)
        if step < 2:
            start(step + 1, w, p)

    def run_part(p):
        lo, hi = PARTS[1][p]
        lax.fori_loop(lo // 128, hi // 128, back_layer, 0)
        cut = pl.ds(lo, hi - lo)
        zero[1, p] = push(
            part.at[1, :, 1 - k, :, :, :, cut], r0.at[1, :, :, :, :, cut], sem0.at[1, p], rsem0.at[1, p], sibling
        )

    def finish_core(p):
        zero[1, p].wait_recv()
        add_core(1, PARTS[1][p][0], PARTS[1][p][1], 0, 64)
        start(0, 1, p)

    for zz in range(4):
        zero[0, zz].wait_recv()
        add_core(0, 0, 1024, 16 * zz, 16 * zz + 16)
    for p in range(3):
        start(0, 0, p)
    run_part(0)
    for p in range(3):
        pass_on(0, 0, p)
    arrived(slope_step)
    slope_step = slopes(3)
    sent += slope_step
    run_part(1)
    finish_core(0)
    for p in range(3):
        end(0, 0, p)
    run_part(2)
    finish_core(1)
    pass_on(0, 1, 0)
    for p in range(3):
        pass_on(1, 0, p)

    sm[0, k] = jnp.concatenate(
        [bias_acc[:, :1024], bias_acc[:, 1024:], grad_bias_out, grad_gain, grad_shift, jnp.zeros((3, 1024), F32)], axis=0
    )
    small = [push(sm.at[0, k], sm.at[0, k], qs.at[0, 0], qr.at[0, 0], sibling)]
    sent += small

    def stage_small(step):
        dim = step - 1
        got = sm[step - 1, 0] + sm[step - 1, 1]
        if step > 1:
            got = (got + sm[step - 1, 2]) + sm[step - 1, 3]
        sm[step, coord[dim]] = got
        copies = []
        for j in (1, 2, 3):
            peer, _ = moved(here, dim, j)
            mine = sm.at[step, coord[dim]]
            copies.append(push(mine, mine, qs.at[step, j - 1], qr.at[step, j - 1], peer))
        return copies

    finish_core(2)
    pass_on(0, 1, 1)
    end(0, 1, 0)
    for p in range(3):
        end(1, 0, p)
    arrived(small)
    small = stage_small(1)
    sent += small
    arrived(slope_step)
    arrived(last)
    pass_on(0, 1, 2)
    end(0, 1, 1)
    pass_on(1, 1, 0)
    for p in range(3):
        pass_on(2, 0, p)

    base = c * 1024 + (y * 4 + x) * 64
    row = (lax.broadcasted_iota(jnp.int32, (256, 128), 1) + base).astype(F32)

    def collect(i, carry):
        name, value = idall[i].reshape(256, 128), cg[i].reshape(256, 128)
        weight = jnp.zeros((256, 128), F32)
        for slot in range(12):
            weight += jnp.where(name[:, slot : slot + 1] == row, value[:, slot : slot + 1], 0.0)
        high = weight.astype(BF16)
        low = (weight - high.astype(F32)).astype(BF16)
        some = qall[i].astype(F32).reshape(32, 16, 512)
        halves = []
        for h in range(2):
            half = some[:, h * 8 : h * 8 + 8].reshape(256, 512).astype(BF16)
            halves.append(dot(high, half, 0, 0) + dot(low, half, 0, 0))
        return tuple(a + b[:64] for a, b in zip(carry, halves))

    sums = lax.fori_loop(0, 4, collect, (jnp.zeros((64, 512), F32),) * 2)
    table_slope = jnp.concatenate(sums, axis=1)
    rows = tab_own[...].astype(F32)
    scale = lax.rsqrt(jnp.sum(rows * rows, axis=1, keepdims=True) + norm_eps)
    unit = rows * scale
    g_table[...] = scale * (table_slope - unit * jnp.sum(unit * table_slope, axis=1, keepdims=True))

    end(0, 1, 2)
    pass_on(1, 1, 1)
    arrived(small)
    small = stage_small(2)
    sent += small
    end(1, 1, 0)
    pass_on(1, 1, 2)
    for p in range(3):
        end(2, 0, p)
    end(1, 1, 1)
    pass_on(2, 1, 0)
    arrived(small)
    small = stage_small(3)
    sent += small
    end(1, 1, 2)
    pass_on(2, 1, 1)
    pass_on(2, 1, 2)
    arrived(small)
    got = ((sm[3, 0] + sm[3, 1]) + sm[3, 2]) + sm[3, 3]
    g_bias_in[:, :1024] = got[0:1]
    g_bias_in[:, 1024:] = got[1:2]
    g_bias_out[...] = got[2:3]
    g_gain[...] = got[3:4]
    g_shift[...] = got[4:5]
    for p in range(3):
        end(2, 1, p)
    for group in groups:
        for copies in group.values():
            sent += copies
    for copy in sent + list(zero.values()):
        copy.wait_send()


def hand_over_kernel(*refs):
    for src, dst in zip(refs[:7], refs[7:]):
        dst[...] = src[...]


def hand_over(*results):
    vmem = pl.BlockSpec(memory_space=pltpu.VMEM)
    return pl.pallas_call(
        hand_over_kernel,
        out_shape=tuple(jax.ShapeDtypeStruct(value.shape, value.dtype) for value in results),
        in_specs=[vmem] * 7,
        out_specs=(vmem,) * 7,
    )(*results)


def step(*operands):
    vmem, hbm = pl.BlockSpec(memory_space=pltpu.VMEM), pl.BlockSpec(memory_space=pl.ANY)

    def scratch(shape, kind):
        return tuple(tuple(pltpu.VMEM(shape + (16, hi - lo), kind) for lo, hi in row) for row in PARTS)

    dma = pltpu.SemaphoreType.DMA
    out = jax.ShapeDtypeStruct
    return pl.pallas_call(
        step_kernel,
        out_shape=(
            out((8, 2048), F32),
            out((1, 2048), F32),
            out((16, 1024), F32),
            out((1, 1024), F32),
            out((1, 1024), F32),
            out((1, 1024), F32),
            out((64, 1024), F32),
        ),
        in_specs=[hbm] * 4 + [vmem] * 6,
        out_specs=(vmem,) * 7,
        scratch_shapes=[
            pltpu.VMEM((1024, 1024), BF16),
            pltpu.VMEM((1024, 2048), BF16),
            pltpu.VMEM((2048, 1024), BF16),
            pltpu.VMEM((1024, 1024), BF16),
            pltpu.VMEM((64, 1024), BF16),
            pltpu.VMEM((1024, 1024), BF16),
            pltpu.VMEM((1024, 2048), BF16),
            pltpu.VMEM((1024, 2048), F32),
            pltpu.VMEM((1024, 1024), F32),
            pltpu.VMEM((1024, 128), F32),
            pltpu.VMEM((1024, 1024), BF16),
            pltpu.VMEM((1024, 256), BF16),
            pltpu.VMEM((1, 2048), F32),
            pltpu.VMEM((4, 2, 4, 4, 16, 512), BF16),
            pltpu.VMEM((4, 2, 4, 4, 8, 128), F32),
            pltpu.VMEM((2, 4, 16, 512), BF16),
            pltpu.VMEM((2, 4, 8, 128), F32),
            pltpu.VMEM((16, 128), F32),
            pltpu.VMEM((7, 16, 128), F32),
            pltpu.VMEM((128, 128), F32),
            pltpu.VMEM((2, 4, 2, 4, 4, 16, 1024), BF16),
            pltpu.VMEM((2, 4, 4, 4, 16, 1024), BF16),
            scratch((3, 4, 4), BF16),
            scratch((4, 4), BF16),
            scratch((2, 4), BF16),
            scratch((2, 4), F32),
            scratch((4,), F32),
            scratch((3,), F32),
            pltpu.VMEM((4, 4, 8, 1024), F32),
            pltpu.VMEM((4, 2, 4, 4, 8, 128), F32),
            dma((8,)),
            dma((5, 2, 3)),
            dma((5, 2, 3)),
            dma((7,)),
            dma((7,)),
            dma((2, 4)),
            dma((2, 4)),
            dma((3, 2, 3, 3)),
            dma((3, 2, 3, 3)),
            dma((4, 3)),
            dma((4, 3)),
            dma((4, 3)),
            dma((4, 3)),
        ],
        compiler_params=pltpu.CompilerParams(
            collective_id=0, has_side_effects=True, vmem_limit_bytes=VMEM_BYTES
        ),
    )(*operands)


def body(
    tokens,
    weight_in,
    bias_in,
    weight_out,
    bias_out,
    norm_gain,
    norm_shift,
    queries,
    corpus_table,
    neg_owner,
    neg_row,
    neg_count,
):
    count_q, seq, width = tokens.shape
    slots = neg_row.shape[1]
    ids = (neg_owner.reshape(count_q, slots) * 1024 + neg_row).astype(F32)
    counts = neg_count.astype(F32)[:, None]
    slot = jnp.concatenate([ids, counts, jnp.full((count_q, 128 - slots - 1), -1.0, F32)], axis=1)
    results = step(
        tokens.reshape(count_q * seq, width),
        weight_in,
        weight_out,
        corpus_table,
        bias_in[None],
        bias_out[None],
        norm_gain[None],
        norm_shift[None],
        queries,
        slot,
    )
    grad_in, g_bias_in, grad_out, g_bias_out, g_gain, g_shift, grad_table = hand_over(*results)
    return (grad_in, g_bias_in[0], grad_out, g_bias_out[0], g_gain[0], g_shift[0], grad_table)


def solution(mesh):
    return jax.shard_map(
        body,
        mesh=mesh,
        in_specs=(
            P(("corpus", "batch"), None, None),
            P(),
            P(),
            P(),
            P(),
            P(),
            P(),
            P(("corpus", "batch"), None),
            P("corpus", None),
            P(("corpus", "batch"), None, None),
            P(("corpus", "batch"), None),
            P(("corpus", "batch")),
        ),
        out_specs=(
            P(("corpus", "batch"), None),
            P(),
            P(("corpus", "batch"), None),
            P(),
            P(),
            P(),
            P(("corpus", "batch"), None),
        ),
        check_vma=False,
    )
```

```python
import functools

import jax
import jax.numpy as jnp
from jax import lax
from jax.experimental import pallas as pl
from jax.experimental.pallas import tpu as pltpu
from jax.sharding import PartitionSpec as P

logit_divisor = 0.05
norm_eps = 1e-06
MESH = pl.DeviceIdType.MESH
F32, BF16 = jnp.float32, jnp.bfloat16
VMEM_BYTES = 60 * 1024 * 1024


def place():
    c, b = lax.axis_index("corpus"), lax.axis_index("batch")
    return c // 2, c % 2, b // 4, b % 4


def device(z, k, y, x):
    return (z * 2 + k, y * 4 + x)


def moved(here, dim, offset):
    z, k, y, x = here
    at = [z, y, x]
    at[dim] = lax.rem(at[dim] + offset, 4)
    return device(at[0], k, at[1], at[2]), at[dim]


def put(here, dim, to):
    z, k, y, x = here
    at = [z, y, x]
    at[dim] = to
    return device(at[0], k, at[1], at[2])


def greet(peers):
    barrier = pltpu.get_barrier_semaphore()
    for peer in peers:
        pl.semaphore_signal(barrier, inc=1, device_id=peer, device_id_type=MESH)


def greeted(peers):
    pl.semaphore_wait(pltpu.get_barrier_semaphore(), len(peers))


def push(src, dst, send, recv, peer):
    copy = pltpu.make_async_remote_copy(
        src_ref=src, dst_ref=dst, send_sem=send, recv_sem=recv, device_id=peer, device_id_type=MESH
    )
    copy.start()
    return copy


PARTS = (
    ((0, 384), (384, 768), (768, 1024)),
    ((0, 256), (256, 512), (512, 640), (640, 768), (768, 896), (896, 1024)),
)
ORDER = ((0, 1, 2), (1, 2, 0), (2, 0, 1)) * 2


def pick(ref, axis, index, columns=None):
    at = [slice(None)] * (len(ref.shape) - 2)
    at[axis] = index
    return ref.at[tuple(at) + (slice(None), slice(None) if columns is None else pl.ds(columns[0], columns[1] - columns[0]))]


def dot(a, b, ca=1, cb=0):
    return lax.dot_general(a, b, (((ca,), (cb,)), ((), ())), preferred_element_type=F32)


def step_kernel(
    tok_hbm, win_hbm, wout_hbm, tab_hbm, bias_in, bias_out, gain, shift, queries, slot,
    g_in, g_bias_in, g_out, g_bias_out, g_gain, g_shift, g_table,
    tok, win, wout, tab, tab_own, tok_t, hidden, slope, normed, inv_std, d_sum, d_pre, bias_acc,
    qall, idall, qcol, idcol, dots, dall, turned,
    part, r0, r1, s1, r2, s2, r3, sm, cg,
    load, sems_q, semr_q, dsem, dsemr, sem0, rsem0, sems, semr, qs, qr, cs, cr,
):
    here = place()
    z, k, y, x = here
    coord = (z, y, x)
    c = z * 2 + k
    sibling = device(z, 1 - k, y, x)
    fst = [(1 - k) * (i + 1 - 2 * lax.rem(i, 2)) + k * (3 - i) for i in coord]
    snd = [k * (i + 1 - 2 * lax.rem(i, 2)) + (1 - k) * (3 - i) for i in coord]
    opp = [lax.rem(i + 2, 4) for i in coord]
    sent = []

    def local(src, dst, n):
        copy = pltpu.make_async_copy(src, dst, load.at[n])
        copy.start()
        return copy

    column = []
    for j in range(4):
        for e in range(2):
            if j or e:
                column.append(device(lax.rem(z + j, 4), lax.rem(k + e, 2), y, x))
    peers = column + [moved(here, dim, j)[0] for dim in (1, 2) for j in (1, 2, 3)]
    greet(peers)
    tok_in = local(tok_hbm, tok, 0)
    win_in = [local(win_hbm.at[:, pl.ds(512 * n, 512)], win.at[:, pl.ds(512 * n, 512)], 1 + n) for n in range(4)]
    tab_in = local(tab_hbm, tab, 5)
    wout_in = local(wout_hbm, wout, 6)
    own_in = local(tab_hbm.at[pl.ds(pl.multiple_of((y * 4 + x) * 64, 64), 64), :], tab_own, 7)

    query = queries[...].astype(F32)
    qall[z, k, y, x] = jnp.concatenate([query[:, :512], query[:, 512:]], axis=0).astype(BF16)
    lane = lax.broadcasted_iota(jnp.int32, (8, 128), 1)
    idall[z, k, y, x] = jnp.where(lane < 12, slot[...], -1.0)
    payload = ((0, qall), (1, idall))

    def gather_first():
        copies = []
        for j in (1, 2, 3):
            peer, _ = moved(here, 0, j)
            for n, buf in payload:
                mine = buf.at[z, k, y, x]
                copies.append(push(mine, mine, sems_q.at[0, n, j - 1], semr_q.at[0, n, j - 1], peer))
        return copies

    def gather_second():
        for copy in first:
            copy.wait_recv()
        copies = []
        for n, buf, dst in ((0, qall, qcol), (1, idall, idcol)):
            copies.append(push(buf.at[:, k, y, x], dst.at[k], sems_q.at[1, n, 0], semr_q.at[1, n, 0], sibling))
        for j in (1, 2, 3):
            peer, _ = moved(here, 1, j)
            for n, buf in payload:
                mine = buf.at[:, k, y, x]
                copies.append(push(mine, mine, sems_q.at[2, n, j - 1], semr_q.at[2, n, j - 1], peer))
        qcol[k] = qall[:, k, y, x]
        idcol[k] = idall[:, k, y, x]
        return copies

    def gather_third():
        copies = []
        for m, to in enumerate((fst[2], snd[2])):
            for n, buf in payload:
                mine = buf.at[:, k, :, x]
                copies.append(push(mine, mine, sems_q.at[3, n, m], semr_q.at[3, n, m], put(here, 2, to)))
        return copies

    def gather_fourth():
        for copy in third[:2]:
            copy.wait_recv()
        copies = []
        for n, buf in payload:
            near = buf.at[:, k, :, fst[2]]
            copies.append(push(near, near, sems_q.at[3, n, 2], semr_q.at[3, n, 2], put(here, 2, snd[2])))
        return copies

    def gather_last():
        copies = []
        for n, buf in payload:
            mine = buf.at[:, k]
            copies.append(push(mine, mine, sems_q.at[4, n, 0], semr_q.at[4, n, 0], sibling))
        return copies

    def project(n, carry):
        at = pl.ds(pl.multiple_of(n * 256, 256), 256)
        weight = win[:, at]
        bias = bias_in[:, at]
        for m in range(4):
            rows = slice(m * 256, m * 256 + 256)
            pre = dot(tok[rows, :], weight) + bias
            cdf = 0.5 * (1.0 + lax.erf(pre * 0.7071067811865476))
            hidden[rows, at] = (pre * cdf).astype(BF16)
            slope[rows, at] = cdf + pre * 0.3989422804014327 * jnp.exp(-0.5 * pre * pre)
        turn = pl.ds(pl.multiple_of(n * 128, 128), 128)
        tok_t[turn, :] = tok[:, turn].T
        return carry

    tok_in.wait()
    win_in[0].wait()
    lax.fori_loop(0, 1, project, 0)
    greeted(peers)
    first = gather_first()
    lax.fori_loop(1, 2, project, 0)
    win_in[1].wait()
    lax.fori_loop(2, 3, project, 0)
    second = gather_second()
    lax.fori_loop(3, 4, project, 0)
    win_in[2].wait()
    lax.fori_loop(4, 5, project, 0)
    for copy in second:
        copy.wait_recv()
    third = gather_third()
    sent += first + second + third

    tab_in.wait()
    own_in.wait()
    wide_q = qcol[...].astype(F32).reshape(8, 16, 512)
    left = wide_q[:, :8].reshape(64, 512).astype(BF16)
    right = wide_q[:, 8:].reshape(64, 512).astype(BF16)
    ids = jnp.concatenate([idcol[...].reshape(64, 128), jnp.zeros((64, 128), F32)], axis=0).T[:16, :64]
    dots[...] = jnp.zeros_like(dots)

    def score_rows(i, carry):
        start = pl.multiple_of(i * 128, 128)
        block = tab[pl.ds(start, 128), :]
        wide = block.astype(F32)
        scale = lax.rsqrt(jnp.sum(wide * wide, axis=1, keepdims=True) + norm_eps)
        score = (dot(block[:, :512], left, 1, 1) + dot(block[:, 512:], right, 1, 1)) * scale
        names = (lax.broadcasted_iota(jnp.int32, (128, 64), 0) + (start + c * 1024)).astype(F32)
        found = []
        for slot in range(12):
            hit = jnp.where(names == ids[slot : slot + 1, :], score, 0.0)
            found.append(jnp.sum(hit, axis=0, keepdims=True))
        found.append(jnp.zeros((4, 64), F32))
        dots[:, :64] += jnp.concatenate(found, axis=0)
        return carry

    lax.fori_loop(0, 8, score_rows, 0)
    back = [push(dots, dall.at[n], dsem.at[n], dsemr.at[n], peer) for n, peer in enumerate(column)]
    sent += back

    lax.fori_loop(5, 6, project, 0)
    win_in[3].wait()
    lax.fori_loop(6, 8, project, 0)

    wout_in.wait()
    which = lax.broadcasted_iota(jnp.int32, (8, 1024), 0)

    def normalise(i, carry):
        rows = pl.ds(pl.multiple_of(i * 256, 256), 256)
        summed = tok[rows, :].astype(F32) + dot(hidden[rows, :], wout[...]) + bias_out[...]
        centred = summed - jnp.mean(summed, axis=1, keepdims=True)
        inv = lax.rsqrt(jnp.mean(centred * centred, axis=1, keepdims=True) + norm_eps)
        value = centred * inv
        normed[rows, :] = value
        inv_std[rows, :] = jnp.broadcast_to(inv, (256, 128))
        for h in range(2):
            line = jnp.sum(value[h * 128 : h * 128 + 128], axis=0, keepdims=True)
            carry = jnp.where(which == 2 * i + h, line, carry)
        return carry

    norm_sum = lax.fori_loop(0, 2, normalise, jnp.zeros((8, 1024), F32))
    fourth = gather_fourth()
    sent += fourth
    norm_sum = lax.fori_loop(2, 4, normalise, norm_sum)

    for copy in back:
        copy.wait_recv()
    total = dots[...]
    for n in range(7):
        total += dall[n]
    turned[...] = jnp.concatenate([total, jnp.zeros((112, 128), F32)], axis=0).T
    raw = turned[pl.ds(pl.multiple_of((k * 4 + z) * 8, 8), 8), :]
    pooled = norm_sum * gain[...] + 128.0 * shift[...]
    emb_scale = lax.rsqrt(jnp.sum(pooled * pooled, axis=1, keepdims=True) + norm_eps)
    emb = pooled * emb_scale
    q_scale = lax.rsqrt(jnp.sum(query * query, axis=1, keepdims=True) + norm_eps)
    question = query * q_scale
    positive = jnp.sum(question * emb, axis=1, keepdims=True) / logit_divisor
    live = lane.astype(F32) < slot[:, 12:13]
    weights = jnp.where(live, jnp.exp(raw * q_scale / logit_divisor), 0.0)
    own = jnp.exp(positive)
    whole = own + jnp.sum(weights, axis=1, keepdims=True)
    cg[z, k, y, x] = weights / whole / logit_divisor * q_scale
    emb_slope = ((own / whole - 1.0) / logit_divisor) * question
    d_pooled = emb_scale * (emb_slope - emb * jnp.sum(emb * emb_slope, axis=1, keepdims=True))
    grad_shift = jnp.sum(d_pooled, axis=0, keepdims=True) * 128.0
    grad_gain = jnp.sum(d_pooled * norm_sum, axis=0, keepdims=True)
    lead = d_pooled * gain[...]

    def slopes(step):
        if step == 0:
            mine = cg.at[z, k, y, x]
            return [push(mine, mine, cs.at[0, 0], cr.at[0, 0], sibling)]
        dim = step - 1
        every = slice(None)
        mine = cg.at[((z, every, y, x), (every, every, y, x), (every, every, every, x))[dim]]
        copies = []
        for j in (1, 2, 3):
            peer, _ = moved(here, dim, j)
            copies.append(push(mine, mine, cs.at[step, j - 1], cr.at[step, j - 1], peer))
        return copies

    def arrived(copies):
        for copy in copies:
            copy.wait_recv()

    slope_step = slopes(0)
    sent += slope_step

    def back_norm(i, carry):
        rows = pl.ds(pl.multiple_of(i * 128, 128), 128)
        g = jnp.sum(jnp.where(which == i, lead, 0.0), axis=0, keepdims=True)
        value = normed[rows, :]
        inv = inv_std[rows, :][:, :1]
        both = jnp.mean(value * g, axis=1, keepdims=True)
        ds = inv * (g - jnp.mean(g, axis=1, keepdims=True) - value * both)
        d_sum[rows, :] = ds.astype(BF16)
        return carry + jnp.sum(ds, axis=0, keepdims=True)

    grad_bias_out = lax.fori_loop(0, 8, back_norm, jnp.zeros((1, 1024), F32))
    for copy in third[2:] + fourth:
        copy.wait_recv()
    last = gather_last()
    sent += last
    arrived(slope_step)
    slope_step = slopes(1)
    sent += slope_step

    def grad_out(zz, core):
        at = pl.ds(pl.multiple_of((zz * 2 + core) * 256, 256), 256)
        value = dot(hidden[:, at], d_sum[...], 0, 0)
        part[0, zz, core] = value.astype(BF16).reshape(4, 4, 16, 1024)

    zero = {}
    for zz in range(4):
        grad_out(zz, 1 - k)
        zero[0, zz] = push(part.at[0, zz, 1 - k], r0.at[0, zz], sem0.at[0, zz], rsem0.at[0, zz], sibling)

    def own_blocks(zz, carry):
        grad_out(zz, k)
        return carry

    lax.fori_loop(0, 4, own_blocks, 0)
    arrived(slope_step)
    slope_step = slopes(2)
    sent += slope_step

    def add_core(w, lo, hi, first, last):
        def one(i, carry):
            a, e = i // 4, lax.rem(i, 4)
            r0[w, a, e, :, :, lo:hi] = r0[w, a, e, :, :, lo:hi] + part[w, a, k, e, :, :, lo:hi]
            return carry
        lax.fori_loop(first, last, one, 0)

    def rest(p):
        return [d for d in (0, 1, 2) if d != ORDER[p][0]]

    def stage_one(w, p):
        dim = ORDER[p][0]
        peer = put(here, dim, fst[dim])
        copies = []
        for n, to in enumerate((opp[dim], fst[dim])):
            src = pick(r0.at[w], dim, to, PARTS[w][p])
            copies.append(push(src, r1[w][p].at[n], sems.at[0, w, p, n], semr.at[0, w, p, n], peer))
        return copies

    def relay_one(w, p):
        dim = ORDER[p][0]
        mine = pick(r0.at[w], dim, snd[dim], PARTS[w][p])

        def one(e, carry):
            mine[e] = mine[e] + r1[w][p][0, e]
            return carry
        lax.fori_loop(0, 4, one, 0)
        return [push(mine, r1[w][p].at[2], sems.at[0, w, p, 2], semr.at[0, w, p, 2], put(here, dim, snd[dim]))]

    def add_one(w, p):
        dim = ORDER[p][0]
        mine = pick(r0.at[w], dim, coord[dim], PARTS[w][p])

        def one(e, carry):
            value = mine[e].astype(F32) + r1[w][p][1, e].astype(F32) + r1[w][p][2, e].astype(F32)
            s1[w][p][e] = value.astype(BF16)
            return carry
        lax.fori_loop(0, 4, one, 0)

    def stage_two(w, p):
        dim = ORDER[p][1]
        copies = []
        for j in (1, 2, 3):
            peer, to = moved(here, dim, j)
            src = pick(s1[w][p], rest(p).index(dim), to)
            copies.append(push(src, r2[w][p].at[j - 1], sems.at[1, w, p, j - 1], semr.at[1, w, p, j - 1], peer))
        return copies

    def add_two(w, p):
        dim = ORDER[p][1]
        value = pick(s1[w][p], rest(p).index(dim), coord[dim])[...].astype(F32)
        for j in range(3):
            value += r2[w][p][j].astype(F32)
        s2[w][p][...] = value

    def stage_three(w, p):
        dim = ORDER[p][2]
        copies = []
        for j in (1, 2, 3):
            peer, to = moved(here, dim, j)
            copies.append(push(s2[w][p].at[to], r3[w][p].at[j - 1], sems.at[2, w, p, j - 1], semr.at[2, w, p, j - 1], peer))
        return copies

    def add_three(w, p):
        lo, hi = PARTS[w][p]
        value = s2[w][p][coord[ORDER[p][2]]] + r3[w][p][0] + r3[w][p][1] + r3[w][p][2]
        if w == 0:
            g_out[:, lo:hi] = value
        else:
            for n in range((hi - lo) // 128):
                tile = value[:, n * 128 : n * 128 + 128]
                g_in[:, 2 * lo + 256 * n : 2 * lo + 256 * n + 128] = tile[:8]
                g_in[:, 2 * lo + 256 * n + 128 : 2 * lo + 256 * n + 256] = tile[8:]

    def back_layer(n, carry):
        at = pl.ds(pl.multiple_of(n * 256, 256), 256)
        weight = wout[at, :]
        line = jnp.zeros((1, 256), F32)
        for m in range(4):
            rows = slice(m * 256, m * 256 + 256)
            value = dot(d_sum[rows, :], weight, 1, 1) * slope[rows, at]
            line += jnp.sum(value, axis=0, keepdims=True)
            d_pre[rows, :] = value.astype(BF16)
        bias_acc[:, at] = line
        to = pl.ds(pl.multiple_of(n * 128, 128), 128)
        for m in range(4):
            value = dot(tok_t[m * 256 : m * 256 + 256, :], d_pre[...])
            value = value.reshape(32, 8, 256)
            value = jnp.concatenate([value[:, :, :128], value[:, :, 128:]], axis=1).astype(BF16)
            part[1, m, :, :, :, :, to] = value.reshape(2, 4, 4, 16, 128)
        return carry

    ones, twos, threes = {}, {}, {}
    groups = (ones, twos, threes)

    def start(step, w, p):
        groups[step][w, p] = (stage_one, stage_two, stage_three)[step](w, p)

    def pass_on(w, p):
        ones[w, p][0].wait_recv()
        ones[w, p] += relay_one(w, p)

    def end(step, w, p):
        for copy in groups[step][w, p][1 if step == 0 else 0 :]:
            copy.wait_recv()
        (add_one, add_two, add_three)[step](w, p)
        if step < 2:
            start(step + 1, w, p)

    def to_sibling(n, lo, hi):
        cut = pl.ds(lo, hi - lo)
        zero[1, n] = push(
            part.at[1, :, 1 - k, :, :, :, cut], r0.at[1, :, :, :, :, cut], sem0.at[1, n], rsem0.at[1, n], sibling
        )

    for zz in range(4):
        zero[0, zz].wait_recv()
        add_core(0, 0, 1024, 4 * zz, 4 * zz + 4)
    for p in range(3):
        start(0, 0, p)
    early, late = (0, 1, 2), (3, 4, 5)
    lax.fori_loop(0, 5, back_layer, 0)
    to_sibling(0, 0, 640)
    for p in early:
        pass_on(0, p)
    arrived(slope_step)
    slope_step = slopes(3)
    sent += slope_step
    lax.fori_loop(5, 6, back_layer, 0)
    zero[1, 0].wait_recv()
    add_core(1, 0, 640, 0, 16)
    for p in early:
        start(0, 1, p)
    for p in range(3):
        end(0, 0, p)
    lax.fori_loop(6, 8, back_layer, 0)
    to_sibling(1, 640, 1024)
    for p in early:
        pass_on(1, p)

    sm[0, k] = jnp.concatenate(
        [bias_acc[:, :1024], bias_acc[:, 1024:], grad_bias_out, grad_gain, grad_shift, jnp.zeros((3, 1024), F32)], axis=0
    )
    small = [push(sm.at[0, k], sm.at[0, k], qs.at[0, 0], qr.at[0, 0], sibling)]
    sent += small

    def stage_small(step):
        dim = step - 1
        got = sm[step - 1, 0] + sm[step - 1, 1]
        if step > 1:
            got = (got + sm[step - 1, 2]) + sm[step - 1, 3]
        sm[step, coord[dim]] = got
        copies = []
        for j in (1, 2, 3):
            peer, _ = moved(here, dim, j)
            mine = sm.at[step, coord[dim]]
            copies.append(push(mine, mine, qs.at[step, j - 1], qr.at[step, j - 1], peer))
        return copies

    for p in range(3):
        end(1, 0, p)
    zero[1, 1].wait_recv()
    add_core(1, 640, 1024, 0, 16)
    for p in late:
        start(0, 1, p)
    arrived(small)
    small = stage_small(1)
    sent += small
    for p in early:
        end(0, 1, p)
    for p in late:
        pass_on(1, p)
    arrived(slope_step)
    arrived(last)

    base = c * 1024 + (y * 4 + x) * 64
    row = (lax.broadcasted_iota(jnp.int32, (256, 128), 1) + base).astype(F32)

    def collect(i, carry):
        name, value = idall[i].reshape(256, 128), cg[i].reshape(256, 128)
        weight = jnp.zeros((256, 128), F32)
        for slot in range(12):
            weight += jnp.where(name[:, slot : slot + 1] == row, value[:, slot : slot + 1], 0.0)
        high = weight.astype(BF16)
        low = (weight - high.astype(F32)).astype(BF16)
        some = qall[i].astype(F32).reshape(32, 16, 512)
        halves = []
        for h in range(2):
            half = some[:, h * 8 : h * 8 + 8].reshape(256, 512).astype(BF16)
            halves.append(dot(high, half, 0, 0) + dot(low, half, 0, 0))
        return tuple(a + b[:64] for a, b in zip(carry, halves))

    sums = lax.fori_loop(0, 4, collect, (jnp.zeros((64, 512), F32),) * 2)
    table_slope = jnp.concatenate(sums, axis=1)
    rows = tab_own[...].astype(F32)
    scale = lax.rsqrt(jnp.sum(rows * rows, axis=1, keepdims=True) + norm_eps)
    unit = rows * scale
    g_table[...] = scale * (table_slope - unit * jnp.sum(unit * table_slope, axis=1, keepdims=True))

    for p in late:
        end(0, 1, p)
    arrived(small)
    small = stage_small(2)
    sent += small
    for p in early:
        end(1, 1, p)
    for p in range(3):
        end(2, 0, p)
    for p in late:
        end(1, 1, p)
    arrived(small)
    small = stage_small(3)
    sent += small
    for p in early:
        end(2, 1, p)
    arrived(small)
    got = ((sm[3, 0] + sm[3, 1]) + sm[3, 2]) + sm[3, 3]
    g_bias_in[:, :1024] = got[0:1]
    g_bias_in[:, 1024:] = got[1:2]
    g_bias_out[...] = got[2:3]
    g_gain[...] = got[3:4]
    g_shift[...] = got[4:5]
    for p in late:
        end(2, 1, p)
    for group in groups:
        for copies in group.values():
            sent += copies
    for copy in sent + list(zero.values()):
        copy.wait_send()


def hand_over_kernel(*refs):
    for src, dst in zip(refs[:7], refs[7:]):
        dst[...] = src[...]


def hand_over(*results):
    vmem = pl.BlockSpec(memory_space=pltpu.VMEM)
    return pl.pallas_call(
        hand_over_kernel,
        out_shape=tuple(jax.ShapeDtypeStruct(value.shape, value.dtype) for value in results),
        in_specs=[vmem] * 7,
        out_specs=(vmem,) * 7,
    )(*results)


def step(*operands):
    vmem, hbm = pl.BlockSpec(memory_space=pltpu.VMEM), pl.BlockSpec(memory_space=pl.ANY)

    def scratch(shape, kind):
        return tuple(tuple(pltpu.VMEM(shape + (16, hi - lo), kind) for lo, hi in row) for row in PARTS)

    dma = pltpu.SemaphoreType.DMA
    out = jax.ShapeDtypeStruct
    return pl.pallas_call(
        step_kernel,
        out_shape=(
            out((8, 2048), F32),
            out((1, 2048), F32),
            out((16, 1024), F32),
            out((1, 1024), F32),
            out((1, 1024), F32),
            out((1, 1024), F32),
            out((64, 1024), F32),
        ),
        in_specs=[hbm] * 4 + [vmem] * 6,
        out_specs=(vmem,) * 7,
        scratch_shapes=[
            pltpu.VMEM((1024, 1024), BF16),
            pltpu.VMEM((1024, 2048), BF16),
            pltpu.VMEM((2048, 1024), BF16),
            pltpu.VMEM((1024, 1024), BF16),
            pltpu.VMEM((64, 1024), BF16),
            pltpu.VMEM((1024, 1024), BF16),
            pltpu.VMEM((1024, 2048), BF16),
            pltpu.VMEM((1024, 2048), F32),
            pltpu.VMEM((1024, 1024), F32),
            pltpu.VMEM((1024, 128), F32),
            pltpu.VMEM((1024, 1024), BF16),
            pltpu.VMEM((1024, 256), BF16),
            pltpu.VMEM((1, 2048), F32),
            pltpu.VMEM((4, 2, 4, 4, 16, 512), BF16),
            pltpu.VMEM((4, 2, 4, 4, 8, 128), F32),
            pltpu.VMEM((2, 4, 16, 512), BF16),
            pltpu.VMEM((2, 4, 8, 128), F32),
            pltpu.VMEM((16, 128), F32),
            pltpu.VMEM((7, 16, 128), F32),
            pltpu.VMEM((128, 128), F32),
            pltpu.VMEM((2, 4, 2, 4, 4, 16, 1024), BF16),
            pltpu.VMEM((2, 4, 4, 4, 16, 1024), BF16),
            scratch((3, 4, 4), BF16),
            scratch((4, 4), BF16),
            scratch((3, 4), BF16),
            scratch((4,), F32),
            scratch((3,), F32),
            pltpu.VMEM((4, 4, 8, 1024), F32),
            pltpu.VMEM((4, 2, 4, 4, 8, 128), F32),
            dma((8,)),
            dma((5, 2, 3)),
            dma((5, 2, 3)),
            dma((7,)),
            dma((7,)),
            dma((2, 4)),
            dma((2, 4)),
            dma((3, 2, 6, 3)),
            dma((3, 2, 6, 3)),
            dma((4, 3)),
            dma((4, 3)),
            dma((4, 3)),
            dma((4, 3)),
        ],
        compiler_params=pltpu.CompilerParams(
            collective_id=0, has_side_effects=True, vmem_limit_bytes=VMEM_BYTES
        ),
    )(*operands)


def body(
    tokens,
    weight_in,
    bias_in,
    weight_out,
    bias_out,
    norm_gain,
    norm_shift,
    queries,
    corpus_table,
    neg_owner,
    neg_row,
    neg_count,
):
    count_q, seq, width = tokens.shape
    slots = neg_row.shape[1]
    ids = (neg_owner.reshape(count_q, slots) * 1024 + neg_row).astype(F32)
    counts = neg_count.astype(F32)[:, None]
    slot = jnp.concatenate([ids, counts, jnp.full((count_q, 128 - slots - 1), -1.0, F32)], axis=1)
    results = step(
        tokens.reshape(count_q * seq, width),
        weight_in,
        weight_out,
        corpus_table,
        bias_in[None],
        bias_out[None],
        norm_gain[None],
        norm_shift[None],
        queries,
        slot,
    )
    grad_in, g_bias_in, grad_out, g_bias_out, g_gain, g_shift, grad_table = hand_over(*results)
    return (grad_in, g_bias_in[0], grad_out, g_bias_out[0], g_gain[0], g_shift[0], grad_table)


def solution(mesh):
    return jax.shard_map(
        body,
        mesh=mesh,
        in_specs=(
            P(("corpus", "batch"), None, None),
            P(),
            P(),
            P(),
            P(),
            P(),
            P(),
            P(("corpus", "batch"), None),
            P("corpus", None),
            P(("corpus", "batch"), None, None),
            P(("corpus", "batch"), None),
            P(("corpus", "batch")),
        ),
        out_specs=(
            P(("corpus", "batch"), None),
            P(),
            P(("corpus", "batch"), None),
            P(),
            P(),
            P(),
            P(("corpus", "batch"), None),
        ),
        check_vma=False,
    )
```

```python
import functools

import jax
import jax.numpy as jnp
from jax import lax
from jax.experimental import pallas as pl
from jax.experimental.pallas import tpu as pltpu
from jax.sharding import PartitionSpec as P

logit_divisor = 0.05
norm_eps = 1e-06
MESH = pl.DeviceIdType.MESH
F32, BF16 = jnp.float32, jnp.bfloat16
VMEM_BYTES = 60 * 1024 * 1024


def place():
    c, b = lax.axis_index("corpus"), lax.axis_index("batch")
    return c // 2, c % 2, b // 4, b % 4


def device(z, k, y, x):
    return (z * 2 + k, y * 4 + x)


def moved(here, dim, offset):
    z, k, y, x = here
    at = [z, y, x]
    at[dim] = lax.rem(at[dim] + offset, 4)
    return device(at[0], k, at[1], at[2]), at[dim]


def put(here, dim, to):
    z, k, y, x = here
    at = [z, y, x]
    at[dim] = to
    return device(at[0], k, at[1], at[2])


def greet(peers):
    barrier = pltpu.get_barrier_semaphore()
    for peer in peers:
        pl.semaphore_signal(barrier, inc=1, device_id=peer, device_id_type=MESH)


def greeted(peers):
    pl.semaphore_wait(pltpu.get_barrier_semaphore(), len(peers))


def push(src, dst, send, recv, peer):
    copy = pltpu.make_async_remote_copy(
        src_ref=src, dst_ref=dst, send_sem=send, recv_sem=recv, device_id=peer, device_id_type=MESH
    )
    copy.start()
    return copy


PARTS = (
    ((0, 384), (384, 768), (768, 1024)),
    ((0, 256), (256, 512), (512, 640), (640, 768), (768, 896), (896, 1024)),
)
ORDER = ((0, 1, 2), (1, 2, 0), (2, 0, 1)) * 2


def pick(ref, axis, index, columns=None):
    at = [slice(None)] * (len(ref.shape) - 2)
    at[axis] = index
    return ref.at[tuple(at) + (slice(None), slice(None) if columns is None else pl.ds(columns[0], columns[1] - columns[0]))]


def dot(a, b, ca=1, cb=0):
    return lax.dot_general(a, b, (((ca,), (cb,)), ((), ())), preferred_element_type=F32)


def step_kernel(
    tok_hbm, win_hbm, wout_hbm, tab_hbm, bias_in, bias_out, gain, shift, queries, slot,
    g_in, g_bias_in, g_out, g_bias_out, g_gain, g_shift, g_table,
    tok, win, wout, tab, tab_own, tok_t, hidden, slope, normed, inv_std, d_sum, d_pre, bias_acc,
    qall, idall, qcol, idcol, dots, dall, turned,
    part, r0, r1, s1, r2, s2, r3, sm, cg,
    load, sems_q, semr_q, dsem, dsemr, sem0, rsem0, sems, semr, qs, qr, cs, cr,
):
    here = place()
    z, k, y, x = here
    coord = (z, y, x)
    c = z * 2 + k
    sibling = device(z, 1 - k, y, x)
    fst = [(1 - k) * (i + 1 - 2 * lax.rem(i, 2)) + k * (3 - i) for i in coord]
    snd = [k * (i + 1 - 2 * lax.rem(i, 2)) + (1 - k) * (3 - i) for i in coord]
    opp = [lax.rem(i + 2, 4) for i in coord]
    sent = []

    def local(src, dst, n):
        copy = pltpu.make_async_copy(src, dst, load.at[n])
        copy.start()
        return copy

    column = []
    for j in range(4):
        for e in range(2):
            if j or e:
                column.append(device(lax.rem(z + j, 4), lax.rem(k + e, 2), y, x))
    peers = column + [moved(here, dim, j)[0] for dim in (1, 2) for j in (1, 2, 3)]
    greet(peers)
    tok_in = local(tok_hbm, tok, 0)
    win_in = [local(win_hbm.at[:, pl.ds(512 * n, 512)], win.at[:, pl.ds(512 * n, 512)], 1 + n) for n in range(4)]
    tab_in = local(tab_hbm, tab, 5)
    wout_in = local(wout_hbm, wout, 6)
    own_in = local(tab_hbm.at[pl.ds(pl.multiple_of((y * 4 + x) * 64, 64), 64), :], tab_own, 7)

    query = queries[...].astype(F32)
    qall[z, k, y, x] = jnp.concatenate([query[:, :512], query[:, 512:]], axis=0).astype(BF16)
    lane = lax.broadcasted_iota(jnp.int32, (8, 128), 1)
    idall[z, k, y, x] = jnp.where(lane < 12, slot[...], -1.0)
    payload = ((0, qall), (1, idall))

    def gather_first():
        copies = []
        for j in (1, 2, 3):
            peer, _ = moved(here, 0, j)
            for n, buf in payload:
                mine = buf.at[z, k, y, x]
                copies.append(push(mine, mine, sems_q.at[0, n, j - 1], semr_q.at[0, n, j - 1], peer))
        return copies

    def gather_second():
        for copy in first:
            copy.wait_recv()
        copies = []
        for n, buf, dst in ((0, qall, qcol), (1, idall, idcol)):
            copies.append(push(buf.at[:, k, y, x], dst.at[k], sems_q.at[1, n, 0], semr_q.at[1, n, 0], sibling))
        for j in (1, 2, 3):
            peer, _ = moved(here, 1, j)
            for n, buf in payload:
                mine = buf.at[:, k, y, x]
                copies.append(push(mine, mine, sems_q.at[2, n, j - 1], semr_q.at[2, n, j - 1], peer))
        qcol[k] = qall[:, k, y, x]
        idcol[k] = idall[:, k, y, x]
        return copies

    def gather_third():
        copies = []
        for m, to in enumerate((fst[2], snd[2])):
            for n, buf in payload:
                mine = buf.at[:, k, :, x]
                copies.append(push(mine, mine, sems_q.at[3, n, m], semr_q.at[3, n, m], put(here, 2, to)))
        return copies

    def gather_fourth():
        for copy in third[:2]:
            copy.wait_recv()
        copies = []
        for n, buf in payload:
            near = buf.at[:, k, :, fst[2]]
            copies.append(push(near, near, sems_q.at[3, n, 2], semr_q.at[3, n, 2], put(here, 2, snd[2])))
        return copies

    def gather_last():
        copies = []
        for n, buf in payload:
            mine = buf.at[:, k]
            copies.append(push(mine, mine, sems_q.at[4, n, 0], semr_q.at[4, n, 0], sibling))
        return copies

    def project(n, carry):
        at = pl.ds(pl.multiple_of(n * 256, 256), 256)
        weight = win[:, at]
        bias = bias_in[:, at]
        for m in range(4):
            rows = slice(m * 256, m * 256 + 256)
            pre = dot(tok[rows, :], weight) + bias
            cdf = 0.5 * (1.0 + lax.erf(pre * 0.7071067811865476))
            hidden[rows, at] = (pre * cdf).astype(BF16)
            slope[rows, at] = cdf + pre * 0.3989422804014327 * jnp.exp(-0.5 * pre * pre)
        turn = pl.ds(pl.multiple_of(n * 128, 128), 128)
        tok_t[turn, :] = tok[:, turn].T
        return carry

    tok_in.wait()
    win_in[0].wait()
    lax.fori_loop(0, 1, project, 0)
    greeted(peers)
    first = gather_first()
    lax.fori_loop(1, 2, project, 0)
    win_in[1].wait()
    lax.fori_loop(2, 4, project, 0)
    second = gather_second()
    win_in[2].wait()
    lax.fori_loop(4, 6, project, 0)
    win_in[3].wait()
    lax.fori_loop(6, 8, project, 0)
    for copy in second:
        copy.wait_recv()
    third = gather_third()
    sent += first + second + third

    tab_in.wait()
    own_in.wait()
    wide_q = qcol[...].astype(F32).reshape(8, 16, 512)
    left = wide_q[:, :8].reshape(64, 512).astype(BF16)
    right = wide_q[:, 8:].reshape(64, 512).astype(BF16)
    ids = jnp.concatenate([idcol[...].reshape(64, 128), jnp.zeros((64, 128), F32)], axis=0).T[:16, :64]
    dots[...] = jnp.zeros_like(dots)

    def score_rows(i, carry):
        start = pl.multiple_of(i * 128, 128)
        block = tab[pl.ds(start, 128), :]
        wide = block.astype(F32)
        scale = lax.rsqrt(jnp.sum(wide * wide, axis=1, keepdims=True) + norm_eps)
        score = (dot(block[:, :512], left, 1, 1) + dot(block[:, 512:], right, 1, 1)) * scale
        names = (lax.broadcasted_iota(jnp.int32, (128, 64), 0) + (start + c * 1024)).astype(F32)
        found = []
        for slot in range(12):
            hit = jnp.where(names == ids[slot : slot + 1, :], score, 0.0)
            found.append(jnp.sum(hit, axis=0, keepdims=True))
        found.append(jnp.zeros((4, 64), F32))
        dots[:, :64] += jnp.concatenate(found, axis=0)
        return carry

    lax.fori_loop(0, 8, score_rows, 0)
    back = [push(dots, dall.at[n], dsem.at[n], dsemr.at[n], peer) for n, peer in enumerate(column)]
    sent += back


    wout_in.wait()
    which = lax.broadcasted_iota(jnp.int32, (8, 1024), 0)

    def normalise(i, carry):
        rows = pl.ds(pl.multiple_of(i * 256, 256), 256)
        summed = tok[rows, :].astype(F32) + dot(hidden[rows, :], wout[...]) + bias_out[...]
        centred = summed - jnp.mean(summed, axis=1, keepdims=True)
        inv = lax.rsqrt(jnp.mean(centred * centred, axis=1, keepdims=True) + norm_eps)
        value = centred * inv
        normed[rows, :] = value
        inv_std[rows, :] = jnp.broadcast_to(inv, (256, 128))
        for h in range(2):
            line = jnp.sum(value[h * 128 : h * 128 + 128], axis=0, keepdims=True)
            carry = jnp.where(which == 2 * i + h, line, carry)
        return carry

    norm_sum = lax.fori_loop(0, 2, normalise, jnp.zeros((8, 1024), F32))
    fourth = gather_fourth()
    sent += fourth
    norm_sum = lax.fori_loop(2, 4, normalise, norm_sum)

    for copy in back:
        copy.wait_recv()
    total = dots[...]
    for n in range(7):
        total += dall[n]
    turned[...] = jnp.concatenate([total, jnp.zeros((112, 128), F32)], axis=0).T
    raw = turned[pl.ds(pl.multiple_of((k * 4 + z) * 8, 8), 8), :]
    pooled = norm_sum * gain[...] + 128.0 * shift[...]
    emb_scale = lax.rsqrt(jnp.sum(pooled * pooled, axis=1, keepdims=True) + norm_eps)
    emb = pooled * emb_scale
    q_scale = lax.rsqrt(jnp.sum(query * query, axis=1, keepdims=True) + norm_eps)
    question = query * q_scale
    positive = jnp.sum(question * emb, axis=1, keepdims=True) / logit_divisor
    live = lane.astype(F32) < slot[:, 12:13]
    weights = jnp.where(live, jnp.exp(raw * q_scale / logit_divisor), 0.0)
    own = jnp.exp(positive)
    whole = own + jnp.sum(weights, axis=1, keepdims=True)
    cg[z, k, y, x] = weights / whole / logit_divisor * q_scale
    emb_slope = ((own / whole - 1.0) / logit_divisor) * question
    d_pooled = emb_scale * (emb_slope - emb * jnp.sum(emb * emb_slope, axis=1, keepdims=True))
    grad_shift = jnp.sum(d_pooled, axis=0, keepdims=True) * 128.0
    grad_gain = jnp.sum(d_pooled * norm_sum, axis=0, keepdims=True)
    lead = d_pooled * gain[...]

    def slopes(step):
        if step == 0:
            mine = cg.at[z, k, y, x]
            return [push(mine, mine, cs.at[0, 0], cr.at[0, 0], sibling)]
        dim = step - 1
        every = slice(None)
        mine = cg.at[((z, every, y, x), (every, every, y, x), (every, every, every, x))[dim]]
        copies = []
        for j in (1, 2, 3):
            peer, _ = moved(here, dim, j)
            copies.append(push(mine, mine, cs.at[step, j - 1], cr.at[step, j - 1], peer))
        return copies

    def arrived(copies):
        for copy in copies:
            copy.wait_recv()

    slope_step = slopes(0)
    sent += slope_step

    def back_norm(i, carry):
        rows = pl.ds(pl.multiple_of(i * 128, 128), 128)
        g = jnp.sum(jnp.where(which == i, lead, 0.0), axis=0, keepdims=True)
        value = normed[rows, :]
        inv = inv_std[rows, :][:, :1]
        both = jnp.mean(value * g, axis=1, keepdims=True)
        ds = inv * (g - jnp.mean(g, axis=1, keepdims=True) - value * both)
        d_sum[rows, :] = ds.astype(BF16)
        return carry + jnp.sum(ds, axis=0, keepdims=True)

    grad_bias_out = lax.fori_loop(0, 8, back_norm, jnp.zeros((1, 1024), F32))
    for copy in third[2:] + fourth:
        copy.wait_recv()
    last = gather_last()
    sent += last
    arrived(slope_step)
    slope_step = slopes(1)
    sent += slope_step

    def grad_out(zz, core):
        at = pl.ds(pl.multiple_of((zz * 2 + core) * 256, 256), 256)
        value = dot(hidden[:, at], d_sum[...], 0, 0)
        part[0, zz, core] = value.astype(BF16).reshape(4, 4, 16, 1024)

    zero = {}
    for zz in range(4):
        grad_out(zz, 1 - k)
        zero[0, zz] = push(part.at[0, zz, 1 - k], r0.at[0, zz], sem0.at[0, zz], rsem0.at[0, zz], sibling)

    arrived(slope_step)
    slope_step = slopes(2)
    sent += slope_step

    def own_blocks(zz, carry):
        grad_out(zz, k)
        return carry

    lax.fori_loop(0, 4, own_blocks, 0)
    arrived(slope_step)
    slope_step = slopes(3)
    sent += slope_step

    def add_core(w, lo, hi, first, last):
        def one(i, carry):
            a, e = i // 4, lax.rem(i, 4)
            r0[w, a, e, :, :, lo:hi] = r0[w, a, e, :, :, lo:hi] + part[w, a, k, e, :, :, lo:hi]
            return carry
        lax.fori_loop(first, last, one, 0)

    def rest(p):
        return [d for d in (0, 1, 2) if d != ORDER[p][0]]

    def stage_one(w, p):
        dim = ORDER[p][0]
        peer = put(here, dim, fst[dim])
        copies = []
        for n, to in enumerate((opp[dim], fst[dim])):
            src = pick(r0.at[w], dim, to, PARTS[w][p])
            copies.append(push(src, r1[w][p].at[n], sems.at[0, w, p, n], semr.at[0, w, p, n], peer))
        return copies

    def relay_one(w, p):
        dim = ORDER[p][0]
        mine = pick(r0.at[w], dim, snd[dim], PARTS[w][p])

        def one(e, carry):
            mine[e] = mine[e] + r1[w][p][0, e]
            return carry
        lax.fori_loop(0, 4, one, 0)
        return [push(mine, r1[w][p].at[2], sems.at[0, w, p, 2], semr.at[0, w, p, 2], put(here, dim, snd[dim]))]

    def add_one(w, p):
        dim = ORDER[p][0]
        mine = pick(r0.at[w], dim, coord[dim], PARTS[w][p])

        def one(e, carry):
            value = mine[e].astype(F32) + r1[w][p][1, e].astype(F32) + r1[w][p][2, e].astype(F32)
            s1[w][p][e] = value.astype(BF16)
            return carry
        lax.fori_loop(0, 4, one, 0)

    def stage_two(w, p):
        dim = ORDER[p][1]
        copies = []
        for j in (1, 2, 3):
            peer, to = moved(here, dim, j)
            src = pick(s1[w][p], rest(p).index(dim), to)
            copies.append(push(src, r2[w][p].at[j - 1], sems.at[1, w, p, j - 1], semr.at[1, w, p, j - 1], peer))
        return copies

    def add_two(w, p):
        dim = ORDER[p][1]
        value = pick(s1[w][p], rest(p).index(dim), coord[dim])[...].astype(F32)
        for j in range(3):
            value += r2[w][p][j].astype(F32)
        s2[w][p][...] = value

    def stage_three(w, p):
        dim = ORDER[p][2]
        copies = []
        for j in (1, 2, 3):
            peer, to = moved(here, dim, j)
            copies.append(push(s2[w][p].at[to], r3[w][p].at[j - 1], sems.at[2, w, p, j - 1], semr.at[2, w, p, j - 1], peer))
        return copies

    def add_three(w, p):
        lo, hi = PARTS[w][p]
        value = s2[w][p][coord[ORDER[p][2]]] + r3[w][p][0] + r3[w][p][1] + r3[w][p][2]
        if w == 0:
            g_out[:, lo:hi] = value
        else:
            for n in range((hi - lo) // 128):
                tile = value[:, n * 128 : n * 128 + 128]
                g_in[:, 2 * lo + 256 * n : 2 * lo + 256 * n + 128] = tile[:8]
                g_in[:, 2 * lo + 256 * n + 128 : 2 * lo + 256 * n + 256] = tile[8:]

    def back_layer(n, carry):
        at = pl.ds(pl.multiple_of(n * 256, 256), 256)
        weight = wout[at, :]
        line = jnp.zeros((1, 256), F32)
        for m in range(4):
            rows = slice(m * 256, m * 256 + 256)
            value = dot(d_sum[rows, :], weight, 1, 1) * slope[rows, at]
            line += jnp.sum(value, axis=0, keepdims=True)
            d_pre[rows, :] = value.astype(BF16)
        bias_acc[:, at] = line
        to = pl.ds(pl.multiple_of(n * 128, 128), 128)
        for m in range(4):
            value = dot(tok_t[m * 256 : m * 256 + 256, :], d_pre[...])
            value = value.reshape(32, 8, 256)
            value = jnp.concatenate([value[:, :, :128], value[:, :, 128:]], axis=1).astype(BF16)
            part[1, m, :, :, :, :, to] = value.reshape(2, 4, 4, 16, 128)
        return carry

    ones, twos, threes = {}, {}, {}
    groups = (ones, twos, threes)

    def start(step, w, p):
        groups[step][w, p] = (stage_one, stage_two, stage_three)[step](w, p)

    def pass_on(w, p):
        ones[w, p][0].wait_recv()
        ones[w, p] += relay_one(w, p)

    def end(step, w, p):
        for copy in groups[step][w, p][1 if step == 0 else 0 :]:
            copy.wait_recv()
        (add_one, add_two, add_three)[step](w, p)
        if step < 2:
            start(step + 1, w, p)

    def to_sibling(n, lo, hi):
        cut = pl.ds(lo, hi - lo)
        zero[1, n] = push(
            part.at[1, :, 1 - k, :, :, :, cut], r0.at[1, :, :, :, :, cut], sem0.at[1, n], rsem0.at[1, n], sibling
        )

    for zz in range(4):
        zero[0, zz].wait_recv()
        add_core(0, 0, 1024, 4 * zz, 4 * zz + 4)
    for p in range(3):
        start(0, 0, p)
    early, late = (0, 1, 2), (3, 4, 5)
    lax.fori_loop(0, 5, back_layer, 0)
    to_sibling(0, 0, 640)
    for p in range(3):
        pass_on(0, p)
    lax.fori_loop(5, 6, back_layer, 0)
    for p in range(3):
        end(0, 0, p)
    lax.fori_loop(6, 7, back_layer, 0)
    zero[1, 0].wait_recv()
    add_core(1, 0, 640, 0, 16)
    for p in early:
        start(0, 1, p)
    lax.fori_loop(7, 8, back_layer, 0)
    to_sibling(1, 640, 1024)
    sm[0, k] = jnp.concatenate(
        [bias_acc[:, :1024], bias_acc[:, 1024:], grad_bias_out, grad_gain, grad_shift, jnp.zeros((3, 1024), F32)], axis=0
    )
    small = [push(sm.at[0, k], sm.at[0, k], qs.at[0, 0], qr.at[0, 0], sibling)]
    sent += small

    def stage_small(step):
        dim = step - 1
        got = sm[step - 1, 0] + sm[step - 1, 1]
        if step > 1:
            got = (got + sm[step - 1, 2]) + sm[step - 1, 3]
        sm[step, coord[dim]] = got
        copies = []
        for j in (1, 2, 3):
            peer, _ = moved(here, dim, j)
            mine = sm.at[step, coord[dim]]
            copies.append(push(mine, mine, qs.at[step, j - 1], qr.at[step, j - 1], peer))
        return copies

    arrived(last)
    arrived(slope_step)
    base = c * 1024 + (y * 4 + x) * 64
    row = (lax.broadcasted_iota(jnp.int32, (256, 128), 1) + base).astype(F32)

    def collect(i):
        name, value = idall[i].reshape(256, 128), cg[i].reshape(256, 128)
        weight = jnp.zeros((256, 128), F32)
        for slot in range(12):
            weight += jnp.where(name[:, slot : slot + 1] == row, value[:, slot : slot + 1], 0.0)
        high = weight.astype(BF16)
        low = (weight - high.astype(F32)).astype(BF16)
        some = qall[i].astype(F32).reshape(32, 16, 512)
        for h in range(2):
            half = some[:, h * 8 : h * 8 + 8].reshape(256, 512).astype(BF16)
            found = (dot(high, half, 0, 0) + dot(low, half, 0, 0))[:64]
            at = slice(h * 512, h * 512 + 512)
            g_table[:, at] = found if i == 0 else g_table[:, at] + found

    collect(0)
    for p in early:
        pass_on(1, p)
    for p in range(3):
        end(1, 0, p)
    arrived(small)
    small = stage_small(1)
    sent += small
    zero[1, 1].wait_recv()
    add_core(1, 640, 1024, 0, 16)
    for p in late:
        start(0, 1, p)
    collect(1)
    for p in early:
        end(0, 1, p)
    for p in late:
        pass_on(1, p)
    arrived(small)
    small = stage_small(2)
    sent += small
    collect(2)
    for p in range(3):
        end(2, 0, p)
    for p in late:
        end(0, 1, p)
    for p in early:
        end(1, 1, p)
    arrived(small)
    small = stage_small(3)
    sent += small
    collect(3)
    for p in late:
        end(1, 1, p)
    table_slope = g_table[...]
    rows = tab_own[...].astype(F32)
    scale = lax.rsqrt(jnp.sum(rows * rows, axis=1, keepdims=True) + norm_eps)
    unit = rows * scale
    g_table[...] = scale * (table_slope - unit * jnp.sum(unit * table_slope, axis=1, keepdims=True))
    for p in early:
        end(2, 1, p)
    arrived(small)
    got = ((sm[3, 0] + sm[3, 1]) + sm[3, 2]) + sm[3, 3]
    g_bias_in[:, :1024] = got[0:1]
    g_bias_in[:, 1024:] = got[1:2]
    g_bias_out[...] = got[2:3]
    g_gain[...] = got[3:4]
    g_shift[...] = got[4:5]
    for p in late:
        end(2, 1, p)
    for group in groups:
        for copies in group.values():
            sent += copies
    for copy in sent + list(zero.values()):
        copy.wait_send()


def hand_over_kernel(*refs):
    for src, dst in zip(refs[:7], refs[7:]):
        dst[...] = src[...]


def hand_over(*results):
    vmem = pl.BlockSpec(memory_space=pltpu.VMEM)
    return pl.pallas_call(
        hand_over_kernel,
        out_shape=tuple(jax.ShapeDtypeStruct(value.shape, value.dtype) for value in results),
        in_specs=[vmem] * 7,
        out_specs=(vmem,) * 7,
    )(*results)


def step(*operands):
    vmem, hbm = pl.BlockSpec(memory_space=pltpu.VMEM), pl.BlockSpec(memory_space=pl.ANY)

    def scratch(shape, kind):
        return tuple(tuple(pltpu.VMEM(shape + (16, hi - lo), kind) for lo, hi in row) for row in PARTS)

    dma = pltpu.SemaphoreType.DMA
    out = jax.ShapeDtypeStruct
    return pl.pallas_call(
        step_kernel,
        out_shape=(
            out((8, 2048), F32),
            out((1, 2048), F32),
            out((16, 1024), F32),
            out((1, 1024), F32),
            out((1, 1024), F32),
            out((1, 1024), F32),
            out((64, 1024), F32),
        ),
        in_specs=[hbm] * 4 + [vmem] * 6,
        out_specs=(vmem,) * 7,
        scratch_shapes=[
            pltpu.VMEM((1024, 1024), BF16),
            pltpu.VMEM((1024, 2048), BF16),
            pltpu.VMEM((2048, 1024), BF16),
            pltpu.VMEM((1024, 1024), BF16),
            pltpu.VMEM((64, 1024), BF16),
            pltpu.VMEM((1024, 1024), BF16),
            pltpu.VMEM((1024, 2048), BF16),
            pltpu.VMEM((1024, 2048), F32),
            pltpu.VMEM((1024, 1024), F32),
            pltpu.VMEM((1024, 128), F32),
            pltpu.VMEM((1024, 1024), BF16),
            pltpu.VMEM((1024, 256), BF16),
            pltpu.VMEM((1, 2048), F32),
            pltpu.VMEM((4, 2, 4, 4, 16, 512), BF16),
            pltpu.VMEM((4, 2, 4, 4, 8, 128), F32),
            pltpu.VMEM((2, 4, 16, 512), BF16),
            pltpu.VMEM((2, 4, 8, 128), F32),
            pltpu.VMEM((16, 128), F32),
            pltpu.VMEM((7, 16, 128), F32),
            pltpu.VMEM((128, 128), F32),
            pltpu.VMEM((2, 4, 2, 4, 4, 16, 1024), BF16),
            pltpu.VMEM((2, 4, 4, 4, 16, 1024), BF16),
            scratch((3, 4, 4), BF16),
            scratch((4, 4), BF16),
            scratch((3, 4), BF16),
            scratch((4,), F32),
            scratch((3,), F32),
            pltpu.VMEM((4, 4, 8, 1024), F32),
            pltpu.VMEM((4, 2, 4, 4, 8, 128), F32),
            dma((8,)),
            dma((5, 2, 3)),
            dma((5, 2, 3)),
            dma((7,)),
            dma((7,)),
            dma((2, 4)),
            dma((2, 4)),
            dma((3, 2, 6, 3)),
            dma((3, 2, 6, 3)),
            dma((4, 3)),
            dma((4, 3)),
            dma((4, 3)),
            dma((4, 3)),
        ],
        compiler_params=pltpu.CompilerParams(
            collective_id=0, has_side_effects=True, vmem_limit_bytes=VMEM_BYTES
        ),
    )(*operands)


def body(
    tokens,
    weight_in,
    bias_in,
    weight_out,
    bias_out,
    norm_gain,
    norm_shift,
    queries,
    corpus_table,
    neg_owner,
    neg_row,
    neg_count,
):
    count_q, seq, width = tokens.shape
    slots = neg_row.shape[1]
    ids = (neg_owner.reshape(count_q, slots) * 1024 + neg_row).astype(F32)
    counts = neg_count.astype(F32)[:, None]
    slot = jnp.concatenate([ids, counts, jnp.full((count_q, 128 - slots - 1), -1.0, F32)], axis=1)
    results = step(
        tokens.reshape(count_q * seq, width),
        weight_in,
        weight_out,
        corpus_table,
        bias_in[None],
        bias_out[None],
        norm_gain[None],
        norm_shift[None],
        queries,
        slot,
    )
    grad_in, g_bias_in, grad_out, g_bias_out, g_gain, g_shift, grad_table = hand_over(*results)
    return (grad_in, g_bias_in[0], grad_out, g_bias_out[0], g_gain[0], g_shift[0], grad_table)


def solution(mesh):
    return jax.shard_map(
        body,
        mesh=mesh,
        in_specs=(
            P(("corpus", "batch"), None, None),
            P(),
            P(),
            P(),
            P(),
            P(),
            P(),
            P(("corpus", "batch"), None),
            P("corpus", None),
            P(("corpus", "batch"), None, None),
            P(("corpus", "batch"), None),
            P(("corpus", "batch")),
        ),
        out_specs=(
            P(("corpus", "batch"), None),
            P(),
            P(("corpus", "batch"), None),
            P(),
            P(),
            P(),
            P(("corpus", "batch"), None),
        ),
        check_vma=False,
    )
```

```python
import functools

import jax
import jax.numpy as jnp
from jax import lax
from jax.experimental import pallas as pl
from jax.experimental.pallas import tpu as pltpu
from jax.sharding import PartitionSpec as P

logit_divisor = 0.05
norm_eps = 1e-06
MESH = pl.DeviceIdType.MESH
F32, BF16 = jnp.float32, jnp.bfloat16
VMEM_BYTES = 60 * 1024 * 1024


def place():
    c, b = lax.axis_index("corpus"), lax.axis_index("batch")
    return c // 2, c % 2, b // 4, b % 4


def device(z, k, y, x):
    return (z * 2 + k, y * 4 + x)


def moved(here, dim, offset):
    z, k, y, x = here
    at = [z, y, x]
    at[dim] = lax.rem(at[dim] + offset, 4)
    return device(at[0], k, at[1], at[2]), at[dim]


def put(here, dim, to):
    z, k, y, x = here
    at = [z, y, x]
    at[dim] = to
    return device(at[0], k, at[1], at[2])


def greet(peers):
    barrier = pltpu.get_barrier_semaphore()
    for peer in peers:
        pl.semaphore_signal(barrier, inc=1, device_id=peer, device_id_type=MESH)


def greeted(peers):
    pl.semaphore_wait(pltpu.get_barrier_semaphore(), len(peers))


def push(src, dst, send, recv, peer):
    copy = pltpu.make_async_remote_copy(
        src_ref=src, dst_ref=dst, send_sem=send, recv_sem=recv, device_id=peer, device_id_type=MESH
    )
    copy.start()
    return copy


PARTS = (
    ((0, 384), (384, 768), (768, 1024)),
    ((0, 256), (256, 512), (512, 640), (640, 768), (768, 896), (896, 1024)),
)
ORDER = ((0, 1, 2), (1, 2, 0), (2, 0, 1)) * 2
JOINED = (((0, 0), (1, 0), (2, 0)), ((0, 384), (1, 384), (2, 256), (3, 0), (4, 0), (5, 0)))
WIDTHS = (640, 640, 384, 128, 128, 128)


def pick(ref, axis, index, columns=None):
    at = [slice(None)] * (len(ref.shape) - 2)
    at[axis] = index
    return ref.at[tuple(at) + (slice(None), slice(None) if columns is None else pl.ds(columns[0], columns[1] - columns[0]))]


def dot(a, b, ca=1, cb=0):
    return lax.dot_general(a, b, (((ca,), (cb,)), ((), ())), preferred_element_type=F32)


def step_kernel(
    tok_hbm, win_hbm, wout_hbm, tab_hbm, bias_in, bias_out, gain, shift, queries, slot,
    g_in, g_bias_in, g_out, g_bias_out, g_gain, g_shift, g_table,
    tok, win, wout, tab, tab_own, tok_t, hidden, slope, normed, inv_std, d_sum, d_pre, bias_acc,
    qall, qcol, dots, dall, turned,
    part, r0, r1, s1, r2, s2, r3, sm, cg, cm,
    load, sems_q, semr_q, dsem, dsemr, sem0, rsem0, sems, semr, qs, qr, cs, cr,
):
    here = place()
    z, k, y, x = here
    coord = (z, y, x)
    c = z * 2 + k
    sibling = device(z, 1 - k, y, x)
    fst = [(1 - k) * (i + 1 - 2 * lax.rem(i, 2)) + k * (3 - i) for i in coord]
    snd = [k * (i + 1 - 2 * lax.rem(i, 2)) + (1 - k) * (3 - i) for i in coord]
    opp = [lax.rem(i + 2, 4) for i in coord]
    sent = []

    def local(src, dst, n):
        copy = pltpu.make_async_copy(src, dst, load.at[n])
        copy.start()
        return copy

    column = []
    for j in range(4):
        for e in range(2):
            if j or e:
                column.append(device(lax.rem(z + j, 4), lax.rem(k + e, 2), y, x))
    peers = column + [moved(here, dim, j)[0] for dim in (1, 2) for j in (1, 2, 3)]
    greet(peers)
    tok_in = local(tok_hbm, tok, 0)
    win_in = [local(win_hbm.at[:, pl.ds(512 * n, 512)], win.at[:, pl.ds(512 * n, 512)], 1 + n) for n in range(4)]
    tab_in = local(tab_hbm, tab, 5)
    wout_in = local(wout_hbm, wout, 6)
    own_in = local(tab_hbm.at[pl.ds(pl.multiple_of((y * 4 + x) * 64, 64), 64), :], tab_own, 7)

    query = queries[...].astype(F32)
    lane = lax.broadcasted_iota(jnp.int32, (8, 128), 1)
    digit = jnp.floor(slot[...] * 0.0078125)
    qall[z, k, y, x] = jnp.concatenate(
        [
            jnp.concatenate([query[:, :512], digit], axis=1),
            jnp.concatenate([query[:, 512:], slot[...] - 128.0 * digit], axis=1),
        ],
        axis=0,
    ).astype(BF16)
    payload = ((0, qall),)

    def gather_first():
        copies = []
        for j in (1, 2, 3):
            peer, _ = moved(here, 0, j)
            for n, buf in payload:
                mine = buf.at[z, k, y, x]
                copies.append(push(mine, mine, sems_q.at[0, n, j - 1], semr_q.at[0, n, j - 1], peer))
        return copies

    def gather_second():
        for copy in first:
            copy.wait_recv()
        copies = []
        for n, buf, dst in ((0, qall, qcol),):
            copies.append(push(buf.at[:, k, y, x], dst.at[k], sems_q.at[1, n, 0], semr_q.at[1, n, 0], sibling))
        for j in (1, 2, 3):
            peer, _ = moved(here, 1, j)
            for n, buf in payload:
                mine = buf.at[:, k, y, x]
                copies.append(push(mine, mine, sems_q.at[2, n, j - 1], semr_q.at[2, n, j - 1], peer))
        qcol[k] = qall[:, k, y, x]
        return copies

    def gather_third():
        copies = []
        for m, to in enumerate((fst[2], snd[2])):
            for n, buf in payload:
                mine = buf.at[:, k, :, x]
                copies.append(push(mine, mine, sems_q.at[3, n, m], semr_q.at[3, n, m], put(here, 2, to)))
        return copies

    def gather_fourth():
        for copy in third[:1]:
            copy.wait_recv()
        copies = []
        for n, buf in payload:
            near = buf.at[:, k, :, fst[2]]
            copies.append(push(near, near, sems_q.at[3, n, 2], semr_q.at[3, n, 2], put(here, 2, snd[2])))
        return copies

    def gather_last():
        copies = []
        for n, buf in payload:
            mine = buf.at[:, k]
            copies.append(push(mine, mine, sems_q.at[4, n, 0], semr_q.at[4, n, 0], sibling))
        return copies

    def project(n, carry):
        at = pl.ds(pl.multiple_of(n * 256, 256), 256)
        weight = win[:, at]
        bias = bias_in[:, at]
        for m in range(4):
            rows = slice(m * 256, m * 256 + 256)
            pre = dot(tok[rows, :], weight) + bias
            cdf = 0.5 * (1.0 + lax.erf(pre * 0.7071067811865476))
            hidden[rows, at] = (pre * cdf).astype(BF16)
            slope[rows, at] = cdf + pre * 0.3989422804014327 * jnp.exp(-0.5 * pre * pre)
        turn = pl.ds(pl.multiple_of(n * 128, 128), 128)
        tok_t[turn, :] = tok[:, turn].T
        return carry

    tok_in.wait()
    win_in[0].wait()
    lax.fori_loop(0, 1, project, 0)
    greeted(peers)
    first = gather_first()
    lax.fori_loop(1, 2, project, 0)
    win_in[1].wait()
    lax.fori_loop(2, 4, project, 0)
    second = gather_second()
    win_in[2].wait()
    lax.fori_loop(4, 6, project, 0)
    win_in[3].wait()
    lax.fori_loop(6, 8, project, 0)
    for copy in second:
        copy.wait_recv()
    third = gather_third()
    sent += first + second + third

    tab_in.wait()
    own_in.wait()
    wide_q = qcol[...].astype(F32).reshape(8, 16, 640)
    left = wide_q[:, :8, :512].reshape(64, 512).astype(BF16)
    right = wide_q[:, 8:, :512].reshape(64, 512).astype(BF16)
    ids = (wide_q[:, :8, 512:] * 128.0 + wide_q[:, 8:, 512:]).reshape(64, 128)
    ids = jnp.concatenate([ids, jnp.zeros((64, 128), F32)], axis=0).T[:16, :64]
    dots[...] = jnp.zeros_like(dots)

    def score_rows(i, carry):
        start = pl.multiple_of(i * 128, 128)
        block = tab[pl.ds(start, 128), :]
        wide = block.astype(F32)
        scale = lax.rsqrt(jnp.sum(wide * wide, axis=1, keepdims=True) + norm_eps)
        score = (dot(block[:, :512], left, 1, 1) + dot(block[:, 512:], right, 1, 1)) * scale
        names = (lax.broadcasted_iota(jnp.int32, (128, 64), 0) + (start + c * 1024)).astype(F32)
        found = []
        for slot in range(12):
            hit = jnp.where(names == ids[slot : slot + 1, :], score, 0.0)
            found.append(jnp.sum(hit, axis=0, keepdims=True))
        found.append(jnp.zeros((4, 64), F32))
        dots[:, :64] += jnp.concatenate(found, axis=0)
        return carry

    lax.fori_loop(0, 8, score_rows, 0)
    back = [push(dots, dall.at[n], dsem.at[n], dsemr.at[n], peer) for n, peer in enumerate(column)]
    sent += back


    wout_in.wait()
    which = lax.broadcasted_iota(jnp.int32, (8, 1024), 0)

    def normalise(i, carry):
        rows = pl.ds(pl.multiple_of(i * 256, 256), 256)
        summed = tok[rows, :].astype(F32) + dot(hidden[rows, :], wout[...]) + bias_out[...]
        centred = summed - jnp.mean(summed, axis=1, keepdims=True)
        inv = lax.rsqrt(jnp.mean(centred * centred, axis=1, keepdims=True) + norm_eps)
        value = centred * inv
        normed[rows, :] = value
        inv_std[rows, :] = jnp.broadcast_to(inv, (256, 128))
        for h in range(2):
            line = jnp.sum(value[h * 128 : h * 128 + 128], axis=0, keepdims=True)
            carry = jnp.where(which == 2 * i + h, line, carry)
        return carry

    norm_sum = lax.fori_loop(0, 2, normalise, jnp.zeros((8, 1024), F32))
    fourth = gather_fourth()
    sent += fourth
    norm_sum = lax.fori_loop(2, 4, normalise, norm_sum)

    for copy in back:
        copy.wait_recv()
    total = dots[...]
    for n in range(7):
        total += dall[n]
    turned[...] = jnp.concatenate([total, jnp.zeros((112, 128), F32)], axis=0).T
    raw = turned[pl.ds(pl.multiple_of((k * 4 + z) * 8, 8), 8), :]
    pooled = norm_sum * gain[...] + 128.0 * shift[...]
    emb_scale = lax.rsqrt(jnp.sum(pooled * pooled, axis=1, keepdims=True) + norm_eps)
    emb = pooled * emb_scale
    q_scale = lax.rsqrt(jnp.sum(query * query, axis=1, keepdims=True) + norm_eps)
    question = query * q_scale
    positive = jnp.sum(question * emb, axis=1, keepdims=True) / logit_divisor
    live = lane.astype(F32) < slot[:, 12:13]
    weights = jnp.where(live, jnp.exp(raw * q_scale / logit_divisor), 0.0)
    own = jnp.exp(positive)
    whole = own + jnp.sum(weights, axis=1, keepdims=True)
    cg[z, k] = weights / whole / logit_divisor * q_scale
    emb_slope = ((own / whole - 1.0) / logit_divisor) * question
    d_pooled = emb_scale * (emb_slope - emb * jnp.sum(emb * emb_slope, axis=1, keepdims=True))
    grad_shift = jnp.sum(d_pooled, axis=0, keepdims=True) * 128.0
    grad_gain = jnp.sum(d_pooled * norm_sum, axis=0, keepdims=True)
    lead = d_pooled * gain[...]

    def slopes(step):
        if step == 0:
            mine = cg.at[z, k]
            return [push(mine, mine, cs.at[0, 0], cr.at[0, 0], sibling)]
        if step == 2:
            tile = cg[0, 0]
            for n in range(1, 8):
                tile += pltpu.roll(cg[n // 2, n % 2], 16 * n, 1)
            cm[y, x] = tile
        dim = step - 1
        mine = (cg.at[z], cm.at[y, x], cm.at[:, x])[dim]
        copies = []
        for j in (1, 2, 3):
            peer, _ = moved(here, dim, j)
            copies.append(push(mine, mine, cs.at[step, j - 1], cr.at[step, j - 1], peer))
        return copies

    def arrived(copies):
        for copy in copies:
            copy.wait_recv()

    slope_step = slopes(0)
    sent += slope_step

    def back_norm(i, carry):
        rows = pl.ds(pl.multiple_of(i * 128, 128), 128)
        g = jnp.sum(jnp.where(which == i, lead, 0.0), axis=0, keepdims=True)
        value = normed[rows, :]
        inv = inv_std[rows, :][:, :1]
        both = jnp.mean(value * g, axis=1, keepdims=True)
        ds = inv * (g - jnp.mean(g, axis=1, keepdims=True) - value * both)
        d_sum[rows, :] = ds.astype(BF16)
        return carry + jnp.sum(ds, axis=0, keepdims=True)

    grad_bias_out = lax.fori_loop(0, 8, back_norm, jnp.zeros((1, 1024), F32))
    for copy in third[1:] + fourth:
        copy.wait_recv()
    last = gather_last()
    sent += last
    arrived(slope_step)
    slope_step = slopes(1)
    sent += slope_step

    def grad_out(zz, core):
        at = pl.ds(pl.multiple_of((zz * 2 + core) * 256, 256), 256)
        value = dot(hidden[:, at], d_sum[...], 0, 0)
        part[0, zz, core] = value.astype(BF16).reshape(4, 4, 16, 1024)

    zero = {}
    for zz in range(4):
        grad_out(zz, 1 - k)
        zero[0, zz] = push(part.at[0, zz, 1 - k], r0.at[0, zz], sem0.at[0, zz], rsem0.at[0, zz], sibling)

    arrived(slope_step)
    slope_step = slopes(2)
    sent += slope_step

    def own_blocks(zz, carry):
        grad_out(zz, k)
        return carry

    lax.fori_loop(0, 4, own_blocks, 0)
    arrived(slope_step)
    slope_step = slopes(3)
    sent += slope_step

    def add_core(w, lo, hi, first, last):
        def one(i, carry):
            a, e = i // 4, lax.rem(i, 4)
            r0[w, a, e, :, :, lo:hi] = r0[w, a, e, :, :, lo:hi] + part[w, a, k, e, :, :, lo:hi]
            return carry
        lax.fori_loop(first, last, one, 0)

    def rest(p):
        return [d for d in (0, 1, 2) if d != ORDER[p][0]]

    def stage_one(w, p):
        dim = ORDER[p][0]
        peer = put(here, dim, fst[dim])
        copies = []
        for n, to in enumerate((opp[dim], fst[dim])):
            src = pick(r0.at[w], dim, to, PARTS[w][p])
            copies.append(push(src, r1[w][p].at[n], sems.at[0, w, p, n], semr.at[0, w, p, n], peer))
        return copies

    def relay_one(w, p):
        dim = ORDER[p][0]
        mine = pick(r0.at[w], dim, snd[dim], PARTS[w][p])

        def one(e, carry):
            mine[e] = mine[e] + r1[w][p][0, e]
            return carry
        lax.fori_loop(0, 4, one, 0)
        return [push(mine, r1[w][p].at[2], sems.at[0, w, p, 2], semr.at[0, w, p, 2], put(here, dim, snd[dim]))]

    def add_one(w, p):
        dim = ORDER[p][0]
        mine = pick(r0.at[w], dim, coord[dim], PARTS[w][p])
        g, lo = JOINED[w][p]
        to = slice(lo, lo + PARTS[w][p][1] - PARTS[w][p][0])

        def one(e, carry):
            value = mine[e].astype(F32) + r1[w][p][1, e].astype(F32) + r1[w][p][2, e].astype(F32)
            s1[g][e, :, :, to] = value.astype(BF16)
            return carry
        lax.fori_loop(0, 4, one, 0)

    def stage_two(g):
        dim = ORDER[g][1]
        copies = []
        for j in (1, 2, 3):
            peer, to = moved(here, dim, j)
            src = pick(s1[g], rest(g).index(dim), to)
            copies.append(push(src, r2[g].at[j - 1], sems.at[1, 0, g, j - 1], semr.at[1, 0, g, j - 1], peer))
        return copies

    def add_two(g):
        dim = ORDER[g][1]
        value = pick(s1[g], rest(g).index(dim), coord[dim])[...].astype(F32)
        for j in range(3):
            value += r2[g][j].astype(F32)
        s2[g][...] = value

    def stage_three(g):
        dim = ORDER[g][2]
        copies = []
        for j in (1, 2, 3):
            peer, to = moved(here, dim, j)
            copies.append(push(s2[g].at[to], r3[g].at[j - 1], sems.at[2, 0, g, j - 1], semr.at[2, 0, g, j - 1], peer))
        return copies

    def add_three(g):
        value = s2[g][coord[ORDER[g][2]]] + r3[g][0] + r3[g][1] + r3[g][2]
        for w in range(2):
            for p, (lo, hi) in enumerate(PARTS[w]):
                if JOINED[w][p][0] != g:
                    continue
                at = JOINED[w][p][1]
                if w == 0:
                    g_out[:, lo:hi] = value[:, at : at + hi - lo]
                    continue
                for n in range((hi - lo) // 128):
                    tile = value[:, at + n * 128 : at + n * 128 + 128]
                    g_in[:, 2 * lo + 256 * n : 2 * lo + 256 * n + 128] = tile[:8]
                    g_in[:, 2 * lo + 256 * n + 128 : 2 * lo + 256 * n + 256] = tile[8:]

    def back_layer(n, carry):
        at = pl.ds(pl.multiple_of(n * 256, 256), 256)
        weight = wout[at, :]
        line = jnp.zeros((1, 256), F32)
        for m in range(4):
            rows = slice(m * 256, m * 256 + 256)
            value = dot(d_sum[rows, :], weight, 1, 1) * slope[rows, at]
            line += jnp.sum(value, axis=0, keepdims=True)
            d_pre[rows, :] = value.astype(BF16)
        bias_acc[:, at] = line
        to = pl.ds(pl.multiple_of(n * 128, 128), 128)
        for m in range(4):
            value = dot(tok_t[m * 256 : m * 256 + 256, :], d_pre[...])
            value = value.reshape(32, 8, 256)
            value = jnp.concatenate([value[:, :, :128], value[:, :, 128:]], axis=1).astype(BF16)
            part[1, m, :, :, :, :, to] = value.reshape(2, 4, 4, 16, 128)
        return carry

    ones, twos, threes = {}, {}, {}

    def start(w, p):
        ones[w, p] = stage_one(w, p)

    def pass_on(w, p):
        ones[w, p][0].wait_recv()
        ones[w, p] += relay_one(w, p)

    def end_one(w, p):
        arrived(ones[w, p][1:])
        add_one(w, p)

    def end_two(g):
        arrived(twos[g])
        add_two(g)
        threes[g] = stage_three(g)

    def end_three(g):
        arrived(threes[g])
        add_three(g)

    def to_sibling(n, lo, hi):
        cut = pl.ds(lo, hi - lo)
        zero[1, n] = push(
            part.at[1, :, 1 - k, :, :, :, cut], r0.at[1, :, :, :, :, cut], sem0.at[1, n], rsem0.at[1, n], sibling
        )

    for zz in range(4):
        zero[0, zz].wait_recv()
        add_core(0, 0, 1024, 4 * zz, 4 * zz + 4)
    for p in range(3):
        start(0, p)
    early, late = (0, 1, 2), (3, 4, 5)
    lax.fori_loop(0, 5, back_layer, 0)
    to_sibling(0, 0, 640)
    for p in range(3):
        pass_on(0, p)
    lax.fori_loop(5, 6, back_layer, 0)
    for p in range(3):
        end_one(0, p)
    lax.fori_loop(6, 7, back_layer, 0)
    zero[1, 0].wait_recv()
    add_core(1, 0, 640, 0, 16)
    for p in early:
        start(1, p)
    lax.fori_loop(7, 8, back_layer, 0)
    to_sibling(1, 640, 1024)
    sm[0, k] = jnp.concatenate(
        [bias_acc[:, :1024], bias_acc[:, 1024:], grad_bias_out, grad_gain, grad_shift, jnp.zeros((3, 1024), F32)], axis=0
    )
    small = [push(sm.at[0, k], sm.at[0, k], qs.at[0, 0], qr.at[0, 0], sibling)]
    sent += small

    def stage_small(step):
        dim = step - 1
        got = sm[step - 1, 0] + sm[step - 1, 1]
        if step > 1:
            got = (got + sm[step - 1, 2]) + sm[step - 1, 3]
        sm[step, coord[dim]] = got
        copies = []
        for j in (1, 2, 3):
            peer, _ = moved(here, dim, j)
            mine = sm.at[step, coord[dim]]
            copies.append(push(mine, mine, qs.at[step, j - 1], qr.at[step, j - 1], peer))
        return copies

    arrived(last)
    arrived(slope_step)
    base = c * 1024 + (y * 4 + x) * 64
    row = (lax.broadcasted_iota(jnp.int32, (256, 128), 1) + base).astype(F32)

    def collect(i):
        some = qall[i].astype(F32).reshape(32, 16, 640)
        name = (some[:, :8, 512:] * 128.0 + some[:, 8:, 512:]).reshape(256, 128)
        tiles = cm[...].reshape(128, 128)
        value = jnp.concatenate([pltpu.roll(tiles, (128 - 16 * n) % 128, 1) for n in (2 * i, 2 * i + 1)], axis=0)
        weight = jnp.zeros((256, 128), F32)
        for slot in range(12):
            weight += jnp.where(name[:, slot : slot + 1] == row, value[:, slot : slot + 1], 0.0)
        high = weight.astype(BF16)
        low = (weight - high.astype(F32)).astype(BF16)
        for h in range(2):
            half = some[:, h * 8 : h * 8 + 8, :512].reshape(256, 512).astype(BF16)
            found = (dot(high, half, 0, 0) + dot(low, half, 0, 0))[:64]
            at = slice(h * 512, h * 512 + 512)
            g_table[:, at] = found if i == 0 else g_table[:, at] + found

    collect(0)
    for p in early:
        pass_on(1, p)
    arrived(small)
    small = stage_small(1)
    sent += small
    zero[1, 1].wait_recv()
    add_core(1, 640, 1024, 0, 16)
    for p in late:
        start(1, p)
    collect(1)
    for p in early:
        end_one(1, p)
        twos[p] = stage_two(p)
    for p in late:
        pass_on(1, p)
    arrived(small)
    small = stage_small(2)
    sent += small
    collect(2)
    for p in late:
        end_one(1, p)
        twos[p] = stage_two(p)
    for p in early:
        end_two(p)
    arrived(small)
    small = stage_small(3)
    sent += small
    collect(3)
    for p in late:
        end_two(p)
    table_slope = g_table[...]
    rows = tab_own[...].astype(F32)
    scale = lax.rsqrt(jnp.sum(rows * rows, axis=1, keepdims=True) + norm_eps)
    unit = rows * scale
    g_table[...] = scale * (table_slope - unit * jnp.sum(unit * table_slope, axis=1, keepdims=True))
    for p in early:
        end_three(p)
    arrived(small)
    got = ((sm[3, 0] + sm[3, 1]) + sm[3, 2]) + sm[3, 3]
    g_bias_in[:, :1024] = got[0:1]
    g_bias_in[:, 1024:] = got[1:2]
    g_bias_out[...] = got[2:3]
    g_gain[...] = got[3:4]
    g_shift[...] = got[4:5]
    for p in late:
        end_three(p)
    for group in (ones, twos, threes):
        for copies in group.values():
            sent += copies
    for copy in sent + list(zero.values()):
        copy.wait_send()


def hand_over_kernel(*refs):
    for src, dst in zip(refs[:7], refs[7:]):
        dst[...] = src[...]


def hand_over(*results):
    vmem = pl.BlockSpec(memory_space=pltpu.VMEM)
    return pl.pallas_call(
        hand_over_kernel,
        out_shape=tuple(jax.ShapeDtypeStruct(value.shape, value.dtype) for value in results),
        in_specs=[vmem] * 7,
        out_specs=(vmem,) * 7,
    )(*results)


def step(*operands):
    vmem, hbm = pl.BlockSpec(memory_space=pltpu.VMEM), pl.BlockSpec(memory_space=pl.ANY)

    def scratch(shape, kind):
        return tuple(tuple(pltpu.VMEM(shape + (16, hi - lo), kind) for lo, hi in row) for row in PARTS)

    def joined(shape, kind):
        return tuple(pltpu.VMEM(shape + (16, width), kind) for width in WIDTHS)

    dma = pltpu.SemaphoreType.DMA
    out = jax.ShapeDtypeStruct
    return pl.pallas_call(
        step_kernel,
        out_shape=(
            out((8, 2048), F32),
            out((1, 2048), F32),
            out((16, 1024), F32),
            out((1, 1024), F32),
            out((1, 1024), F32),
            out((1, 1024), F32),
            out((64, 1024), F32),
        ),
        in_specs=[hbm] * 4 + [vmem] * 6,
        out_specs=(vmem,) * 7,
        scratch_shapes=[
            pltpu.VMEM((1024, 1024), BF16),
            pltpu.VMEM((1024, 2048), BF16),
            pltpu.VMEM((2048, 1024), BF16),
            pltpu.VMEM((1024, 1024), BF16),
            pltpu.VMEM((64, 1024), BF16),
            pltpu.VMEM((1024, 1024), BF16),
            pltpu.VMEM((1024, 2048), BF16),
            pltpu.VMEM((1024, 2048), F32),
            pltpu.VMEM((1024, 1024), F32),
            pltpu.VMEM((1024, 128), F32),
            pltpu.VMEM((1024, 1024), BF16),
            pltpu.VMEM((1024, 256), BF16),
            pltpu.VMEM((1, 2048), F32),
            pltpu.VMEM((4, 2, 4, 4, 16, 640), BF16),
            pltpu.VMEM((2, 4, 16, 640), BF16),
            pltpu.VMEM((16, 128), F32),
            pltpu.VMEM((7, 16, 128), F32),
            pltpu.VMEM((128, 128), F32),
            pltpu.VMEM((2, 4, 2, 4, 4, 16, 1024), BF16),
            pltpu.VMEM((2, 4, 4, 4, 16, 1024), BF16),
            scratch((3, 4, 4), BF16),
            joined((4, 4), BF16),
            joined((3, 4), BF16),
            joined((4,), F32),
            joined((3,), F32),
            pltpu.VMEM((4, 4, 8, 1024), F32),
            pltpu.VMEM((4, 2, 8, 128), F32),
            pltpu.VMEM((4, 4, 8, 128), F32),
            dma((8,)),
            dma((5, 1, 3)),
            dma((5, 1, 3)),
            dma((7,)),
            dma((7,)),
            dma((2, 4)),
            dma((2, 4)),
            dma((3, 2, 6, 3)),
            dma((3, 2, 6, 3)),
            dma((4, 3)),
            dma((4, 3)),
            dma((4, 3)),
            dma((4, 3)),
        ],
        compiler_params=pltpu.CompilerParams(
            collective_id=0, has_side_effects=True, vmem_limit_bytes=VMEM_BYTES
        ),
    )(*operands)


def body(
    tokens,
    weight_in,
    bias_in,
    weight_out,
    bias_out,
    norm_gain,
    norm_shift,
    queries,
    corpus_table,
    neg_owner,
    neg_row,
    neg_count,
):
    count_q, seq, width = tokens.shape
    slots = neg_row.shape[1]
    ids = (neg_owner.reshape(count_q, slots) * 1024 + neg_row).astype(F32)
    counts = neg_count.astype(F32)[:, None]
    slot = jnp.concatenate([ids, counts, jnp.full((count_q, 128 - slots - 1), -1.0, F32)], axis=1)
    results = step(
        tokens.reshape(count_q * seq, width),
        weight_in,
        weight_out,
        corpus_table,
        bias_in[None],
        bias_out[None],
        norm_gain[None],
        norm_shift[None],
        queries,
        slot,
    )
    grad_in, g_bias_in, grad_out, g_bias_out, g_gain, g_shift, grad_table = hand_over(*results)
    return (grad_in, g_bias_in[0], grad_out, g_bias_out[0], g_gain[0], g_shift[0], grad_table)


def solution(mesh):
    return jax.shard_map(
        body,
        mesh=mesh,
        in_specs=(
            P(("corpus", "batch"), None, None),
            P(),
            P(),
            P(),
            P(),
            P(),
            P(),
            P(("corpus", "batch"), None),
            P("corpus", None),
            P(("corpus", "batch"), None, None),
            P(("corpus", "batch"), None),
            P(("corpus", "batch")),
        ),
        out_specs=(
            P(("corpus", "batch"), None),
            P(),
            P(("corpus", "batch"), None),
            P(),
            P(),
            P(),
            P(("corpus", "batch"), None),
        ),
        check_vma=False,
    )
```

```python
import functools

import jax
import jax.numpy as jnp
from jax import lax
from jax.experimental import pallas as pl
from jax.experimental.pallas import tpu as pltpu
from jax.sharding import PartitionSpec as P

logit_divisor = 0.05
norm_eps = 1e-06
MESH = pl.DeviceIdType.MESH
F32, BF16 = jnp.float32, jnp.bfloat16
VMEM_BYTES = 60 * 1024 * 1024


def place():
    c, b = lax.axis_index("corpus"), lax.axis_index("batch")
    return c // 2, c % 2, b // 4, b % 4


def device(z, k, y, x):
    return (z * 2 + k, y * 4 + x)


def moved(here, dim, offset):
    z, k, y, x = here
    at = [z, y, x]
    at[dim] = lax.rem(at[dim] + offset, 4)
    return device(at[0], k, at[1], at[2]), at[dim]


def put(here, dim, to):
    z, k, y, x = here
    at = [z, y, x]
    at[dim] = to
    return device(at[0], k, at[1], at[2])


def greet(peers):
    barrier = pltpu.get_barrier_semaphore()
    for peer in peers:
        pl.semaphore_signal(barrier, inc=1, device_id=peer, device_id_type=MESH)


def greeted(peers):
    pl.semaphore_wait(pltpu.get_barrier_semaphore(), len(peers))


def push(src, dst, send, recv, peer):
    copy = pltpu.make_async_remote_copy(
        src_ref=src, dst_ref=dst, send_sem=send, recv_sem=recv, device_id=peer, device_id_type=MESH
    )
    copy.start()
    return copy


PARTS = (
    ((0, 384), (384, 768), (768, 1024)),
    ((0, 256), (256, 512), (512, 640), (640, 768), (768, 896), (896, 1024)),
)
ORDER = ((0, 1, 2), (1, 2, 0), (2, 0, 1)) * 2
JOINED = (((0, 0), (1, 0), (2, 0)), ((0, 384), (1, 384), (2, 256), (3, 0), (4, 0), (5, 0)))
WIDTHS = (640, 640, 384, 128, 128, 128)


def pick(ref, axis, index, columns=None):
    at = [slice(None)] * (len(ref.shape) - 2)
    at[axis] = index
    return ref.at[tuple(at) + (slice(None), slice(None) if columns is None else pl.ds(columns[0], columns[1] - columns[0]))]


def dot(a, b, ca=1, cb=0):
    return lax.dot_general(a, b, (((ca,), (cb,)), ((), ())), preferred_element_type=F32)


def step_kernel(
    tok_hbm, win_hbm, wout_hbm, tab_hbm, bias_in, bias_out, gain, shift, queries, slot,
    g_in, g_bias_in, g_out, g_bias_out, g_gain, g_shift, g_table,
    tok, win, wout, tab, tab_own, tok_t, hidden, slope, normed, inv_std, d_sum, d_pre, bias_acc,
    qall, qcol, dots, dall, turned,
    part, r0, r1, s1, r2, s2, r3, sm, cg, cm,
    load, sems_q, semr_q, dsem, dsemr, sem0, rsem0, sems, semr, qs, qr, cs, cr,
):
    here = place()
    z, k, y, x = here
    coord = (z, y, x)
    c = z * 2 + k
    sibling = device(z, 1 - k, y, x)
    fst = [(1 - k) * (i + 1 - 2 * lax.rem(i, 2)) + k * (3 - i) for i in coord]
    snd = [k * (i + 1 - 2 * lax.rem(i, 2)) + (1 - k) * (3 - i) for i in coord]
    opp = [lax.rem(i + 2, 4) for i in coord]
    sent = []

    def local(src, dst, n):
        copy = pltpu.make_async_copy(src, dst, load.at[n])
        copy.start()
        return copy

    column = []
    for j in range(4):
        for e in range(2):
            if j or e:
                column.append(device(lax.rem(z + j, 4), lax.rem(k + e, 2), y, x))
    peers = column + [moved(here, dim, j)[0] for dim in (1, 2) for j in (1, 2, 3)]
    greet(peers)
    tok_in = local(tok_hbm, tok, 0)
    win_in = [local(win_hbm.at[:, pl.ds(512 * n, 512)], win.at[:, pl.ds(512 * n, 512)], 1 + n) for n in range(4)]
    tab_in = local(tab_hbm, tab, 5)
    wout_in = local(wout_hbm, wout, 6)
    own_in = local(tab_hbm.at[pl.ds(pl.multiple_of((y * 4 + x) * 64, 64), 64), :], tab_own, 7)

    query = queries[...].astype(F32)
    lane = lax.broadcasted_iota(jnp.int32, (8, 128), 1)
    digit = jnp.floor(slot[...] * 0.0078125)
    qall[z, k, y, x] = jnp.concatenate(
        [
            jnp.concatenate([query[:, :512], digit], axis=1),
            jnp.concatenate([query[:, 512:], slot[...] - 128.0 * digit], axis=1),
        ],
        axis=0,
    ).astype(BF16)
    payload = ((0, qall),)

    def gather_first():
        copies = []
        for j in (1, 2, 3):
            peer, _ = moved(here, 0, j)
            for n, buf in payload:
                mine = buf.at[z, k, y, x]
                copies.append(push(mine, mine, sems_q.at[0, n, j - 1], semr_q.at[0, n, j - 1], peer))
        return copies

    def gather_second():
        for copy in first:
            copy.wait_recv()
        copies = []
        for n, buf, dst in ((0, qall, qcol),):
            copies.append(push(buf.at[:, k, y, x], dst.at[k], sems_q.at[1, n, 0], semr_q.at[1, n, 0], sibling))
        for j in (1, 2, 3):
            peer, _ = moved(here, 1, j)
            for n, buf in payload:
                mine = buf.at[:, k, y, x]
                copies.append(push(mine, mine, sems_q.at[2, n, j - 1], semr_q.at[2, n, j - 1], peer))
        qcol[k] = qall[:, k, y, x]
        return copies

    def gather_third():
        copies = []
        for m, to in enumerate((fst[2], snd[2])):
            for n, buf in payload:
                mine = buf.at[:, k, :, x]
                copies.append(push(mine, mine, sems_q.at[3, n, m], semr_q.at[3, n, m], put(here, 2, to)))
        return copies

    def gather_fourth():
        for copy in third[:1]:
            copy.wait_recv()
        copies = []
        for n, buf in payload:
            near = buf.at[:, k, :, fst[2]]
            copies.append(push(near, near, sems_q.at[3, n, 2], semr_q.at[3, n, 2], put(here, 2, snd[2])))
        return copies

    def gather_last():
        copies = []
        for n, buf in payload:
            mine = buf.at[:, k]
            copies.append(push(mine, mine, sems_q.at[4, n, 0], semr_q.at[4, n, 0], sibling))
        return copies

    def project(n, carry):
        at = pl.ds(pl.multiple_of(n * 256, 256), 256)
        weight = win[:, at]
        bias = bias_in[:, at]
        for m in range(4):
            rows = slice(m * 256, m * 256 + 256)
            pre = dot(tok[rows, :], weight) + bias
            cdf = 0.5 * (1.0 + lax.erf(pre * 0.7071067811865476))
            hidden[rows, at] = (pre * cdf).astype(BF16)
            slope[rows, at] = cdf + pre * 0.3989422804014327 * jnp.exp(-0.5 * pre * pre)
        turn = pl.ds(pl.multiple_of(n * 128, 128), 128)
        tok_t[turn, :] = tok[:, turn].T
        return carry

    tok_in.wait()
    win_in[0].wait()
    lax.fori_loop(0, 1, project, 0)
    greeted(peers)
    first = gather_first()
    lax.fori_loop(1, 2, project, 0)
    win_in[1].wait()
    lax.fori_loop(2, 4, project, 0)
    second = gather_second()
    win_in[2].wait()
    lax.fori_loop(4, 6, project, 0)
    win_in[3].wait()
    lax.fori_loop(6, 8, project, 0)
    for copy in second:
        copy.wait_recv()
    third = gather_third()
    sent += first + second + third

    tab_in.wait()
    own_in.wait()
    wide_q = qcol[...].astype(F32).reshape(8, 16, 640)
    left = wide_q[:, :8, :512].reshape(64, 512).astype(BF16)
    right = wide_q[:, 8:, :512].reshape(64, 512).astype(BF16)
    ids = (wide_q[:, :8, 512:] * 128.0 + wide_q[:, 8:, 512:]).reshape(64, 128)
    ids = jnp.concatenate([ids, jnp.zeros((64, 128), F32)], axis=0).T[:16, :64]
    dots[...] = jnp.zeros_like(dots)

    def score_rows(i, carry):
        start = pl.multiple_of(i * 128, 128)
        block = tab[pl.ds(start, 128), :]
        wide = block.astype(F32)
        scale = lax.rsqrt(jnp.sum(wide * wide, axis=1, keepdims=True) + norm_eps)
        score = (dot(block[:, :512], left, 1, 1) + dot(block[:, 512:], right, 1, 1)) * scale
        names = (lax.broadcasted_iota(jnp.int32, (128, 64), 0) + (start + c * 1024)).astype(F32)
        found = []
        for slot in range(12):
            hit = jnp.where(names == ids[slot : slot + 1, :], score, 0.0)
            found.append(jnp.sum(hit, axis=0, keepdims=True))
        found.append(jnp.zeros((4, 64), F32))
        dots[:, :64] += jnp.concatenate(found, axis=0)
        return carry

    lax.fori_loop(0, 8, score_rows, 0)
    back = [push(dots, dall.at[n], dsem.at[n], dsemr.at[n], peer) for n, peer in enumerate(column)]
    sent += back


    wout_in.wait()
    which = lax.broadcasted_iota(jnp.int32, (8, 1024), 0)

    def normalise(i, carry):
        rows = pl.ds(pl.multiple_of(i * 256, 256), 256)
        summed = tok[rows, :].astype(F32) + dot(hidden[rows, :], wout[...]) + bias_out[...]
        centred = summed - jnp.mean(summed, axis=1, keepdims=True)
        inv = lax.rsqrt(jnp.mean(centred * centred, axis=1, keepdims=True) + norm_eps)
        value = centred * inv
        normed[rows, :] = value
        inv_std[rows, :] = jnp.broadcast_to(inv, (256, 128))
        for h in range(2):
            line = jnp.sum(value[h * 128 : h * 128 + 128], axis=0, keepdims=True)
            carry = jnp.where(which == 2 * i + h, line, carry)
        return carry

    norm_sum = lax.fori_loop(0, 2, normalise, jnp.zeros((8, 1024), F32))
    fourth = gather_fourth()
    sent += fourth
    norm_sum = lax.fori_loop(2, 4, normalise, norm_sum)

    for copy in back:
        copy.wait_recv()
    total = dots[...]
    for n in range(7):
        total += dall[n]
    turned[...] = jnp.concatenate([total, jnp.zeros((112, 128), F32)], axis=0).T
    raw = turned[pl.ds(pl.multiple_of((k * 4 + z) * 8, 8), 8), :]
    pooled = norm_sum * gain[...] + 128.0 * shift[...]
    emb_scale = lax.rsqrt(jnp.sum(pooled * pooled, axis=1, keepdims=True) + norm_eps)
    emb = pooled * emb_scale
    q_scale = lax.rsqrt(jnp.sum(query * query, axis=1, keepdims=True) + norm_eps)
    question = query * q_scale
    positive = jnp.sum(question * emb, axis=1, keepdims=True) / logit_divisor
    live = lane.astype(F32) < slot[:, 12:13]
    weights = jnp.where(live, jnp.exp(raw * q_scale / logit_divisor), 0.0)
    own = jnp.exp(positive)
    whole = own + jnp.sum(weights, axis=1, keepdims=True)
    cg[z, k] = weights / whole / logit_divisor * q_scale
    emb_slope = ((own / whole - 1.0) / logit_divisor) * question
    d_pooled = emb_scale * (emb_slope - emb * jnp.sum(emb * emb_slope, axis=1, keepdims=True))
    grad_shift = jnp.sum(d_pooled, axis=0, keepdims=True) * 128.0
    grad_gain = jnp.sum(d_pooled * norm_sum, axis=0, keepdims=True)
    lead = d_pooled * gain[...]

    def slopes(step):
        if step == 0:
            mine = cg.at[z, k]
            return [push(mine, mine, cs.at[0, 0], cr.at[0, 0], sibling)]
        if step == 2:
            tile = cg[0, 0]
            for n in range(1, 8):
                tile += pltpu.roll(cg[n // 2, n % 2], 16 * n, 1)
            cm[y, x] = tile
        dim = step - 1
        mine = (cg.at[z], cm.at[y, x], cm.at[:, x])[dim]
        copies = []
        for j in (1, 2, 3):
            peer, _ = moved(here, dim, j)
            copies.append(push(mine, mine, cs.at[step, j - 1], cr.at[step, j - 1], peer))
        return copies

    def arrived(copies):
        for copy in copies:
            copy.wait_recv()

    slope_step = slopes(0)
    sent += slope_step

    def back_norm(i, carry):
        rows = pl.ds(pl.multiple_of(i * 128, 128), 128)
        g = jnp.sum(jnp.where(which == i, lead, 0.0), axis=0, keepdims=True)
        value = normed[rows, :]
        inv = inv_std[rows, :][:, :1]
        both = jnp.mean(value * g, axis=1, keepdims=True)
        ds = inv * (g - jnp.mean(g, axis=1, keepdims=True) - value * both)
        d_sum[rows, :] = ds.astype(BF16)
        return carry + jnp.sum(ds, axis=0, keepdims=True)

    grad_bias_out = lax.fori_loop(0, 8, back_norm, jnp.zeros((1, 1024), F32))
    for copy in third[1:] + fourth:
        copy.wait_recv()
    last = gather_last()
    sent += last
    arrived(slope_step)
    slope_step = slopes(1)
    sent += slope_step

    def grad_out(zz, core):
        at = pl.ds(pl.multiple_of((zz * 2 + core) * 256, 256), 256)
        value = dot(hidden[:, at], d_sum[...], 0, 0)
        part[0, zz, core] = value.astype(BF16).reshape(4, 4, 16, 1024)

    zero = {}
    for zz in range(4):
        grad_out(zz, 1 - k)
        zero[0, zz] = push(part.at[0, zz, 1 - k], r0.at[0, zz], sem0.at[0, zz], rsem0.at[0, zz], sibling)

    arrived(slope_step)
    slope_step = slopes(2)
    sent += slope_step

    def own_blocks(zz, carry):
        grad_out(zz, k)
        return carry

    lax.fori_loop(0, 4, own_blocks, 0)
    arrived(slope_step)
    slope_step = slopes(3)
    sent += slope_step

    def add_core(w, lo, hi, first, last):
        def one(i, carry):
            a, e = i // 4, lax.rem(i, 4)
            r0[w, a, e, :, :, lo:hi] = r0[w, a, e, :, :, lo:hi] + part[w, a, k, e, :, :, lo:hi]
            return carry
        lax.fori_loop(first, last, one, 0)

    def rest(p):
        return [d for d in (0, 1, 2) if d != ORDER[p][0]]

    def sides(w, p):
        return (snd, fst) if w == 1 and p > 2 else (fst, snd)

    def stage_one(w, p):
        dim = ORDER[p][0]
        fst, snd = sides(w, p)
        peer = put(here, dim, fst[dim])
        copies = []
        for n, to in enumerate((opp[dim], fst[dim])):
            src = pick(r0.at[w], dim, to, PARTS[w][p])
            copies.append(push(src, r1[w][p].at[n], sems.at[0, w, p, n], semr.at[0, w, p, n], peer))
        return copies

    def relay_one(w, p):
        dim = ORDER[p][0]
        fst, snd = sides(w, p)
        mine = pick(r0.at[w], dim, snd[dim], PARTS[w][p])

        def one(e, carry):
            mine[e] = mine[e] + r1[w][p][0, e]
            return carry
        lax.fori_loop(0, 4, one, 0)
        return [push(mine, r1[w][p].at[2], sems.at[0, w, p, 2], semr.at[0, w, p, 2], put(here, dim, snd[dim]))]

    def add_one(w, p):
        dim = ORDER[p][0]
        mine = pick(r0.at[w], dim, coord[dim], PARTS[w][p])
        g, lo = JOINED[w][p]
        to = slice(lo, lo + PARTS[w][p][1] - PARTS[w][p][0])

        def one(e, carry):
            value = mine[e].astype(F32) + r1[w][p][1, e].astype(F32) + r1[w][p][2, e].astype(F32)
            s1[g][e, :, :, to] = value.astype(BF16)
            return carry
        lax.fori_loop(0, 4, one, 0)

    def stage_two(g):
        dim = ORDER[g][1]
        copies = []
        for j in (1, 2, 3):
            peer, to = moved(here, dim, j)
            src = pick(s1[g], rest(g).index(dim), to)
            copies.append(push(src, r2[g].at[j - 1], sems.at[1, 0, g, j - 1], semr.at[1, 0, g, j - 1], peer))
        return copies

    def add_two(g):
        dim = ORDER[g][1]
        value = pick(s1[g], rest(g).index(dim), coord[dim])[...].astype(F32)
        for j in range(3):
            value += r2[g][j].astype(F32)
        s2[g][...] = value

    def stage_three(g):
        dim = ORDER[g][2]
        copies = []
        for j in (1, 2, 3):
            peer, to = moved(here, dim, j)
            copies.append(push(s2[g].at[to], r3[g].at[j - 1], sems.at[2, 0, g, j - 1], semr.at[2, 0, g, j - 1], peer))
        return copies

    def add_three(g):
        value = s2[g][coord[ORDER[g][2]]] + r3[g][0] + r3[g][1] + r3[g][2]
        for w in range(2):
            for p, (lo, hi) in enumerate(PARTS[w]):
                if JOINED[w][p][0] != g:
                    continue
                at = JOINED[w][p][1]
                if w == 0:
                    g_out[:, lo:hi] = value[:, at : at + hi - lo]
                    continue
                for n in range((hi - lo) // 128):
                    tile = value[:, at + n * 128 : at + n * 128 + 128]
                    g_in[:, 2 * lo + 256 * n : 2 * lo + 256 * n + 128] = tile[:8]
                    g_in[:, 2 * lo + 256 * n + 128 : 2 * lo + 256 * n + 256] = tile[8:]

    def back_layer(n, carry):
        at = pl.ds(pl.multiple_of(n * 256, 256), 256)
        weight = wout[at, :]
        line = jnp.zeros((1, 256), F32)
        for m in range(4):
            rows = slice(m * 256, m * 256 + 256)
            value = dot(d_sum[rows, :], weight, 1, 1) * slope[rows, at]
            line += jnp.sum(value, axis=0, keepdims=True)
            d_pre[rows, :] = value.astype(BF16)
        bias_acc[:, at] = line
        to = pl.ds(pl.multiple_of(n * 128, 128), 128)
        for m in range(4):
            value = dot(tok_t[m * 256 : m * 256 + 256, :], d_pre[...])
            value = value.reshape(32, 8, 256)
            value = jnp.concatenate([value[:, :, :128], value[:, :, 128:]], axis=1).astype(BF16)
            part[1, m, :, :, :, :, to] = value.reshape(2, 4, 4, 16, 128)
        return carry

    ones, twos, threes = {}, {}, {}

    def start(w, p):
        ones[w, p] = stage_one(w, p)

    def pass_on(w, p):
        ones[w, p][0].wait_recv()
        ones[w, p] += relay_one(w, p)

    def end_one(w, p):
        arrived(ones[w, p][1:])
        add_one(w, p)

    def end_two(g):
        arrived(twos[g])
        add_two(g)
        threes[g] = stage_three(g)

    def end_three(g):
        arrived(threes[g])
        add_three(g)

    def to_sibling(n, lo, hi):
        cut = pl.ds(lo, hi - lo)
        zero[1, n] = push(
            part.at[1, :, 1 - k, :, :, :, cut], r0.at[1, :, :, :, :, cut], sem0.at[1, n], rsem0.at[1, n], sibling
        )

    for zz in range(4):
        zero[0, zz].wait_recv()
        add_core(0, 0, 1024, 4 * zz, 4 * zz + 4)
    for p in range(3):
        start(0, p)
    early, late = (0, 1, 2), (3, 4, 5)
    lax.fori_loop(0, 5, back_layer, 0)
    to_sibling(0, 0, 640)
    for p in range(3):
        pass_on(0, p)
    lax.fori_loop(5, 6, back_layer, 0)
    for p in range(3):
        end_one(0, p)
    lax.fori_loop(6, 7, back_layer, 0)
    zero[1, 0].wait_recv()
    add_core(1, 0, 640, 0, 16)
    for p in early:
        start(1, p)
    lax.fori_loop(7, 8, back_layer, 0)
    to_sibling(1, 640, 1024)
    sm[0, k] = jnp.concatenate(
        [bias_acc[:, :1024], bias_acc[:, 1024:], grad_bias_out, grad_gain, grad_shift, jnp.zeros((3, 1024), F32)], axis=0
    )
    small = [push(sm.at[0, k], sm.at[0, k], qs.at[0, 0], qr.at[0, 0], sibling)]
    sent += small

    def stage_small(step):
        dim = step - 1
        got = sm[step - 1, 0] + sm[step - 1, 1]
        if step > 1:
            got = (got + sm[step - 1, 2]) + sm[step - 1, 3]
        sm[step, coord[dim]] = got
        copies = []
        for j in (1, 2, 3):
            peer, _ = moved(here, dim, j)
            mine = sm.at[step, coord[dim]]
            copies.append(push(mine, mine, qs.at[step, j - 1], qr.at[step, j - 1], peer))
        return copies

    arrived(last)
    arrived(slope_step)
    base = c * 1024 + (y * 4 + x) * 64
    row = (lax.broadcasted_iota(jnp.int32, (256, 128), 1) + base).astype(F32)

    def collect(i):
        some = qall[i].astype(F32).reshape(32, 16, 640)
        name = (some[:, :8, 512:] * 128.0 + some[:, 8:, 512:]).reshape(256, 128)
        tiles = cm[...].reshape(128, 128)
        value = jnp.concatenate([pltpu.roll(tiles, (128 - 16 * n) % 128, 1) for n in (2 * i, 2 * i + 1)], axis=0)
        weight = jnp.zeros((256, 128), F32)
        for slot in range(12):
            weight += jnp.where(name[:, slot : slot + 1] == row, value[:, slot : slot + 1], 0.0)
        high = weight.astype(BF16)
        low = (weight - high.astype(F32)).astype(BF16)
        for h in range(2):
            half = some[:, h * 8 : h * 8 + 8, :512].reshape(256, 512).astype(BF16)
            found = (dot(high, half, 0, 0) + dot(low, half, 0, 0))[:64]
            at = slice(h * 512, h * 512 + 512)
            g_table[:, at] = found if i == 0 else g_table[:, at] + found

    collect(0)
    for p in early:
        pass_on(1, p)
    arrived(small)
    small = stage_small(1)
    sent += small
    zero[1, 1].wait_recv()
    add_core(1, 640, 1024, 0, 16)
    for p in late:
        start(1, p)
    collect(1)
    for p in early:
        end_one(1, p)
        twos[p] = stage_two(p)
    for p in late:
        pass_on(1, p)
    arrived(small)
    small = stage_small(2)
    sent += small
    collect(2)
    for p in late:
        end_one(1, p)
        twos[p] = stage_two(p)
    for p in early:
        end_two(p)
    arrived(small)
    small = stage_small(3)
    sent += small
    collect(3)
    for p in late:
        end_two(p)
    table_slope = g_table[...]
    rows = tab_own[...].astype(F32)
    scale = lax.rsqrt(jnp.sum(rows * rows, axis=1, keepdims=True) + norm_eps)
    unit = rows * scale
    g_table[...] = scale * (table_slope - unit * jnp.sum(unit * table_slope, axis=1, keepdims=True))
    for p in early:
        end_three(p)
    arrived(small)
    got = ((sm[3, 0] + sm[3, 1]) + sm[3, 2]) + sm[3, 3]
    g_bias_in[:, :1024] = got[0:1]
    g_bias_in[:, 1024:] = got[1:2]
    g_bias_out[...] = got[2:3]
    g_gain[...] = got[3:4]
    g_shift[...] = got[4:5]
    for p in late:
        end_three(p)
    for group in (ones, twos, threes):
        for copies in group.values():
            sent += copies
    for copy in sent + list(zero.values()):
        copy.wait_send()


def hand_over_kernel(*refs):
    for src, dst in zip(refs[:7], refs[7:]):
        dst[...] = src[...]


def hand_over(*results):
    vmem = pl.BlockSpec(memory_space=pltpu.VMEM)
    return pl.pallas_call(
        hand_over_kernel,
        out_shape=tuple(jax.ShapeDtypeStruct(value.shape, value.dtype) for value in results),
        in_specs=[vmem] * 7,
        out_specs=(vmem,) * 7,
    )(*results)


def step(*operands):
    vmem, hbm = pl.BlockSpec(memory_space=pltpu.VMEM), pl.BlockSpec(memory_space=pl.ANY)

    def scratch(shape, kind):
        return tuple(tuple(pltpu.VMEM(shape + (16, hi - lo), kind) for lo, hi in row) for row in PARTS)

    def joined(shape, kind):
        return tuple(pltpu.VMEM(shape + (16, width), kind) for width in WIDTHS)

    dma = pltpu.SemaphoreType.DMA
    out = jax.ShapeDtypeStruct
    return pl.pallas_call(
        step_kernel,
        out_shape=(
            out((8, 2048), F32),
            out((1, 2048), F32),
            out((16, 1024), F32),
            out((1, 1024), F32),
            out((1, 1024), F32),
            out((1, 1024), F32),
            out((64, 1024), F32),
        ),
        in_specs=[hbm] * 4 + [vmem] * 6,
        out_specs=(vmem,) * 7,
        scratch_shapes=[
            pltpu.VMEM((1024, 1024), BF16),
            pltpu.VMEM((1024, 2048), BF16),
            pltpu.VMEM((2048, 1024), BF16),
            pltpu.VMEM((1024, 1024), BF16),
            pltpu.VMEM((64, 1024), BF16),
            pltpu.VMEM((1024, 1024), BF16),
            pltpu.VMEM((1024, 2048), BF16),
            pltpu.VMEM((1024, 2048), F32),
            pltpu.VMEM((1024, 1024), F32),
            pltpu.VMEM((1024, 128), F32),
            pltpu.VMEM((1024, 1024), BF16),
            pltpu.VMEM((1024, 256), BF16),
            pltpu.VMEM((1, 2048), F32),
            pltpu.VMEM((4, 2, 4, 4, 16, 640), BF16),
            pltpu.VMEM((2, 4, 16, 640), BF16),
            pltpu.VMEM((16, 128), F32),
            pltpu.VMEM((7, 16, 128), F32),
            pltpu.VMEM((128, 128), F32),
            pltpu.VMEM((2, 4, 2, 4, 4, 16, 1024), BF16),
            pltpu.VMEM((2, 4, 4, 4, 16, 1024), BF16),
            scratch((3, 4, 4), BF16),
            joined((4, 4), BF16),
            joined((3, 4), BF16),
            joined((4,), F32),
            joined((3,), F32),
            pltpu.VMEM((4, 4, 8, 1024), F32),
            pltpu.VMEM((4, 2, 8, 128), F32),
            pltpu.VMEM((4, 4, 8, 128), F32),
            dma((8,)),
            dma((5, 1, 3)),
            dma((5, 1, 3)),
            dma((7,)),
            dma((7,)),
            dma((2, 4)),
            dma((2, 4)),
            dma((3, 2, 6, 3)),
            dma((3, 2, 6, 3)),
            dma((4, 3)),
            dma((4, 3)),
            dma((4, 3)),
            dma((4, 3)),
        ],
        compiler_params=pltpu.CompilerParams(
            collective_id=0, has_side_effects=True, vmem_limit_bytes=VMEM_BYTES
        ),
    )(*operands)


def body(
    tokens,
    weight_in,
    bias_in,
    weight_out,
    bias_out,
    norm_gain,
    norm_shift,
    queries,
    corpus_table,
    neg_owner,
    neg_row,
    neg_count,
):
    count_q, seq, width = tokens.shape
    slots = neg_row.shape[1]
    ids = (neg_owner.reshape(count_q, slots) * 1024 + neg_row).astype(F32)
    counts = neg_count.astype(F32)[:, None]
    slot = jnp.concatenate([ids, counts, jnp.full((count_q, 128 - slots - 1), -1.0, F32)], axis=1)
    results = step(
        tokens.reshape(count_q * seq, width),
        weight_in,
        weight_out,
        corpus_table,
        bias_in[None],
        bias_out[None],
        norm_gain[None],
        norm_shift[None],
        queries,
        slot,
    )
    grad_in, g_bias_in, grad_out, g_bias_out, g_gain, g_shift, grad_table = hand_over(*results)
    return (grad_in, g_bias_in[0], grad_out, g_bias_out[0], g_gain[0], g_shift[0], grad_table)


def solution(mesh):
    return jax.shard_map(
        body,
        mesh=mesh,
        in_specs=(
            P(("corpus", "batch"), None, None),
            P(),
            P(),
            P(),
            P(),
            P(),
            P(),
            P(("corpus", "batch"), None),
            P("corpus", None),
            P(("corpus", "batch"), None, None),
            P(("corpus", "batch"), None),
            P(("corpus", "batch")),
        ),
        out_specs=(
            P(("corpus", "batch"), None),
            P(),
            P(("corpus", "batch"), None),
            P(),
            P(),
            P(),
            P(("corpus", "batch"), None),
        ),
        check_vma=False,
    )
```

```python
import functools

import jax
import jax.numpy as jnp
from jax import lax
from jax.experimental import pallas as pl
from jax.experimental.pallas import tpu as pltpu
from jax.sharding import PartitionSpec as P

logit_divisor = 0.05
norm_eps = 1e-06
MESH = pl.DeviceIdType.MESH
F32, BF16 = jnp.float32, jnp.bfloat16
VMEM_BYTES = 60 * 1024 * 1024


def place():
    c, b = lax.axis_index("corpus"), lax.axis_index("batch")
    return c // 2, c % 2, b // 4, b % 4


def device(z, k, y, x):
    return (z * 2 + k, y * 4 + x)


def moved(here, dim, offset):
    z, k, y, x = here
    at = [z, y, x]
    at[dim] = lax.rem(at[dim] + offset, 4)
    return device(at[0], k, at[1], at[2]), at[dim]


def put(here, dim, to):
    z, k, y, x = here
    at = [z, y, x]
    at[dim] = to
    return device(at[0], k, at[1], at[2])


def greet(peers):
    barrier = pltpu.get_barrier_semaphore()
    for peer in peers:
        pl.semaphore_signal(barrier, inc=1, device_id=peer, device_id_type=MESH)


def greeted(peers):
    pl.semaphore_wait(pltpu.get_barrier_semaphore(), len(peers))


def push(src, dst, send, recv, peer):
    copy = pltpu.make_async_remote_copy(
        src_ref=src, dst_ref=dst, send_sem=send, recv_sem=recv, device_id=peer, device_id_type=MESH
    )
    copy.start()
    return copy


PARTS = (
    ((0, 384), (384, 768), (768, 1024)),
    ((0, 256), (256, 512), (512, 640), (640, 768), (768, 896), (896, 1024)),
)
ORDER = ((0, 1, 2), (1, 2, 0), (2, 0, 1)) * 2
JOINED = (((0, 0), (1, 0), (2, 0)), ((0, 384), (1, 384), (2, 256), (3, 0), (4, 0), (5, 0)))
WIDTHS = (640, 640, 384, 128, 128, 128)


def pick(ref, axis, index, columns=None):
    at = [slice(None)] * (len(ref.shape) - 2)
    at[axis] = index
    return ref.at[tuple(at) + (slice(None), slice(None) if columns is None else pl.ds(columns[0], columns[1] - columns[0]))]


def dot(a, b, ca=1, cb=0):
    return lax.dot_general(a, b, (((ca,), (cb,)), ((), ())), preferred_element_type=F32)


def step_kernel(
    tok_hbm, win_hbm, wout_hbm, tab_hbm, bias_in, bias_out, gain, shift, queries, slot,
    g_in, g_bias_in, g_out, g_bias_out, g_gain, g_shift, g_table,
    tok, win, wout, tab, tab_own, tok_t, hidden, slope, normed, inv_std, d_sum, d_pre, bias_acc,
    qall, qcol, dots, dall, turned,
    part, r0, r1, s1, r2, s2, r3, sm, cg, cm,
    load, sems_q, semr_q, dsem, dsemr, sem0, rsem0, sems, semr, qs, qr, cs, cr,
):
    here = place()
    z, k, y, x = here
    coord = (z, y, x)
    c = z * 2 + k
    sibling = device(z, 1 - k, y, x)
    fst = [(1 - k) * (i + 1 - 2 * lax.rem(i, 2)) + k * (3 - i) for i in coord]
    snd = [k * (i + 1 - 2 * lax.rem(i, 2)) + (1 - k) * (3 - i) for i in coord]
    opp = [lax.rem(i + 2, 4) for i in coord]
    sent = []

    def local(src, dst, n):
        copy = pltpu.make_async_copy(src, dst, load.at[n])
        copy.start()
        return copy

    column = []
    for j in range(4):
        for e in range(2):
            if j or e:
                column.append(device(lax.rem(z + j, 4), lax.rem(k + e, 2), y, x))
    peers = column + [moved(here, dim, j)[0] for dim in (1, 2) for j in (1, 2, 3)]
    greet(peers)
    tok_in = local(tok_hbm, tok, 0)
    win_in = [local(win_hbm.at[:, pl.ds(512 * n, 512)], win.at[:, pl.ds(512 * n, 512)], 1 + n) for n in range(4)]
    tab_in = local(tab_hbm, tab, 5)
    wout_in = local(wout_hbm, wout, 6)
    own_in = local(tab_hbm.at[pl.ds(pl.multiple_of((y * 4 + x) * 64, 64), 64), :], tab_own, 7)

    query = queries[...].astype(F32)
    lane = lax.broadcasted_iota(jnp.int32, (8, 128), 1)
    digit = jnp.floor(slot[...] * 0.0078125)
    qall[z, k, y, x] = jnp.concatenate(
        [
            jnp.concatenate([query[:, :512], digit], axis=1),
            jnp.concatenate([query[:, 512:], slot[...] - 128.0 * digit], axis=1),
        ],
        axis=0,
    ).astype(BF16)
    payload = ((0, qall),)

    def gather_first():
        copies = []
        for j in (1, 2, 3):
            peer, _ = moved(here, 0, j)
            for n, buf in payload:
                mine = buf.at[z, k, y, x]
                copies.append(push(mine, mine, sems_q.at[0, n, j - 1], semr_q.at[0, n, j - 1], peer))
        return copies

    def gather_second():
        for copy in first:
            copy.wait_recv()
        copies = []
        for n, buf, dst in ((0, qall, qcol),):
            copies.append(push(buf.at[:, k, y, x], dst.at[k], sems_q.at[1, n, 0], semr_q.at[1, n, 0], sibling))
        for j in (1, 2, 3):
            peer, _ = moved(here, 1, j)
            for n, buf in payload:
                mine = buf.at[:, k, y, x]
                copies.append(push(mine, mine, sems_q.at[2, n, j - 1], semr_q.at[2, n, j - 1], peer))
        qcol[k] = qall[:, k, y, x]
        return copies

    def gather_third():
        copies = []
        for m, to in enumerate((fst[2], snd[2])):
            for n, buf in payload:
                mine = buf.at[:, k, :, x]
                copies.append(push(mine, mine, sems_q.at[3, n, m], semr_q.at[3, n, m], put(here, 2, to)))
        return copies

    def gather_fourth():
        for copy in third[:1]:
            copy.wait_recv()
        copies = []
        for n, buf in payload:
            near = buf.at[:, k, :, fst[2]]
            copies.append(push(near, near, sems_q.at[3, n, 2], semr_q.at[3, n, 2], put(here, 2, snd[2])))
        return copies

    def gather_last():
        copies = []
        for n, buf in payload:
            mine = buf.at[:, k]
            copies.append(push(mine, mine, sems_q.at[4, n, 0], semr_q.at[4, n, 0], sibling))
        return copies

    def project(n, carry):
        at = pl.ds(pl.multiple_of(n * 256, 256), 256)
        weight = win[:, at]
        bias = bias_in[:, at]
        for m in range(4):
            rows = slice(m * 256, m * 256 + 256)
            pre = dot(tok[rows, :], weight) + bias
            cdf = 0.5 * (1.0 + lax.erf(pre * 0.7071067811865476))
            hidden[rows, at] = (pre * cdf).astype(BF16)
            slope[rows, at] = cdf + pre * 0.3989422804014327 * jnp.exp(-0.5 * pre * pre)
        turn = pl.ds(pl.multiple_of(n * 128, 128), 128)
        tok_t[turn, :] = tok[:, turn].T
        return carry

    tok_in.wait()
    win_in[0].wait()
    lax.fori_loop(0, 1, project, 0)
    greeted(peers)
    first = gather_first()
    lax.fori_loop(1, 2, project, 0)
    win_in[1].wait()
    lax.fori_loop(2, 4, project, 0)
    second = gather_second()
    win_in[2].wait()
    lax.fori_loop(4, 6, project, 0)
    win_in[3].wait()
    lax.fori_loop(6, 8, project, 0)
    for copy in second:
        copy.wait_recv()
    third = gather_third()
    sent += first + second + third

    tab_in.wait()
    own_in.wait()
    wide_q = qcol[...].astype(F32).reshape(8, 16, 640)
    left = wide_q[:, :8, :512].reshape(64, 512).astype(BF16)
    right = wide_q[:, 8:, :512].reshape(64, 512).astype(BF16)
    ids = (wide_q[:, :8, 512:] * 128.0 + wide_q[:, 8:, 512:]).reshape(64, 128)
    ids = jnp.concatenate([ids, jnp.zeros((64, 128), F32)], axis=0).T[:16, :64]
    dots[...] = jnp.zeros_like(dots)

    def score_rows(i, carry):
        start = pl.multiple_of(i * 128, 128)
        block = tab[pl.ds(start, 128), :]
        wide = block.astype(F32)
        scale = lax.rsqrt(jnp.sum(wide * wide, axis=1, keepdims=True) + norm_eps)
        score = (dot(block[:, :512], left, 1, 1) + dot(block[:, 512:], right, 1, 1)) * scale
        names = (lax.broadcasted_iota(jnp.int32, (128, 64), 0) + (start + c * 1024)).astype(F32)
        found = []
        for slot in range(12):
            hit = jnp.where(names == ids[slot : slot + 1, :], score, 0.0)
            found.append(jnp.sum(hit, axis=0, keepdims=True))
        found.append(jnp.zeros((4, 64), F32))
        dots[:, :64] += jnp.concatenate(found, axis=0)
        return carry

    lax.fori_loop(0, 8, score_rows, 0)
    back = [push(dots, dall.at[n], dsem.at[n], dsemr.at[n], peer) for n, peer in enumerate(column)]
    sent += back


    wout_in.wait()
    which = lax.broadcasted_iota(jnp.int32, (8, 1024), 0)

    def normalise(i, carry):
        rows = pl.ds(pl.multiple_of(i * 256, 256), 256)
        summed = tok[rows, :].astype(F32) + dot(hidden[rows, :], wout[...]) + bias_out[...]
        centred = summed - jnp.mean(summed, axis=1, keepdims=True)
        inv = lax.rsqrt(jnp.mean(centred * centred, axis=1, keepdims=True) + norm_eps)
        value = centred * inv
        normed[rows, :] = value
        inv_std[rows, :] = jnp.broadcast_to(inv, (256, 128))
        for h in range(2):
            line = jnp.sum(value[h * 128 : h * 128 + 128], axis=0, keepdims=True)
            carry = jnp.where(which == 2 * i + h, line, carry)
        return carry

    norm_sum = lax.fori_loop(0, 2, normalise, jnp.zeros((8, 1024), F32))
    fourth = gather_fourth()
    sent += fourth
    norm_sum = lax.fori_loop(2, 4, normalise, norm_sum)

    for copy in back:
        copy.wait_recv()
    total = dots[...]
    for n in range(7):
        total += dall[n]
    turned[...] = jnp.concatenate([total, jnp.zeros((112, 128), F32)], axis=0).T
    raw = turned[pl.ds(pl.multiple_of((k * 4 + z) * 8, 8), 8), :]
    pooled = norm_sum * gain[...] + 128.0 * shift[...]
    emb_scale = lax.rsqrt(jnp.sum(pooled * pooled, axis=1, keepdims=True) + norm_eps)
    emb = pooled * emb_scale
    q_scale = lax.rsqrt(jnp.sum(query * query, axis=1, keepdims=True) + norm_eps)
    question = query * q_scale
    positive = jnp.sum(question * emb, axis=1, keepdims=True) / logit_divisor
    live = lane.astype(F32) < slot[:, 12:13]
    weights = jnp.where(live, jnp.exp(raw * q_scale / logit_divisor), 0.0)
    own = jnp.exp(positive)
    whole = own + jnp.sum(weights, axis=1, keepdims=True)
    cg[z, k] = weights / whole / logit_divisor * q_scale
    emb_slope = ((own / whole - 1.0) / logit_divisor) * question
    d_pooled = emb_scale * (emb_slope - emb * jnp.sum(emb * emb_slope, axis=1, keepdims=True))
    grad_shift = jnp.sum(d_pooled, axis=0, keepdims=True) * 128.0
    grad_gain = jnp.sum(d_pooled * norm_sum, axis=0, keepdims=True)
    lead = d_pooled * gain[...]

    def slopes(step):
        if step == 0:
            mine = cg.at[z, k]
            return [push(mine, mine, cs.at[0, 0], cr.at[0, 0], sibling)]
        if step == 2:
            tile = cg[0, 0]
            for n in range(1, 8):
                tile += pltpu.roll(cg[n // 2, n % 2], 16 * n, 1)
            cm[y, x] = tile
        dim = step - 1
        mine = (cg.at[z], cm.at[y, x], cm.at[:, x])[dim]
        copies = []
        for j in (1, 2, 3):
            peer, _ = moved(here, dim, j)
            copies.append(push(mine, mine, cs.at[step, j - 1], cr.at[step, j - 1], peer))
        return copies

    def arrived(copies):
        for copy in copies:
            copy.wait_recv()

    slope_step = slopes(0)
    sent += slope_step

    def back_norm(i, carry):
        rows = pl.ds(pl.multiple_of(i * 128, 128), 128)
        g = jnp.sum(jnp.where(which == i, lead, 0.0), axis=0, keepdims=True)
        value = normed[rows, :]
        inv = inv_std[rows, :][:, :1]
        both = jnp.mean(value * g, axis=1, keepdims=True)
        ds = inv * (g - jnp.mean(g, axis=1, keepdims=True) - value * both)
        d_sum[rows, :] = ds.astype(BF16)
        return carry + jnp.sum(ds, axis=0, keepdims=True)

    grad_bias_out = lax.fori_loop(0, 8, back_norm, jnp.zeros((1, 1024), F32))
    for copy in third[1:] + fourth:
        copy.wait_recv()
    arrived(slope_step)
    slope_step = slopes(1)
    sent += slope_step

    def grad_out(zz, core):
        at = pl.ds(pl.multiple_of((zz * 2 + core) * 256, 256), 256)
        value = dot(hidden[:, at], d_sum[...], 0, 0)
        part[0, zz, core] = value.astype(BF16).reshape(4, 4, 16, 1024)

    zero = {}
    for zz in range(4):
        grad_out(zz, 1 - k)
        zero[0, zz] = push(part.at[0, zz, 1 - k], r0.at[0, zz], sem0.at[0, zz], rsem0.at[0, zz], sibling)

    arrived(slope_step)
    slope_step = slopes(2)
    sent += slope_step

    def own_blocks(zz, carry):
        grad_out(zz, k)
        return carry

    lax.fori_loop(0, 4, own_blocks, 0)
    arrived(slope_step)
    slope_step = slopes(3)
    sent += slope_step

    def add_core(w, lo, hi, first, last):
        def one(i, carry):
            a, e = i // 4, lax.rem(i, 4)
            r0[w, a, e, :, :, lo:hi] = r0[w, a, e, :, :, lo:hi] + part[w, a, k, e, :, :, lo:hi]
            return carry
        lax.fori_loop(first, last, one, 0)

    def rest(p):
        return [d for d in (0, 1, 2) if d != ORDER[p][0]]

    def stage_one(w, p):
        dim = ORDER[p][0]
        peer = put(here, dim, fst[dim])
        copies = []
        for n, to in enumerate((opp[dim], fst[dim])):
            src = pick(r0.at[w], dim, to, PARTS[w][p])
            copies.append(push(src, r1[w][p].at[n], sems.at[0, w, p, n], semr.at[0, w, p, n], peer))
        return copies

    def relay_one(w, p):
        dim = ORDER[p][0]
        mine = pick(r0.at[w], dim, snd[dim], PARTS[w][p])

        def one(e, carry):
            mine[e] = mine[e] + r1[w][p][0, e]
            return carry
        lax.fori_loop(0, 4, one, 0)
        return [push(mine, r1[w][p].at[2], sems.at[0, w, p, 2], semr.at[0, w, p, 2], put(here, dim, snd[dim]))]

    def add_one(w, p):
        dim = ORDER[p][0]
        mine = pick(r0.at[w], dim, coord[dim], PARTS[w][p])
        g, lo = JOINED[w][p]
        to = slice(lo, lo + PARTS[w][p][1] - PARTS[w][p][0])

        def one(e, carry):
            value = mine[e].astype(F32) + r1[w][p][1, e].astype(F32) + r1[w][p][2, e].astype(F32)
            s1[g][e, :, :, to] = value.astype(BF16)
            return carry
        lax.fori_loop(0, 4, one, 0)

    def stage_two(g):
        dim = ORDER[g][1]
        copies = []
        for j in (1, 2, 3):
            peer, to = moved(here, dim, j)
            src = pick(s1[g], rest(g).index(dim), to)
            copies.append(push(src, r2[g].at[j - 1], sems.at[1, 0, g, j - 1], semr.at[1, 0, g, j - 1], peer))
        return copies

    def add_two(g):
        dim = ORDER[g][1]
        value = pick(s1[g], rest(g).index(dim), coord[dim])[...].astype(F32)
        for j in range(3):
            value += r2[g][j].astype(F32)
        s2[g][...] = value

    def stage_three(g):
        dim = ORDER[g][2]
        copies = []
        for j in (1, 2, 3):
            peer, to = moved(here, dim, j)
            copies.append(push(s2[g].at[to], r3[g].at[j - 1], sems.at[2, 0, g, j - 1], semr.at[2, 0, g, j - 1], peer))
        return copies

    def add_three(g):
        value = s2[g][coord[ORDER[g][2]]] + r3[g][0] + r3[g][1] + r3[g][2]
        for w in range(2):
            for p, (lo, hi) in enumerate(PARTS[w]):
                if JOINED[w][p][0] != g:
                    continue
                at = JOINED[w][p][1]
                if w == 0:
                    g_out[:, lo:hi] = value[:, at : at + hi - lo]
                    continue
                for n in range((hi - lo) // 128):
                    tile = value[:, at + n * 128 : at + n * 128 + 128]
                    g_in[:, 2 * lo + 256 * n : 2 * lo + 256 * n + 128] = tile[:8]
                    g_in[:, 2 * lo + 256 * n + 128 : 2 * lo + 256 * n + 256] = tile[8:]

    def back_layer(n, carry):
        at = pl.ds(pl.multiple_of(n * 256, 256), 256)
        weight = wout[at, :]
        line = jnp.zeros((1, 256), F32)
        for m in range(4):
            rows = slice(m * 256, m * 256 + 256)
            value = dot(d_sum[rows, :], weight, 1, 1) * slope[rows, at]
            line += jnp.sum(value, axis=0, keepdims=True)
            d_pre[rows, :] = value.astype(BF16)
        bias_acc[:, at] = line
        to = pl.ds(pl.multiple_of(n * 128, 128), 128)
        for m in range(4):
            value = dot(tok_t[m * 256 : m * 256 + 256, :], d_pre[...])
            value = value.reshape(32, 8, 256)
            value = jnp.concatenate([value[:, :, :128], value[:, :, 128:]], axis=1).astype(BF16)
            part[1, m, :, :, :, :, to] = value.reshape(2, 4, 4, 16, 128)
        return carry

    ones, twos, threes = {}, {}, {}

    def start(w, p):
        ones[w, p] = stage_one(w, p)

    def pass_on(w, p):
        ones[w, p][0].wait_recv()
        ones[w, p] += relay_one(w, p)

    def end_one(w, p):
        arrived(ones[w, p][1:])
        add_one(w, p)

    def end_two(g):
        arrived(twos[g])
        add_two(g)
        threes[g] = stage_three(g)

    def end_three(g):
        arrived(threes[g])
        add_three(g)

    def to_sibling(n, lo, hi):
        cut = pl.ds(lo, hi - lo)
        zero[1, n] = push(
            part.at[1, :, 1 - k, :, :, :, cut], r0.at[1, :, :, :, :, cut], sem0.at[1, n], rsem0.at[1, n], sibling
        )

    for zz in range(4):
        zero[0, zz].wait_recv()
        add_core(0, 0, 1024, 4 * zz, 4 * zz + 4)
    for p in range(3):
        start(0, p)
    early, late = (0, 1, 2), (3, 4, 5)
    last = gather_last()
    sent += last
    lax.fori_loop(0, 3, back_layer, 0)
    to_sibling(0, 0, 384)
    lax.fori_loop(3, 5, back_layer, 0)
    to_sibling(2, 384, 640)
    for p in range(3):
        pass_on(0, p)
    lax.fori_loop(5, 6, back_layer, 0)
    for p in range(3):
        end_one(0, p)
    lax.fori_loop(6, 7, back_layer, 0)
    zero[1, 0].wait_recv()
    zero[1, 2].wait_recv()
    add_core(1, 0, 640, 0, 16)
    for p in early:
        start(1, p)
    lax.fori_loop(7, 8, back_layer, 0)
    to_sibling(1, 640, 1024)
    sm[0, k] = jnp.concatenate(
        [bias_acc[:, :1024], bias_acc[:, 1024:], grad_bias_out, grad_gain, grad_shift, jnp.zeros((3, 1024), F32)], axis=0
    )
    small = [push(sm.at[0, k], sm.at[0, k], qs.at[0, 0], qr.at[0, 0], sibling)]
    sent += small

    def stage_small(step):
        dim = step - 1
        got = sm[step - 1, 0] + sm[step - 1, 1]
        if step > 1:
            got = (got + sm[step - 1, 2]) + sm[step - 1, 3]
        sm[step, coord[dim]] = got
        copies = []
        for j in (1, 2, 3):
            peer, _ = moved(here, dim, j)
            mine = sm.at[step, coord[dim]]
            copies.append(push(mine, mine, qs.at[step, j - 1], qr.at[step, j - 1], peer))
        return copies

    arrived(last)
    arrived(slope_step)
    base = c * 1024 + (y * 4 + x) * 64
    row = (lax.broadcasted_iota(jnp.int32, (256, 128), 1) + base).astype(F32)

    def collect(i):
        some = qall[i].astype(F32).reshape(32, 16, 640)
        name = (some[:, :8, 512:] * 128.0 + some[:, 8:, 512:]).reshape(256, 128)
        tiles = cm[...].reshape(128, 128)
        value = jnp.concatenate([pltpu.roll(tiles, (128 - 16 * n) % 128, 1) for n in (2 * i, 2 * i + 1)], axis=0)
        weight = jnp.zeros((256, 128), F32)
        for slot in range(12):
            weight += jnp.where(name[:, slot : slot + 1] == row, value[:, slot : slot + 1], 0.0)
        high = weight.astype(BF16)
        low = (weight - high.astype(F32)).astype(BF16)
        for h in range(2):
            half = some[:, h * 8 : h * 8 + 8, :512].reshape(256, 512).astype(BF16)
            found = (dot(high, half, 0, 0) + dot(low, half, 0, 0))[:64]
            at = slice(h * 512, h * 512 + 512)
            g_table[:, at] = found if i == 0 else g_table[:, at] + found

    collect(0)
    for p in early:
        pass_on(1, p)
    arrived(small)
    small = stage_small(1)
    sent += small
    zero[1, 1].wait_recv()
    add_core(1, 640, 1024, 0, 16)
    for p in late:
        start(1, p)
    collect(1)
    for p in early:
        end_one(1, p)
        twos[p] = stage_two(p)
    for p in late:
        pass_on(1, p)
    arrived(small)
    small = stage_small(2)
    sent += small
    collect(2)
    for p in late:
        end_one(1, p)
        twos[p] = stage_two(p)
    for p in early:
        end_two(p)
    arrived(small)
    small = stage_small(3)
    sent += small
    collect(3)
    for p in late:
        end_two(p)
    table_slope = g_table[...]
    rows = tab_own[...].astype(F32)
    scale = lax.rsqrt(jnp.sum(rows * rows, axis=1, keepdims=True) + norm_eps)
    unit = rows * scale
    g_table[...] = scale * (table_slope - unit * jnp.sum(unit * table_slope, axis=1, keepdims=True))
    for p in early:
        end_three(p)
    arrived(small)
    got = ((sm[3, 0] + sm[3, 1]) + sm[3, 2]) + sm[3, 3]
    g_bias_in[:, :1024] = got[0:1]
    g_bias_in[:, 1024:] = got[1:2]
    g_bias_out[...] = got[2:3]
    g_gain[...] = got[3:4]
    g_shift[...] = got[4:5]
    for p in late:
        end_three(p)
    for group in (ones, twos, threes):
        for copies in group.values():
            sent += copies
    for copy in sent + list(zero.values()):
        copy.wait_send()


def hand_over_kernel(*refs):
    for src, dst in zip(refs[:7], refs[7:]):
        dst[...] = src[...]


def hand_over(*results):
    vmem = pl.BlockSpec(memory_space=pltpu.VMEM)
    return pl.pallas_call(
        hand_over_kernel,
        out_shape=tuple(jax.ShapeDtypeStruct(value.shape, value.dtype) for value in results),
        in_specs=[vmem] * 7,
        out_specs=(vmem,) * 7,
    )(*results)


def step(*operands):
    vmem, hbm = pl.BlockSpec(memory_space=pltpu.VMEM), pl.BlockSpec(memory_space=pl.ANY)

    def scratch(shape, kind):
        return tuple(tuple(pltpu.VMEM(shape + (16, hi - lo), kind) for lo, hi in row) for row in PARTS)

    def joined(shape, kind):
        return tuple(pltpu.VMEM(shape + (16, width), kind) for width in WIDTHS)

    dma = pltpu.SemaphoreType.DMA
    out = jax.ShapeDtypeStruct
    return pl.pallas_call(
        step_kernel,
        out_shape=(
            out((8, 2048), F32),
            out((1, 2048), F32),
            out((16, 1024), F32),
            out((1, 1024), F32),
            out((1, 1024), F32),
            out((1, 1024), F32),
            out((64, 1024), F32),
        ),
        in_specs=[hbm] * 4 + [vmem] * 6,
        out_specs=(vmem,) * 7,
        scratch_shapes=[
            pltpu.VMEM((1024, 1024), BF16),
            pltpu.VMEM((1024, 2048), BF16),
            pltpu.VMEM((2048, 1024), BF16),
            pltpu.VMEM((1024, 1024), BF16),
            pltpu.VMEM((64, 1024), BF16),
            pltpu.VMEM((1024, 1024), BF16),
            pltpu.VMEM((1024, 2048), BF16),
            pltpu.VMEM((1024, 2048), F32),
            pltpu.VMEM((1024, 1024), F32),
            pltpu.VMEM((1024, 128), F32),
            pltpu.VMEM((1024, 1024), BF16),
            pltpu.VMEM((1024, 256), BF16),
            pltpu.VMEM((1, 2048), F32),
            pltpu.VMEM((4, 2, 4, 4, 16, 640), BF16),
            pltpu.VMEM((2, 4, 16, 640), BF16),
            pltpu.VMEM((16, 128), F32),
            pltpu.VMEM((7, 16, 128), F32),
            pltpu.VMEM((128, 128), F32),
            pltpu.VMEM((2, 4, 2, 4, 4, 16, 1024), BF16),
            pltpu.VMEM((2, 4, 4, 4, 16, 1024), BF16),
            scratch((3, 4, 4), BF16),
            joined((4, 4), BF16),
            joined((3, 4), BF16),
            joined((4,), F32),
            joined((3,), F32),
            pltpu.VMEM((4, 4, 8, 1024), F32),
            pltpu.VMEM((4, 2, 8, 128), F32),
            pltpu.VMEM((4, 4, 8, 128), F32),
            dma((8,)),
            dma((5, 1, 3)),
            dma((5, 1, 3)),
            dma((7,)),
            dma((7,)),
            dma((2, 4)),
            dma((2, 4)),
            dma((3, 2, 6, 3)),
            dma((3, 2, 6, 3)),
            dma((4, 3)),
            dma((4, 3)),
            dma((4, 3)),
            dma((4, 3)),
        ],
        compiler_params=pltpu.CompilerParams(
            collective_id=0, has_side_effects=True, vmem_limit_bytes=VMEM_BYTES
        ),
    )(*operands)


def body(
    tokens,
    weight_in,
    bias_in,
    weight_out,
    bias_out,
    norm_gain,
    norm_shift,
    queries,
    corpus_table,
    neg_owner,
    neg_row,
    neg_count,
):
    count_q, seq, width = tokens.shape
    slots = neg_row.shape[1]
    ids = (neg_owner.reshape(count_q, slots) * 1024 + neg_row).astype(F32)
    counts = neg_count.astype(F32)[:, None]
    slot = jnp.concatenate([ids, counts, jnp.full((count_q, 128 - slots - 1), -1.0, F32)], axis=1)
    results = step(
        tokens.reshape(count_q * seq, width),
        weight_in,
        weight_out,
        corpus_table,
        bias_in[None],
        bias_out[None],
        norm_gain[None],
        norm_shift[None],
        queries,
        slot,
    )
    grad_in, g_bias_in, grad_out, g_bias_out, g_gain, g_shift, grad_table = hand_over(*results)
    return (grad_in, g_bias_in[0], grad_out, g_bias_out[0], g_gain[0], g_shift[0], grad_table)


def solution(mesh):
    return jax.shard_map(
        body,
        mesh=mesh,
        in_specs=(
            P(("corpus", "batch"), None, None),
            P(),
            P(),
            P(),
            P(),
            P(),
            P(),
            P(("corpus", "batch"), None),
            P("corpus", None),
            P(("corpus", "batch"), None, None),
            P(("corpus", "batch"), None),
            P(("corpus", "batch")),
        ),
        out_specs=(
            P(("corpus", "batch"), None),
            P(),
            P(("corpus", "batch"), None),
            P(),
            P(),
            P(),
            P(("corpus", "batch"), None),
        ),
        check_vma=False,
    )
```

```python
import functools

import jax
import jax.numpy as jnp
from jax import lax
from jax.experimental import pallas as pl
from jax.experimental.pallas import tpu as pltpu
from jax.sharding import PartitionSpec as P

logit_divisor = 0.05
norm_eps = 1e-06
MESH = pl.DeviceIdType.MESH
F32, BF16 = jnp.float32, jnp.bfloat16
VMEM_BYTES = 60 * 1024 * 1024


def place():
    c, b = lax.axis_index("corpus"), lax.axis_index("batch")
    return c // 2, c % 2, b // 4, b % 4


def device(z, k, y, x):
    return (z * 2 + k, y * 4 + x)


def moved(here, dim, offset):
    z, k, y, x = here
    at = [z, y, x]
    at[dim] = lax.rem(at[dim] + offset, 4)
    return device(at[0], k, at[1], at[2]), at[dim]


def put(here, dim, to):
    z, k, y, x = here
    at = [z, y, x]
    at[dim] = to
    return device(at[0], k, at[1], at[2])


def greet(peers):
    barrier = pltpu.get_barrier_semaphore()
    for peer in peers:
        pl.semaphore_signal(barrier, inc=1, device_id=peer, device_id_type=MESH)


def greeted(peers):
    pl.semaphore_wait(pltpu.get_barrier_semaphore(), len(peers))


def push(src, dst, send, recv, peer):
    copy = pltpu.make_async_remote_copy(
        src_ref=src, dst_ref=dst, send_sem=send, recv_sem=recv, device_id=peer, device_id_type=MESH
    )
    copy.start()
    return copy


PARTS = (
    ((0, 384), (384, 768), (768, 1024)),
    ((0, 256), (256, 512), (512, 640), (640, 768), (768, 896), (896, 1024)),
)
ORDER = ((0, 1, 2), (1, 2, 0), (2, 0, 1)) * 2
JOINED = (((0, 0), (1, 0), (2, 0)), ((0, 384), (1, 384), (2, 256), (3, 0), (4, 0), (5, 0)))
WIDTHS = (640, 640, 384, 128, 128, 128)


def pick(ref, axis, index, columns=None):
    at = [slice(None)] * (len(ref.shape) - 2)
    at[axis] = index
    return ref.at[tuple(at) + (slice(None), slice(None) if columns is None else pl.ds(columns[0], columns[1] - columns[0]))]


def dot(a, b, ca=1, cb=0):
    return lax.dot_general(a, b, (((ca,), (cb,)), ((), ())), preferred_element_type=F32)


def step_kernel(
    tok_hbm, win_hbm, wout_hbm, tab_hbm, bias_in, bias_out, gain, shift, queries, slot,
    g_in, g_bias_in, g_out, g_bias_out, g_gain, g_shift, g_table,
    tok, win, wout, tab, tab_own, tok_t, hidden, slope, normed, inv_std, d_sum, d_pre, bias_acc,
    qall, qcol, dots, dall, turned,
    part, r0, r1, s1, r2, s2, r3, sm, cg, cm,
    load, sems_q, semr_q, dsem, dsemr, sem0, rsem0, sems, semr, qs, qr, cs, cr,
):
    here = place()
    z, k, y, x = here
    coord = (z, y, x)
    c = z * 2 + k
    sibling = device(z, 1 - k, y, x)
    fst = [(1 - k) * (i + 1 - 2 * lax.rem(i, 2)) + k * (3 - i) for i in coord]
    snd = [k * (i + 1 - 2 * lax.rem(i, 2)) + (1 - k) * (3 - i) for i in coord]
    opp = [lax.rem(i + 2, 4) for i in coord]
    sent = []

    def local(src, dst, n):
        copy = pltpu.make_async_copy(src, dst, load.at[n])
        copy.start()
        return copy

    column = []
    for j in range(4):
        for e in range(2):
            if j or e:
                column.append(device(lax.rem(z + j, 4), lax.rem(k + e, 2), y, x))
    peers = column + [moved(here, dim, j)[0] for dim in (1, 2) for j in (1, 2, 3)]
    greet(peers)
    tok_in = local(tok_hbm, tok, 0)
    win_in = [local(win_hbm.at[:, pl.ds(512 * n, 512)], win.at[:, pl.ds(512 * n, 512)], 1 + n) for n in range(4)]
    tab_in = local(tab_hbm, tab, 5)
    wout_in = local(wout_hbm, wout, 6)
    own_in = local(tab_hbm.at[pl.ds(pl.multiple_of((y * 4 + x) * 64, 64), 64), :], tab_own, 7)

    query = queries[...].astype(F32)
    lane = lax.broadcasted_iota(jnp.int32, (8, 128), 1)
    digit = jnp.floor(slot[...] * 0.0078125)
    qall[z, k, y, x] = jnp.concatenate(
        [
            jnp.concatenate([query[:, :512], digit], axis=1),
            jnp.concatenate([query[:, 512:], slot[...] - 128.0 * digit], axis=1),
        ],
        axis=0,
    ).astype(BF16)
    payload = ((0, qall),)

    def gather_first():
        copies = []
        for j in (1, 2, 3):
            peer, _ = moved(here, 0, j)
            for n, buf in payload:
                mine = buf.at[z, k, y, x]
                copies.append(push(mine, mine, sems_q.at[0, n, j - 1], semr_q.at[0, n, j - 1], peer))
        return copies

    def gather_second():
        for copy in first:
            copy.wait_recv()
        copies = []
        for n, buf, dst in ((0, qall, qcol),):
            copies.append(push(buf.at[:, k, y, x], dst.at[k], sems_q.at[1, n, 0], semr_q.at[1, n, 0], sibling))
        for j in (1, 2, 3):
            peer, _ = moved(here, 1, j)
            for n, buf in payload:
                mine = buf.at[:, k, y, x]
                copies.append(push(mine, mine, sems_q.at[2, n, j - 1], semr_q.at[2, n, j - 1], peer))
        qcol[k] = qall[:, k, y, x]
        return copies

    def gather_third():
        copies = []
        for m, to in enumerate((fst[2], snd[2])):
            for n, buf in payload:
                mine = buf.at[:, k, :, x]
                copies.append(push(mine, mine, sems_q.at[3, n, m], semr_q.at[3, n, m], put(here, 2, to)))
        return copies

    def gather_fourth():
        for copy in third[:1]:
            copy.wait_recv()
        copies = []
        for n, buf in payload:
            near = buf.at[:, k, :, fst[2]]
            copies.append(push(near, near, sems_q.at[3, n, 2], semr_q.at[3, n, 2], put(here, 2, snd[2])))
        return copies

    def gather_last():
        copies = []
        for n, buf in payload:
            mine = buf.at[:, k]
            copies.append(push(mine, mine, sems_q.at[4, n, 0], semr_q.at[4, n, 0], sibling))
        return copies

    def project(n, carry):
        at = pl.ds(pl.multiple_of(n * 256, 256), 256)
        weight = win[:, at]
        bias = bias_in[:, at]
        for m in range(4):
            rows = slice(m * 256, m * 256 + 256)
            pre = dot(tok[rows, :], weight) + bias
            cdf = 0.5 * (1.0 + lax.erf(pre * 0.7071067811865476))
            hidden[rows, at] = (pre * cdf).astype(BF16)
            slope[rows, at] = cdf + pre * 0.3989422804014327 * jnp.exp(-0.5 * pre * pre)
        turn = pl.ds(pl.multiple_of(n * 128, 128), 128)
        tok_t[turn, :] = tok[:, turn].T
        return carry

    tok_in.wait()
    win_in[0].wait()
    lax.fori_loop(0, 1, project, 0)
    greeted(peers)
    first = gather_first()
    lax.fori_loop(1, 2, project, 0)
    win_in[1].wait()
    lax.fori_loop(2, 4, project, 0)
    second = gather_second()
    win_in[2].wait()
    lax.fori_loop(4, 6, project, 0)
    win_in[3].wait()
    lax.fori_loop(6, 8, project, 0)
    for copy in second:
        copy.wait_recv()
    third = gather_third()
    sent += first + second + third

    tab_in.wait()
    own_in.wait()
    wide_q = qcol[...].astype(F32).reshape(8, 16, 640)
    left = wide_q[:, :8, :512].reshape(64, 512).astype(BF16)
    right = wide_q[:, 8:, :512].reshape(64, 512).astype(BF16)
    ids = (wide_q[:, :8, 512:] * 128.0 + wide_q[:, 8:, 512:]).reshape(64, 128)
    ids = jnp.concatenate([ids, jnp.zeros((64, 128), F32)], axis=0).T[:16, :64]
    dots[...] = jnp.zeros_like(dots)

    def score_rows(i, carry):
        start = pl.multiple_of(i * 128, 128)
        block = tab[pl.ds(start, 128), :]
        wide = block.astype(F32)
        scale = lax.rsqrt(jnp.sum(wide * wide, axis=1, keepdims=True) + norm_eps)
        score = (dot(block[:, :512], left, 1, 1) + dot(block[:, 512:], right, 1, 1)) * scale
        names = (lax.broadcasted_iota(jnp.int32, (128, 64), 0) + (start + c * 1024)).astype(F32)
        found = []
        for slot in range(12):
            hit = jnp.where(names == ids[slot : slot + 1, :], score, 0.0)
            found.append(jnp.sum(hit, axis=0, keepdims=True))
        found.append(jnp.zeros((4, 64), F32))
        dots[:, :64] += jnp.concatenate(found, axis=0)
        return carry

    lax.fori_loop(0, 8, score_rows, 0)
    back = [push(dots, dall.at[n], dsem.at[n], dsemr.at[n], peer) for n, peer in enumerate(column)]
    sent += back


    wout_in.wait()
    which = lax.broadcasted_iota(jnp.int32, (8, 1024), 0)

    def normalise(i, carry):
        rows = pl.ds(pl.multiple_of(i * 256, 256), 256)
        summed = tok[rows, :].astype(F32) + dot(hidden[rows, :], wout[...]) + bias_out[...]
        centred = summed - jnp.mean(summed, axis=1, keepdims=True)
        inv = lax.rsqrt(jnp.mean(centred * centred, axis=1, keepdims=True) + norm_eps)
        value = centred * inv
        normed[rows, :] = value
        inv_std[rows, :] = jnp.broadcast_to(inv, (256, 128))
        for h in range(2):
            line = jnp.sum(value[h * 128 : h * 128 + 128], axis=0, keepdims=True)
            carry = jnp.where(which == 2 * i + h, line, carry)
        return carry

    norm_sum = lax.fori_loop(0, 2, normalise, jnp.zeros((8, 1024), F32))
    fourth = gather_fourth()
    sent += fourth
    norm_sum = lax.fori_loop(2, 4, normalise, norm_sum)

    for copy in back:
        copy.wait_recv()
    total = dots[...]
    for n in range(7):
        total += dall[n]
    turned[...] = jnp.concatenate([total, jnp.zeros((112, 128), F32)], axis=0).T
    raw = turned[pl.ds(pl.multiple_of((k * 4 + z) * 8, 8), 8), :]
    pooled = norm_sum * gain[...] + 128.0 * shift[...]
    emb_scale = lax.rsqrt(jnp.sum(pooled * pooled, axis=1, keepdims=True) + norm_eps)
    emb = pooled * emb_scale
    q_scale = lax.rsqrt(jnp.sum(query * query, axis=1, keepdims=True) + norm_eps)
    question = query * q_scale
    positive = jnp.sum(question * emb, axis=1, keepdims=True) / logit_divisor
    live = lane.astype(F32) < slot[:, 12:13]
    weights = jnp.where(live, jnp.exp(raw * q_scale / logit_divisor), 0.0)
    own = jnp.exp(positive)
    whole = own + jnp.sum(weights, axis=1, keepdims=True)
    cg[z, k] = weights / whole / logit_divisor * q_scale
    emb_slope = ((own / whole - 1.0) / logit_divisor) * question
    d_pooled = emb_scale * (emb_slope - emb * jnp.sum(emb * emb_slope, axis=1, keepdims=True))
    grad_shift = jnp.sum(d_pooled, axis=0, keepdims=True) * 128.0
    grad_gain = jnp.sum(d_pooled * norm_sum, axis=0, keepdims=True)
    lead = d_pooled * gain[...]

    def slopes(step):
        if step == 0:
            mine = cg.at[z, k]
            return [push(mine, mine, cs.at[0, 0], cr.at[0, 0], sibling)]
        if step == 2:
            tile = cg[0, 0]
            for n in range(1, 8):
                tile += pltpu.roll(cg[n // 2, n % 2], 16 * n, 1)
            cm[y, x] = tile
        dim = step - 1
        mine = (cg.at[z], cm.at[y, x], cm.at[:, x])[dim]
        copies = []
        for j in (1, 2, 3):
            peer, _ = moved(here, dim, j)
            copies.append(push(mine, mine, cs.at[step, j - 1], cr.at[step, j - 1], peer))
        return copies

    def arrived(copies):
        for copy in copies:
            copy.wait_recv()

    slope_step = slopes(0)
    sent += slope_step

    def back_norm(i, carry):
        rows = pl.ds(pl.multiple_of(i * 128, 128), 128)
        g = jnp.sum(jnp.where(which == i, lead, 0.0), axis=0, keepdims=True)
        value = normed[rows, :]
        inv = inv_std[rows, :][:, :1]
        both = jnp.mean(value * g, axis=1, keepdims=True)
        ds = inv * (g - jnp.mean(g, axis=1, keepdims=True) - value * both)
        d_sum[rows, :] = ds.astype(BF16)
        return carry + jnp.sum(ds, axis=0, keepdims=True)

    grad_bias_out = lax.fori_loop(0, 8, back_norm, jnp.zeros((1, 1024), F32))
    for copy in third[1:] + fourth:
        copy.wait_recv()
    last = gather_last()
    sent += last
    arrived(slope_step)
    slope_step = slopes(1)
    sent += slope_step

    def grad_out(zz, core):
        at = pl.ds(pl.multiple_of((zz * 2 + core) * 256, 256), 256)
        value = dot(hidden[:, at], d_sum[...], 0, 0)
        part[0, zz, core] = value.astype(BF16).reshape(4, 4, 16, 1024)

    zero = {}
    for zz in range(4):
        grad_out(zz, 1 - k)
        zero[0, zz] = push(part.at[0, zz, 1 - k], r0.at[0, zz], sem0.at[0, zz], rsem0.at[0, zz], sibling)

    arrived(slope_step)
    slope_step = slopes(2)
    sent += slope_step

    def own_blocks(zz, carry):
        grad_out(zz, k)
        return carry

    lax.fori_loop(0, 4, own_blocks, 0)
    arrived(slope_step)
    slope_step = slopes(3)
    sent += slope_step

    def add_core(w, lo, hi, first, last):
        def one(i, carry):
            a, e = i // 4, lax.rem(i, 4)
            r0[w, a, e, :, :, lo:hi] = r0[w, a, e, :, :, lo:hi] + part[w, a, k, e, :, :, lo:hi]
            return carry
        lax.fori_loop(first, last, one, 0)

    def rest(p):
        return [d for d in (0, 1, 2) if d != ORDER[p][0]]

    def stage_one(w, p):
        dim = ORDER[p][0]
        peer = put(here, dim, fst[dim])
        copies = []
        for n, to in enumerate((opp[dim], fst[dim])):
            src = pick(r0.at[w], dim, to, PARTS[w][p])
            copies.append(push(src, r1[w][p].at[n], sems.at[0, w, p, n], semr.at[0, w, p, n], peer))
        return copies

    def relay_one(w, p):
        dim = ORDER[p][0]
        mine = pick(r0.at[w], dim, snd[dim], PARTS[w][p])

        def one(e, carry):
            mine[e] = mine[e] + r1[w][p][0, e]
            return carry
        lax.fori_loop(0, 4, one, 0)
        return [push(mine, r1[w][p].at[2], sems.at[0, w, p, 2], semr.at[0, w, p, 2], put(here, dim, snd[dim]))]

    def add_one(w, p):
        dim = ORDER[p][0]
        mine = pick(r0.at[w], dim, coord[dim], PARTS[w][p])
        g, lo = JOINED[w][p]
        to = slice(lo, lo + PARTS[w][p][1] - PARTS[w][p][0])

        def one(e, carry):
            value = mine[e].astype(F32) + r1[w][p][1, e].astype(F32) + r1[w][p][2, e].astype(F32)
            s1[g][e, :, :, to] = value.astype(BF16)
            return carry
        lax.fori_loop(0, 4, one, 0)

    def stage_two(g):
        dim = ORDER[g][1]
        copies = []
        for j in (1, 2, 3):
            peer, to = moved(here, dim, j)
            src = pick(s1[g], rest(g).index(dim), to)
            copies.append(push(src, r2[g].at[j - 1], sems.at[1, 0, g, j - 1], semr.at[1, 0, g, j - 1], peer))
        return copies

    def add_two(g):
        dim = ORDER[g][1]
        value = pick(s1[g], rest(g).index(dim), coord[dim])[...].astype(F32)
        for j in range(3):
            value += r2[g][j].astype(F32)
        s2[g][...] = value

    def stage_three(g):
        dim = ORDER[g][2]
        copies = []
        if g < 3:
            for n, to in enumerate((opp[dim], fst[dim])):
                land, peer = r3[g].at[n], put(here, dim, fst[dim])
                copies.append(push(s2[g].at[to], land, sems.at[2, 0, g, n], semr.at[2, 0, g, n], peer))
            return copies
        for j in (1, 2, 3):
            peer, to = moved(here, dim, j)
            copies.append(push(s2[g].at[to], r3[g].at[j - 1], sems.at[2, 0, g, j - 1], semr.at[2, 0, g, j - 1], peer))
        return copies

    def relay_three(g):
        dim = ORDER[g][2]
        threes[g][0].wait_recv()
        s2[g][snd[dim]] += r3[g][0]
        src, peer = s2[g].at[snd[dim]], put(here, dim, snd[dim])
        threes[g].append(push(src, r3[g].at[2], sems.at[2, 0, g, 2], semr.at[2, 0, g, 2], peer))

    def add_three(g):
        value = s2[g][coord[ORDER[g][2]]] + r3[g][1] + r3[g][2]
        if g > 2:
            value += r3[g][0]
        for w in range(2):
            for p, (lo, hi) in enumerate(PARTS[w]):
                if JOINED[w][p][0] != g:
                    continue
                at = JOINED[w][p][1]
                if w == 0:
                    g_out[:, lo:hi] = value[:, at : at + hi - lo]
                    continue
                for n in range((hi - lo) // 128):
                    tile = value[:, at + n * 128 : at + n * 128 + 128]
                    g_in[:, 2 * lo + 256 * n : 2 * lo + 256 * n + 128] = tile[:8]
                    g_in[:, 2 * lo + 256 * n + 128 : 2 * lo + 256 * n + 256] = tile[8:]

    def back_layer(n, carry):
        at = pl.ds(pl.multiple_of(n * 256, 256), 256)
        weight = wout[at, :]
        line = jnp.zeros((1, 256), F32)
        for m in range(4):
            rows = slice(m * 256, m * 256 + 256)
            value = dot(d_sum[rows, :], weight, 1, 1) * slope[rows, at]
            line += jnp.sum(value, axis=0, keepdims=True)
            d_pre[rows, :] = value.astype(BF16)
        bias_acc[:, at] = line
        to = pl.ds(pl.multiple_of(n * 128, 128), 128)
        for m in range(4):
            value = dot(tok_t[m * 256 : m * 256 + 256, :], d_pre[...])
            value = value.reshape(32, 8, 256)
            value = jnp.concatenate([value[:, :, :128], value[:, :, 128:]], axis=1).astype(BF16)
            part[1, m, :, :, :, :, to] = value.reshape(2, 4, 4, 16, 128)
        return carry

    ones, twos, threes = {}, {}, {}

    def start(w, p):
        ones[w, p] = stage_one(w, p)

    def pass_on(w, p):
        ones[w, p][0].wait_recv()
        ones[w, p] += relay_one(w, p)

    def end_one(w, p):
        arrived(ones[w, p][1:])
        add_one(w, p)

    def end_two(g):
        arrived(twos[g])
        add_two(g)
        threes[g] = stage_three(g)

    def end_three(g):
        arrived(threes[g][1:] if g < 3 else threes[g])
        add_three(g)

    def to_sibling(n, lo, hi):
        cut = pl.ds(lo, hi - lo)
        zero[1, n] = push(
            part.at[1, :, 1 - k, :, :, :, cut], r0.at[1, :, :, :, :, cut], sem0.at[1, n], rsem0.at[1, n], sibling
        )

    for zz in range(4):
        zero[0, zz].wait_recv()
        add_core(0, 0, 1024, 4 * zz, 4 * zz + 4)
    for p in range(3):
        start(0, p)
    early, late = (0, 1, 2), (3, 4, 5)
    lax.fori_loop(0, 5, back_layer, 0)
    to_sibling(0, 0, 640)
    for p in range(3):
        pass_on(0, p)
    lax.fori_loop(5, 6, back_layer, 0)
    for p in range(3):
        end_one(0, p)
    lax.fori_loop(6, 7, back_layer, 0)
    zero[1, 0].wait_recv()
    add_core(1, 0, 640, 0, 16)
    for p in early:
        start(1, p)
    lax.fori_loop(7, 8, back_layer, 0)
    to_sibling(1, 640, 1024)
    sm[0, k] = jnp.concatenate(
        [bias_acc[:, :1024], bias_acc[:, 1024:], grad_bias_out, grad_gain, grad_shift, jnp.zeros((3, 1024), F32)], axis=0
    )
    small = [push(sm.at[0, k], sm.at[0, k], qs.at[0, 0], qr.at[0, 0], sibling)]
    sent += small

    def stage_small(step):
        dim = step - 1
        got = sm[step - 1, 0] + sm[step - 1, 1]
        if step > 1:
            got = (got + sm[step - 1, 2]) + sm[step - 1, 3]
        sm[step, coord[dim]] = got
        copies = []
        for j in (1, 2, 3):
            peer, _ = moved(here, dim, j)
            mine = sm.at[step, coord[dim]]
            copies.append(push(mine, mine, qs.at[step, j - 1], qr.at[step, j - 1], peer))
        return copies

    arrived(last)
    arrived(slope_step)
    base = c * 1024 + (y * 4 + x) * 64
    row = (lax.broadcasted_iota(jnp.int32, (256, 128), 1) + base).astype(F32)

    def collect(i):
        some = qall[i].astype(F32).reshape(32, 16, 640)
        name = (some[:, :8, 512:] * 128.0 + some[:, 8:, 512:]).reshape(256, 128)
        tiles = cm[...].reshape(128, 128)
        value = jnp.concatenate([pltpu.roll(tiles, (128 - 16 * n) % 128, 1) for n in (2 * i, 2 * i + 1)], axis=0)
        weight = jnp.zeros((256, 128), F32)
        for slot in range(12):
            weight += jnp.where(name[:, slot : slot + 1] == row, value[:, slot : slot + 1], 0.0)
        high = weight.astype(BF16)
        low = (weight - high.astype(F32)).astype(BF16)
        for h in range(2):
            half = some[:, h * 8 : h * 8 + 8, :512].reshape(256, 512).astype(BF16)
            found = (dot(high, half, 0, 0) + dot(low, half, 0, 0))[:64]
            at = slice(h * 512, h * 512 + 512)
            g_table[:, at] = found if i == 0 else g_table[:, at] + found

    collect(0)
    for p in early:
        pass_on(1, p)
    arrived(small)
    small = stage_small(1)
    sent += small
    zero[1, 1].wait_recv()
    add_core(1, 640, 1024, 0, 16)
    for p in late:
        start(1, p)
    collect(1)
    for p in early:
        end_one(1, p)
        twos[p] = stage_two(p)
    for p in late:
        pass_on(1, p)
    arrived(small)
    small = stage_small(2)
    sent += small
    collect(2)
    for p in late:
        end_one(1, p)
        twos[p] = stage_two(p)
    for p in early:
        end_two(p)
    arrived(small)
    small = stage_small(3)
    sent += small
    collect(3)
    for g in early:
        relay_three(g)
    for p in late:
        end_two(p)
    table_slope = g_table[...]
    rows = tab_own[...].astype(F32)
    scale = lax.rsqrt(jnp.sum(rows * rows, axis=1, keepdims=True) + norm_eps)
    unit = rows * scale
    g_table[...] = scale * (table_slope - unit * jnp.sum(unit * table_slope, axis=1, keepdims=True))
    for p in early:
        end_three(p)
    arrived(small)
    got = ((sm[3, 0] + sm[3, 1]) + sm[3, 2]) + sm[3, 3]
    g_bias_in[:, :1024] = got[0:1]
    g_bias_in[:, 1024:] = got[1:2]
    g_bias_out[...] = got[2:3]
    g_gain[...] = got[3:4]
    g_shift[...] = got[4:5]
    for p in late:
        end_three(p)
    for group in (ones, twos, threes):
        for copies in group.values():
            sent += copies
    for copy in sent + list(zero.values()):
        copy.wait_send()


def hand_over_kernel(*refs):
    for src, dst in zip(refs[:7], refs[7:]):
        dst[...] = src[...]


def hand_over(*results):
    vmem = pl.BlockSpec(memory_space=pltpu.VMEM)
    return pl.pallas_call(
        hand_over_kernel,
        out_shape=tuple(jax.ShapeDtypeStruct(value.shape, value.dtype) for value in results),
        in_specs=[vmem] * 7,
        out_specs=(vmem,) * 7,
    )(*results)


def step(*operands):
    vmem, hbm = pl.BlockSpec(memory_space=pltpu.VMEM), pl.BlockSpec(memory_space=pl.ANY)

    def scratch(shape, kind):
        return tuple(tuple(pltpu.VMEM(shape + (16, hi - lo), kind) for lo, hi in row) for row in PARTS)

    def joined(shape, kind):
        return tuple(pltpu.VMEM(shape + (16, width), kind) for width in WIDTHS)

    dma = pltpu.SemaphoreType.DMA
    out = jax.ShapeDtypeStruct
    return pl.pallas_call(
        step_kernel,
        out_shape=(
            out((8, 2048), F32),
            out((1, 2048), F32),
            out((16, 1024), F32),
            out((1, 1024), F32),
            out((1, 1024), F32),
            out((1, 1024), F32),
            out((64, 1024), F32),
        ),
        in_specs=[hbm] * 4 + [vmem] * 6,
        out_specs=(vmem,) * 7,
        scratch_shapes=[
            pltpu.VMEM((1024, 1024), BF16),
            pltpu.VMEM((1024, 2048), BF16),
            pltpu.VMEM((2048, 1024), BF16),
            pltpu.VMEM((1024, 1024), BF16),
            pltpu.VMEM((64, 1024), BF16),
            pltpu.VMEM((1024, 1024), BF16),
            pltpu.VMEM((1024, 2048), BF16),
            pltpu.VMEM((1024, 2048), F32),
            pltpu.VMEM((1024, 1024), F32),
            pltpu.VMEM((1024, 128), F32),
            pltpu.VMEM((1024, 1024), BF16),
            pltpu.VMEM((1024, 256), BF16),
            pltpu.VMEM((1, 2048), F32),
            pltpu.VMEM((4, 2, 4, 4, 16, 640), BF16),
            pltpu.VMEM((2, 4, 16, 640), BF16),
            pltpu.VMEM((16, 128), F32),
            pltpu.VMEM((7, 16, 128), F32),
            pltpu.VMEM((128, 128), F32),
            pltpu.VMEM((2, 4, 2, 4, 4, 16, 1024), BF16),
            pltpu.VMEM((2, 4, 4, 4, 16, 1024), BF16),
            scratch((3, 4, 4), BF16),
            joined((4, 4), BF16),
            joined((3, 4), BF16),
            joined((4,), F32),
            joined((3,), F32),
            pltpu.VMEM((4, 4, 8, 1024), F32),
            pltpu.VMEM((4, 2, 8, 128), F32),
            pltpu.VMEM((4, 4, 8, 128), F32),
            dma((8,)),
            dma((5, 1, 3)),
            dma((5, 1, 3)),
            dma((7,)),
            dma((7,)),
            dma((2, 4)),
            dma((2, 4)),
            dma((3, 2, 6, 3)),
            dma((3, 2, 6, 3)),
            dma((4, 3)),
            dma((4, 3)),
            dma((4, 3)),
            dma((4, 3)),
        ],
        compiler_params=pltpu.CompilerParams(
            collective_id=0, has_side_effects=True, vmem_limit_bytes=VMEM_BYTES
        ),
    )(*operands)


def body(
    tokens,
    weight_in,
    bias_in,
    weight_out,
    bias_out,
    norm_gain,
    norm_shift,
    queries,
    corpus_table,
    neg_owner,
    neg_row,
    neg_count,
):
    count_q, seq, width = tokens.shape
    slots = neg_row.shape[1]
    ids = (neg_owner.reshape(count_q, slots) * 1024 + neg_row).astype(F32)
    counts = neg_count.astype(F32)[:, None]
    slot = jnp.concatenate([ids, counts, jnp.full((count_q, 128 - slots - 1), -1.0, F32)], axis=1)
    results = step(
        tokens.reshape(count_q * seq, width),
        weight_in,
        weight_out,
        corpus_table,
        bias_in[None],
        bias_out[None],
        norm_gain[None],
        norm_shift[None],
        queries,
        slot,
    )
    grad_in, g_bias_in, grad_out, g_bias_out, g_gain, g_shift, grad_table = hand_over(*results)
    return (grad_in, g_bias_in[0], grad_out, g_bias_out[0], g_gain[0], g_shift[0], grad_table)


def solution(mesh):
    return jax.shard_map(
        body,
        mesh=mesh,
        in_specs=(
            P(("corpus", "batch"), None, None),
            P(),
            P(),
            P(),
            P(),
            P(),
            P(),
            P(("corpus", "batch"), None),
            P("corpus", None),
            P(("corpus", "batch"), None, None),
            P(("corpus", "batch"), None),
            P(("corpus", "batch")),
        ),
        out_specs=(
            P(("corpus", "batch"), None),
            P(),
            P(("corpus", "batch"), None),
            P(),
            P(),
            P(),
            P(("corpus", "batch"), None),
        ),
        check_vma=False,
    )
```
